128 devices in a mesh: ctx: 2 (over z_hi), fsdp: 4 (over x), rep: 16 (over y, z_lo, core).
Axes of the slice: x: 4, y: 4, z: 4 (z_hi: 2, z_lo: 2; z = z_hi * 2 + z_lo), core: 2. Of those that a mesh axis runs over, the one named last changes fastest.
Arguments:
- tokens: bfloat16 [64, 512, 1536], P(('fsdp', 'rep'), 'ctx'), may hold values from -6 to 6
- segments: int32 [64, 512], P(('fsdp', 'rep')), may hold values from 0 to 3, as said below
- cotangent: bfloat16 [64, 512, 1536], P(('fsdp', 'rep'), 'ctx'), may hold values from -6 to 6
- gate_proj: bfloat16 [1536, 3072], P('fsdp'), may hold values from -0.15625 to 0.15625
- mixer_proj: bfloat16 [1536, 3328], P('fsdp'), may hold values from -0.15625 to 0.15625
- step_proj: bfloat16 [1536, 48], P('fsdp'), may hold values from -0.15625 to 0.15625
- final_proj: bfloat16 [3072, 1536], P('fsdp'), may hold values from -0.109375 to 0.109375
- norm_gain: float32 [1536], replicated, may hold values from 0.5 to 1.5
- conv_kernel: float32 [4, 3328], replicated, may hold values from -3 to 3
- conv_bias: float32 [3328], replicated, may hold values from -3 to 3
- step_offset: float32 [48], replicated, may hold values from -4.5 to -2
- log_rates: float32 [48], replicated, may hold values from -3 to 0.5
- skip_gain: float32 [48], replicated, may hold values from 0.5 to 1.5
- gating_gain: float32 [3072], replicated, may hold values from 0.5 to 1.5
Outputs:
- layer_out: float32 [64, 512, 1536], P(('fsdp', 'rep'), 'ctx')
- grad_tokens: float32 [64, 512, 1536], P(('fsdp', 'rep'), 'ctx')
- grad_gate: float32 [1536, 3072], P('fsdp')
- grad_mixer: float32 [1536, 3328], P('fsdp')
- grad_step: float32 [1536, 48], P('fsdp')
- grad_final: float32 [3072, 1536], P('fsdp')
- grad_norm: float32 [1536], replicated
- grad_kernel: float32 [4, 3328], replicated
- grad_bias: float32 [3328], replicated
- grad_offset: float32 [48], replicated
- grad_rates: float32 [48], replicated
- grad_skip: float32 [48], replicated
- grad_gating: float32 [3072], replicated
The draws below stay inside these ranges and needn't reach their ends.
Inputs may be any that keep to these rules, and one draw needn't show every extreme that they name: `segments`: segment numbers of a sequence start at 0, never fall and rise by one at exactly three positions, so every sequence holds four documents; no document begins at positions k * 256 - 3 to k * 256 + 3.
All inputs are finite; a program needn't handle non-finite values.
Results may differ from the reference program's by a relative error of at most 0.02.
Values may be sent and summed in bfloat16 or wider, within the bound.
No kernel may reach another device: no remote copies, remote signals or barrier semaphores. Data moves between devices by JAX's collectives and lax.ppermute only.
A program may use at most 256 MiB of HBM per device.

```python
import jax
import jax.numpy as jnp
from jax import lax

D = 1536
INNER = 3072
STATE = 128
HEAD_DIM = 64
CONV_K = 4
SPAN = 256
SEQ_LEN = 512
HEADS = 48
CONV_CH = 3328
LOCAL = 256
SEQS = 64


cut_count = 3


def draw_segments(key, part):
    key = jax.random.fold_in(key, 7)
    positions = jnp.arange(SEQ_LEN)
    within = positions % LOCAL
    allowed = (positions > 0) & (within > 3) & (within < LOCAL - 3)
    row_keys = jax.random.split(key, SEQS)
    ranking = jax.vmap(lambda row_key: jax.random.permutation(row_key, SEQ_LEN))(row_keys).astype(jnp.int32)
    scored = jnp.where(allowed[None, :], ranking, ranking + SEQ_LEN).astype(jnp.int32)
    lowest, _ = lax.top_k(-scored, cut_count)
    border = -lowest[:, cut_count - 1]
    cuts = (scored <= border[:, None]).astype(jnp.int32)
    return jnp.cumsum(cuts, axis=1).astype(jnp.int32)


def shard_levels(own_key, shape, cuts, smallest, largest):
    gain = 1.0
    for position, parts in cuts:
        heights = jax.random.uniform(jax.random.fold_in(jax.random.fold_in(own_key, 6), position), (parts,), jnp.float32, smallest / len(cuts), largest / len(cuts))
        gain = gain * jnp.repeat(jnp.exp(heights), shape[position] // parts).reshape((-1,) + (1,) * (len(shape) - 1 - position))
    return gain


def noise(stream_key, extent, width, reach, cuts=(), dtype=jnp.bfloat16):
    loudness = shard_levels(stream_key, extent, cuts, -0.22, 0.18) if cuts else 1.0
    drawn = jax.random.normal(stream_key, extent, jnp.float32) * width * loudness
    return jnp.minimum(jnp.maximum(drawn, -reach), reach).astype(dtype)


def setup_inputs(seed: int = 0) -> dict:
    seeds = jax.random.split(jax.random.key(seed), 15)
    return {
        "tokens": noise(seeds[0], (SEQS, SEQ_LEN, D), 1.0, 6.0, ((0, 64), (1, 2))),
        "segments": draw_segments(jax.random.fold_in(seeds[14], 71), 0),
        "cotangent": noise(seeds[2], (SEQS, SEQ_LEN, D), 1.0, 6.0, ((0, 64), (1, 2))),
        "gate_proj": noise(seeds[3], (D, INNER), D ** -0.5, 0.15625, ((0, 4),)),
        "mixer_proj": noise(seeds[4], (D, CONV_CH), D ** -0.5, 0.15625, ((0, 4),)),
        "step_proj": noise(seeds[5], (D, HEADS), D ** -0.5, 0.15625, ((0, 4),)),
        "final_proj": noise(seeds[6], (INNER, D), INNER ** -0.5, 0.109375, ((0, 4),)),
        "norm_gain": jnp.clip(1.0 + 0.1 * jax.random.normal(seeds[7], (D,), jnp.float32), 0.5, 1.5),
        "conv_kernel": noise(seeds[8], (CONV_K, CONV_CH), CONV_K ** -0.5, 3.0, (), jnp.float32),
        "conv_bias": noise(seeds[9], (CONV_CH,), 0.5, 3.0, (), jnp.float32),
        "step_offset": jnp.clip(jax.random.uniform(seeds[10], (HEADS,), jnp.float32, -4.5, -2.0), -4.5, -2.0),
        "log_rates": jnp.clip(jax.random.uniform(seeds[11], (HEADS,), jnp.float32, -3.0, 0.5), -3.0, 0.5),
        "skip_gain": jnp.clip(jax.random.uniform(seeds[12], (HEADS,), jnp.float32, 0.5, 1.5), 0.5, 1.5),
        "gating_gain": jnp.clip(1.0 + 0.1 * jax.random.normal(seeds[13], (INNER,), jnp.float32), 0.5, 1.5),
    }


HIGH = lax.Precision.HIGHEST
eps = 1e-05

@jax.custom_vjp
def low(v):
    return lax.optimization_barrier(v.astype(jnp.bfloat16)).astype(jnp.float32)

@jax.custom_vjp
def low_back(v):
    return v

def low_keep(v):
    return (low(v), None)

def low_pass(kept, grad):
    return (grad,)

def back_keep(v):
    return (v, None)

def back_low(kept, grad):
    return (low(grad),)
low.defvjp(low_keep, low_pass)
low_back.defvjp(back_keep, back_low)

def project(values, matrix):
    return jnp.einsum('gtd,df->gtf', values, matrix, precision=HIGH)

def tiny_norm(values, gain_vec):
    inverse_rms = lax.rsqrt(lax.optimization_barrier(jnp.mean(values * values, -1, keepdims=True)) + eps)
    return values * inverse_rms * gain_vec

def convolve(mixer_in, segments, conv_kernel, conv_bias):
    group_size = mixer_in.shape[0]
    lead_rows = jnp.zeros((group_size, CONV_K - 1, mixer_in.shape[2]), jnp.float32)
    extended = jnp.concatenate([lead_rows, mixer_in], axis=1)
    lead_seg = jnp.full((group_size, CONV_K - 1), -1, jnp.int32)
    padded = jnp.concatenate([lead_seg, segments.astype(jnp.int32)], axis=1)
    accumulated = conv_bias
    for lag in range(CONV_K):
        offset = CONV_K - 1 - lag
        keeping = (padded[:, offset:offset + SEQ_LEN] == segments).astype(jnp.float32)
        accumulated = accumulated + conv_kernel[lag] * extended[:, offset:offset + SEQ_LEN] * keeping[..., None]
    return jax.nn.silu(accumulated)

def split_inputs(conv_out, step_raw, step_offset, log_rates):
    head_values = conv_out[:, :INNER].reshape(conv_out.shape[0], HEADS, HEAD_DIM)
    in_basis = conv_out[:, INNER:INNER + STATE]
    out_basis = conv_out[:, INNER + STATE:]
    step_size = jax.nn.softplus(step_raw + step_offset)
    decay_rate = step_size * -jnp.exp(log_rates)
    return (head_values, in_basis, out_basis, step_size, decay_rate)

def span_step(state_now, last_seg, head_values, in_basis, out_basis, step_size, decay_rate, segment, skip_gain):
    size = segment.shape[0]
    cumulative = jnp.cumsum(decay_rate, axis=0)
    positions = jnp.arange(size)
    keeping = (segment[:, None] == segment[None, :]) & (positions[:, None] >= positions[None, :])
    gaps = jnp.where(keeping[..., None], cumulative[:, None, :] - cumulative[None, :, :], 0.0)
    mixing = jnp.where(keeping[..., None], jnp.exp(gaps), 0.0)
    scores = jnp.dot(out_basis, in_basis.T, precision=HIGH)
    weights = mixing * scores[..., None] * step_size[None, :, :]
    result = jnp.einsum('tsh,shp->thp', weights, head_values, precision=HIGH)
    entry_gate = (segment == last_seg).astype(jnp.float32)[:, None] * jnp.exp(cumulative)
    result = result + entry_gate[..., None] * jnp.einsum('tn,hpn->thp', out_basis, state_now, precision=HIGH)
    result = result + skip_gain[None, :, None] * head_values
    tail_weight = (segment == segment[-1]).astype(jnp.float32)[:, None] * jnp.exp(cumulative[-1][None, :] - cumulative) * step_size
    fresh_state = jnp.einsum('sh,shp,sn->hpn', tail_weight, head_values, in_basis, precision=HIGH)
    carry_gate = (segment[-1] == last_seg).astype(jnp.float32) * jnp.exp(cumulative[-1])
    return (result, fresh_state + carry_gate[:, None, None] * state_now, segment[-1])

def scan_sequence(conv_out, step_raw, segment, step_offset, log_rates, skip_gain):
    head_values, in_basis, out_basis, step_size, decay_rate = split_inputs(conv_out, step_raw, step_offset, log_rates)
    blocks = SEQ_LEN // SPAN

    def reshaped(values):
        return values.reshape((blocks, SPAN) + values.shape[1:])

    def advance(carry, group_data):
        state_now, last_seg = carry
        result, new_state, new_last = span_step(state_now, last_seg, *group_data, skip_gain)
        return ((new_state, new_last), result)
    start = (jnp.zeros((HEADS, HEAD_DIM, STATE), jnp.float32), jnp.array(-1, jnp.int32))
    inputs = tuple((reshaped(values) for values in (head_values, in_basis, out_basis, step_size, decay_rate, segment.astype(jnp.int32))))
    _, outputs = lax.scan(jax.checkpoint(advance), start, inputs)
    return outputs.reshape(SEQ_LEN, HEADS, HEAD_DIM)

def forward(tokens, params, segments):
    gate_proj, mixer_proj, step_proj, final_proj, norm_gain, conv_kernel, conv_bias, step_offset, log_rates, skip_gain, gating_gain = params
    group_size = tokens.shape[0]
    normed = low(tiny_norm(tokens, norm_gain))
    gate_val = low_back(project(normed, gate_proj))
    mixer_in = low(low_back(project(normed, mixer_proj)))
    step_raw = low_back(project(normed, step_proj))
    conv_out = convolve(mixer_in, segments, conv_kernel, conv_bias)
    heads_out = jax.vmap(scan_sequence, in_axes=(0, 0, 0, None, None, None))(conv_out, step_raw, segments, step_offset, log_rates, skip_gain)
    gated = heads_out.reshape(group_size, SEQ_LEN, INNER) * jax.nn.silu(gate_val)
    mixed = low(tiny_norm(gated, gating_gain))
    return tokens + project(mixed, final_proj)

def reference(tokens, segments, cotangent, gate_proj, mixer_proj, step_proj, final_proj, norm_gain, conv_kernel, conv_bias, step_offset, log_rates, skip_gain, gating_gain):
    params = tuple((values.astype(jnp.float32) for values in (gate_proj, mixer_proj, step_proj, final_proj, norm_gain, conv_kernel, conv_bias, step_offset, log_rates, skip_gain, gating_gain)))
    group_size = 4
    groups = SEQS // group_size

    def regroup(values):
        return values.reshape((groups, group_size) + values.shape[1:])

    def group_step(accumulated, group_data):
        block_tokens, block_segments, block_cot = group_data

        def apply_layer(values, weights_all):
            return forward(values, weights_all, block_segments)
        result, pullback = jax.vjp(apply_layer, block_tokens.astype(jnp.float32), params)
        grad_values, grad_params = pullback(block_cot.astype(jnp.float32))
        return (jax.tree.map(jnp.add, accumulated, grad_params), (result, grad_values))
    zeros_all = jax.tree.map(jnp.zeros_like, params)
    summed, (layer_out, grad_tokens) = lax.scan(group_step, zeros_all, (regroup(tokens), regroup(segments), regroup(cotangent)))
    return (layer_out.reshape(SEQS, SEQ_LEN, D), grad_tokens.reshape(SEQS, SEQ_LEN, D), summed[0], summed[1], summed[2], summed[3], summed[4], summed[5], summed[6], summed[7], summed[8], summed[9], summed[10])
```

```python
import functools

import jax
import jax.numpy as jnp
from jax import lax
from jax.experimental import pallas as pl
from jax.experimental.pallas import tpu as pltpu
from jax.sharding import PartitionSpec as P

D = 1536
INNER = 3072
STATE = 128
HEADS = 48
HEAD_DIM = 64
CONV_CH = 3328
LOCAL = 256
GROUP = 8
OWN = 6
HP = OWN * HEAD_DIM
CH = HP + 2 * STATE
ROWS = D // 4
EPS = 1e-05
F32 = jnp.float32
BF16 = jnp.bfloat16
HIGH = lax.Precision.HIGHEST
MASKED = -1e30
VMEM_LIMIT = 56 * 1024 * 1024


def x_shift(value, steps):
    return lax.ppermute(value, "fsdp", [(i, (i + steps) % 4) for i in range(4)])


def y_shift(value, steps):
    pairs = [(r, ((r // 4 + steps) % 4) * 4 + r % 4) for r in range(16)]
    return lax.ppermute(value, "rep", pairs)


def core_swap(value):
    return lax.ppermute(value, "rep", [(r, r ^ 1) for r in range(16)])


def z_swap(value, bit):
    if bit == 0:
        return lax.ppermute(value, "rep", [(r, r ^ 2) for r in range(16)])
    return lax.ppermute(value, "ctx", [(0, 1), (1, 0)])


def ring_gather(own, shift):
    half = own.shape[0] // 2
    below = shift(own, 1)
    above = shift(own, -1)
    far_a = shift(below[:half], 1)
    far_b = shift(above[half:], -1)
    return own, below, jnp.concatenate([far_a, far_b], axis=0), above


def ring_scatter(own, ahead, far, behind, shift):
    half = own.shape[0] // 2
    up = shift(far[:half], 1)
    down = shift(far[half:], -1)
    ahead = jnp.concatenate([ahead[:half] + up, ahead[half:]], axis=0)
    behind = jnp.concatenate([behind[:half], behind[half:] + down], axis=0)
    from_below = shift(ahead, 1)
    from_above = shift(behind, -1)
    return own.astype(F32) + from_below.astype(F32) + from_above.astype(F32)


def sum_z(value):
    value = value + z_swap(value, 0)
    return value + z_swap(value, 1)


def rolled(blocks, start, count):
    twice = jnp.concatenate([blocks, blocks], axis=0)
    return lax.dynamic_slice_in_dim(twice, start % 4, count, axis=0)


def mm(a, b, dims, precision=None):
    return lax.dot_general(a, b, (dims, ((), ())), precision=precision, preferred_element_type=F32)


NN = ((1,), (0,))
NT = ((1,), (1,))
TN = ((0,), (0,))


def lane_ids(rows, cols):
    return lax.broadcasted_iota(jnp.int32, (rows, cols), 1)


def pair(values, p, left):
    return jnp.where(left, values[:, 2 * p : 2 * p + 1], values[:, 2 * p + 1 : 2 * p + 2])


def triangle():
    row = lax.broadcasted_iota(jnp.int32, (LOCAL, LOCAL), 0)
    col = lax.broadcasted_iota(jnp.int32, (LOCAL, LOCAL), 1)
    return row >= col


def mask_bias(cols, rows):
    same = cols[:, 5:6] == rows[0:1, :]
    return jnp.where(same & triangle(), 0.0, MASKED)


def taps(x, halo, cols, k):
    ext = jnp.concatenate([halo, x], axis=0)
    return ext[8 - k : 8 - k + LOCAL] * cols[:, k - 1 : k]


def conv_kernel_fn(
    ctx_ref, xbc_ref, halo_ref, raw_ref, cols_ref, par_ref, hp_ref,
    u_ref, xc_ref, dt_ref, cum_ref, state_ref,
):
    x = xbc_ref[0].astype(F32)
    halo = halo_ref[0]
    cols = cols_ref[0]
    par = par_ref[...]
    hp = hp_ref[...]
    u = par[4:5] + par[0:1] * x
    for k in range(1, 4):
        u = u + par[k : k + 1] * taps(x, halo, cols, k)
    u_ref[0] = u
    xc = u * jax.nn.sigmoid(u)
    xc_ref[0] = xc.astype(BF16)
    raw = raw_ref[0] + hp[0:1]
    dt = jnp.maximum(raw, 0.0) + jnp.log1p(jnp.exp(-jnp.abs(raw)))
    dt_ref[0] = dt
    cum = mm(triangle().astype(F32), dt * hp[1:2], NN, HIGH)
    cum_ref[0] = cum

    @pl.when(ctx_ref[0] == 0)
    def _():
        weight = cols[:, 4:5] * jnp.exp(cum[LOCAL - 1 : LOCAL] - cum) * dt
        left = lane_ids(LOCAL, 128) < HEAD_DIM
        basis = xc[:, HP : HP + STATE].astype(BF16)
        for p in range(3):
            part = xc[:, 128 * p : 128 * p + 128] * pair(weight, p, left)
            state_ref[0, 128 * p : 128 * p + 128] = mm(part.astype(BF16), basis, TN).astype(BF16)

    @pl.when(ctx_ref[0] != 0)
    def _():
        state_ref[0] = jnp.zeros((HP, STATE), BF16)


def scan_kernel_fn(xc_ref, dt_ref, cum_ref, cols_ref, rows_ref, hp_ref, y_ref):
    xc = xc_ref[0]
    dt = dt_ref[0]
    cum = cum_ref[0]
    hp = hp_ref[...]
    cum_t = cum.T
    basis, out_basis = xc[:, HP : HP + STATE], xc[:, HP + STATE :]
    scores = mm(out_basis, basis, NT)
    bias = mask_bias(cols_ref[0], rows_ref[0])
    left = lane_ids(LOCAL, 128) < HEAD_DIM
    left1 = lane_ids(1, 128) < HEAD_DIM
    for p in range(3):
        x = xc[:, 128 * p : 128 * p + 128].astype(F32)
        scaled = (x * pair(dt, p, left)).astype(BF16)
        halves = []
        for h in (2 * p, 2 * p + 1):
            mix = jnp.exp(cum[:, h : h + 1] - cum_t[h : h + 1] + bias) * scores
            halves.append(mm(mix.astype(BF16), scaled, NN))
        y = jnp.where(left, halves[0], halves[1]) + pair(hp[2:3], p, left1) * x
        y_ref[0, :, 128 * p : 128 * p + 128] = y


def gate_kernel_fn(
    ctx_ref, y_ref, state_ref, z_ref, dmix_ref, xc_ref, cum_ref, cols_ref, gain_ref,
    yall_ref, sums_ref,
):
    yall_ref[0] = y_ref[0]

    @pl.when(ctx_ref[0] != 0)
    def _():
        out_basis = xc_ref[0][:, HP + STATE :]
        enter = cols_ref[0][:, 3:4] * jnp.exp(cum_ref[0])
        left = lane_ids(LOCAL, 128) < HEAD_DIM
        for p in range(3):
            at = slice(128 * p, 128 * p + 128)
            yall_ref[0, :, at] += pair(enter, p, left) * mm(out_basis, state_ref[0, at], NT)

    z = z_ref[0]
    gated = yall_ref[0] * (z * jax.nn.sigmoid(z))
    first = jnp.sum(gated * gated, axis=1, keepdims=True)
    second = jnp.sum(dmix_ref[0] * gain_ref[0:1] * gated, axis=1, keepdims=True)
    lane = lane_ids(LOCAL, 128)
    both = jnp.where(lane == 0, first, jnp.where(lane == 1, second, 0.0))
    sums_ref[0] = both.T[0:8]


def ungate_kernel_fn(
    ctx_ref, y_ref, z_ref, dmix_ref, sums_ref, xc_ref, cum_ref, cols_ref, gain_ref,
    mixed_ref, dy_ref, dz_ref, dstate_ref, dgain_ref,
):
    step = pl.program_id(0)
    pad = jnp.concatenate([sums_ref[0], jnp.zeros((120, LOCAL), F32)], axis=0).T
    inv = lax.rsqrt(pad[:, 0:1] / INNER + EPS)
    mean_ev = inv * pad[:, 1:2] / INNER
    y = y_ref[0]
    z = z_ref[0]
    dmix = dmix_ref[0]
    gain = gain_ref[0:1]
    sig = jax.nn.sigmoid(z)
    act = z * sig
    v = y * act * inv
    mixed_ref[0] = (v * gain).astype(BF16)
    d_gated = inv * (dmix * gain - v * mean_ev)
    dy = (d_gated * act).astype(BF16)
    dy_ref[0] = dy
    dz_ref[0] = (d_gated * y * sig * (1.0 + z * (1.0 - sig))).astype(BF16)
    part = jnp.sum(dmix * v, axis=0, keepdims=True)

    @pl.when(step == 0)
    def _():
        dgain_ref[...] = jnp.zeros_like(dgain_ref)

    dgain_ref[0:1] += part

    @pl.when(ctx_ref[0] != 0)
    def _():
        out_basis = xc_ref[0][:, HP + STATE :]
        enter = cols_ref[0][:, 3:4] * jnp.exp(cum_ref[0])
        left = lane_ids(LOCAL, 128) < HEAD_DIM
        for p in range(3):
            at = slice(128 * p, 128 * p + 128)
            part = (dy[:, at].astype(F32) * pair(enter, p, left)).astype(BF16)
            dstate_ref[0, at] = mm(part, out_basis, TN).astype(BF16)

    @pl.when(ctx_ref[0] == 0)
    def _():
        dstate_ref[0] = jnp.zeros((HP, STATE), BF16)


def back_scan_kernel_fn(
    ctx_ref, dy_ref, xc_ref, dt_ref, cum_ref, cols_ref, rows_ref, hp_ref, state_ref,
    dxs_ref, dbc_ref, dcum_ref, ddt_ref, dskip_ref, turn_ref,
):
    step = pl.program_id(0)
    xc = xc_ref[0]
    dy = dy_ref[0]
    dt = dt_ref[0]
    cum = cum_ref[0]
    hp = hp_ref[...]
    cum_t = cum.T
    dt_t = dt.T
    basis, out_basis = xc[:, HP : HP + STATE], xc[:, HP + STATE :]
    scores = mm(out_basis, basis, NT)
    bias = mask_bias(cols_ref[0], rows_ref[0])
    lane = lane_ids(LOCAL, 128)
    left = lane < HEAD_DIM
    left1 = lane_ids(1, 128) < HEAD_DIM

    @pl.when(step == 0)
    def _():
        dskip_ref[...] = jnp.zeros_like(dskip_ref)

    turn_ref[...] = jnp.zeros_like(turn_ref)
    d_scores = jnp.zeros((LOCAL, LOCAL), F32)
    row_sums = jnp.zeros((LOCAL, 128), F32)
    for p in range(3):
        at = slice(128 * p, 128 * p + 128)
        x = xc[:, at]
        g = dy[:, at]
        halves = []
        for h in (2 * p, 2 * p + 1):
            mine = left if h % 2 == 0 else ~left
            prod = mm(jnp.where(mine, g, jnp.zeros_like(g)), x, NT)
            mix = jnp.exp(cum[:, h : h + 1] - cum_t[h : h + 1] + bias)
            weighed = mix * prod
            d_scores = d_scores + weighed * dt_t[h : h + 1]
            kp = weighed * scores
            turn_ref[h : h + 1] = jnp.sum(kp, axis=0, keepdims=True)
            rows = jnp.sum(kp * dt_t[h : h + 1], axis=1, keepdims=True)
            row_sums = jnp.where(lane == h, rows, row_sums)
            halves.append(mm((mix * scores).astype(BF16), g, TN))
        gf = g.astype(F32)
        skip = pair(hp[2:3], p, left1)
        dxs_ref[0, :, at] = pair(dt, p, left) * jnp.where(left, halves[0], halves[1]) + skip * gf
        dskip_ref[0:1, at] += jnp.sum(gf * x.astype(F32), axis=0, keepdims=True)
    ddt = turn_ref[...].T
    ddt_ref[0] = ddt
    dcum_ref[0] = row_sums - dt * ddt
    low = d_scores.astype(BF16)
    dbc_ref[0, :, 0:STATE] = mm(low, out_basis, TN)
    dbc_ref[0, :, STATE:] = mm(low, basis, NN)

    @pl.when(ctx_ref[0] != 0)
    def _():
        enter = cols_ref[0][:, 3:4] * jnp.exp(cum)
        d_out = jnp.zeros((LOCAL, STATE), F32)
        extra = jnp.zeros((LOCAL, 128), F32)
        for p in range(3):
            at = slice(128 * p, 128 * p + 128)
            gate = pair(enter, p, left)
            state = state_ref[0, at]
            scaled = dy[:, at].astype(F32) * gate
            d_out = d_out + mm(scaled.astype(BF16), state, NN)
            both = scaled * mm(out_basis, state, NT)
            for h, mine in ((2 * p, left), (2 * p + 1, ~left)):
                total = jnp.sum(jnp.where(mine, both, 0.0), axis=1, keepdims=True)
                extra = jnp.where(lane == h, total, extra)
        dbc_ref[0, :, STATE:] += d_out
        dcum_ref[0] += extra


def back_conv_kernel_fn(
    ctx_ref, dxs_ref, dbc_ref, dcum_ref, ddt_ref, xc_ref, u_ref, xbc_ref, halo_ref, dt_ref,
    cum_ref, raw_ref, cols_ref, par_ref, hp_ref, dstate_ref,
    dxbc_ref, dhalo_ref, draw_ref, dpar_ref, dhead_ref, dxc_ref, dc_ref, dd_ref,
):
    step = pl.program_id(0)
    cols = cols_ref[0]
    par = par_ref[...]
    hp = hp_ref[...]
    dt = dt_ref[0]
    lane = lane_ids(LOCAL, 128)
    left = lane < HEAD_DIM
    dxc_ref[:, 0:HP] = dxs_ref[0]
    dxc_ref[:, HP:] = dbc_ref[0]
    dc_ref[...] = dcum_ref[0]
    dd_ref[...] = ddt_ref[0]

    @pl.when(step == 0)
    def _():
        dpar_ref[...] = jnp.zeros_like(dpar_ref)
        dhead_ref[...] = jnp.zeros_like(dhead_ref)

    @pl.when(ctx_ref[0] == 0)
    def _():
        cum = cum_ref[0]
        tail = cols[:, 4:5] * jnp.exp(cum[LOCAL - 1 : LOCAL] - cum)
        weight = tail * dt
        basis = xc_ref[0][:, HP : HP + STATE]
        d_basis = jnp.zeros((LOCAL, STATE), F32)
        d_weight = jnp.zeros((LOCAL, 128), F32)
        for p in range(3):
            at = slice(128 * p, 128 * p + 128)
            x = xc_ref[0][:, at].astype(F32)
            w = pair(weight, p, left)
            ds = dstate_ref[0, at]
            seen = mm(basis, ds, NT)
            dxc_ref[:, at] += w * seen
            d_basis = d_basis + mm((x * w).astype(BF16), ds, NN)
            both = x * seen
            for h, mine in ((2 * p, left), (2 * p + 1, ~left)):
                total = jnp.sum(jnp.where(mine, both, 0.0), axis=1, keepdims=True)
                d_weight = jnp.where(lane == h, total, d_weight)
        dxc_ref[:, HP : HP + STATE] += d_basis
        dd_ref[...] += tail * d_weight
        moved = weight * d_weight
        dc_ref[...] -= moved
        dc_ref[LOCAL - 1 : LOCAL] += jnp.sum(moved, axis=0, keepdims=True)

    d_decay = mm(triangle().astype(F32), dc_ref[...], TN, HIGH)
    rate = hp[1:2]
    d_raw = (dd_ref[...] + d_decay * rate) * jax.nn.sigmoid(raw_ref[0] + hp[0:1])
    draw_ref[0] = d_raw.astype(BF16)
    dhead_ref[0:1] += jnp.sum(d_decay * dt, axis=0, keepdims=True) * rate
    dhead_ref[1:2] += jnp.sum(d_raw, axis=0, keepdims=True)

    x = xbc_ref[0].astype(F32)
    halo = halo_ref[0]
    u = u_ref[0]
    sig = jax.nn.sigmoid(u)
    du = dxc_ref[...] * sig * (1.0 + u * (1.0 - sig))
    dpar_ref[4:5] += jnp.sum(du, axis=0, keepdims=True)
    dpar_ref[0:1] += jnp.sum(du * x, axis=0, keepdims=True)
    zeros = jnp.zeros((8, CH), F32)
    total = par[0:1] * du
    before = jnp.zeros((8, CH), F32)
    for k in range(1, 4):
        dpar_ref[k : k + 1] += jnp.sum(du * taps(x, halo, cols, k), axis=0, keepdims=True)
        ext = jnp.concatenate([zeros, du * cols[:, k - 1 : k] * par[k : k + 1], zeros], axis=0)
        total = total + ext[8 + k : 8 + k + LOCAL]
        before = before + ext[k : k + 8]
    dxbc_ref[0] = total.astype(BF16)
    dhalo_ref[0] = before


def spec(*shape):
    return shape


def call(fn, name, inputs, outputs, scratch=()):
    def block(shape, blocked):
        if blocked:
            rest = tuple(shape[1:])
            return pl.BlockSpec((1,) + rest, lambda i: (i,) + (0,) * len(rest))
        return pl.BlockSpec(tuple(shape), lambda i: (0,) * len(shape))

    in_specs = []
    for value, blocked in inputs:
        if value.ndim == 1:
            in_specs.append(pl.BlockSpec(memory_space=pltpu.SMEM))
        else:
            in_specs.append(block(value.shape, blocked))
    return pl.pallas_call(
        fn,
        name=name,
        grid=(GROUP,),
        in_specs=in_specs,
        out_specs=[block(shape, blocked) for shape, _, blocked in outputs],
        out_shape=[jax.ShapeDtypeStruct(shape, dtype) for shape, dtype, _ in outputs],
        scratch_shapes=list(scratch),
        compiler_params=pltpu.CompilerParams(
            dimension_semantics=("arbitrary",), vmem_limit_bytes=VMEM_LIMIT
        ),
    )(*[value for value, _ in inputs])


def place_kernel_fn(extra, where_ref, own_ref, sib_ref, out_ref):
    y = where_ref[0]
    core = where_ref[1]
    for mine, refs in ((0, (own_ref, sib_ref)), (1, (sib_ref, own_ref))):

        @pl.when(core == mine)
        def _(refs=refs):
            for c in range(2):
                for line in range(4):
                    slot = lax.rem(y - line + 4, 4)
                    block = refs[c][slot].astype(F32)
                    for a in range(2):
                        first = (2 * c + a) * 768 + 192 * line
                        out_ref[:, first : first + 192] = block[:, 192 * a : 192 * a + 192]
                if extra:
                    total = refs[c][0, :, HP:].astype(F32)
                    for slot in range(1, 4):
                        total = total + refs[c][slot, :, HP:].astype(F32)
                    out_ref[:, INNER + STATE * c : INNER + STATE * c + STATE] = total


def place(where, own, sib, columns):
    block = ROWS // 4
    width = own.shape[2]
    return pl.pallas_call(
        functools.partial(place_kernel_fn, columns > INNER),
        name="place_slabs",
        grid=(4,),
        in_specs=[
            pl.BlockSpec(memory_space=pltpu.SMEM),
            pl.BlockSpec((4, block, width), lambda i: (0, i, 0)),
            pl.BlockSpec((4, block, width), lambda i: (0, i, 0)),
        ],
        out_specs=pl.BlockSpec((block, columns), lambda i: (i, 0)),
        out_shape=jax.ShapeDtypeStruct((ROWS, columns), F32),
        compiler_params=pltpu.CompilerParams(
            dimension_semantics=("arbitrary",), vmem_limit_bytes=VMEM_LIMIT
        ),
    )(where, own, sib)


def dot(left, right, dims, dtype=F32):
    out = lax.dot_general(left, right, (dims, ((), ())), preferred_element_type=F32)
    return out.astype(dtype)


def per_device(
    tokens,
    segments,
    cotangent,
    gate_proj,
    mixer_proj,
    step_proj,
    final_proj,
    norm_gain,
    conv_kernel,
    conv_bias,
    step_offset,
    log_rates,
    skip_gain,
    gating_gain,
):
    ctx = lax.axis_index("ctx")
    x = lax.axis_index("fsdp")
    rep = lax.axis_index("rep")
    y, core = rep // 4, rep % 2
    flag = ctx.astype(jnp.int32).reshape(1)
    heads_at = [12 * (2 * core + a) + 3 * y for a in range(2)]

    def slab(values):
        wide = values.shape[-1] // HEADS
        parts = [
            lax.dynamic_slice_in_dim(values, at * wide, 3 * wide, axis=values.ndim - 1)
            for at in heads_at
        ]
        return jnp.concatenate(parts, axis=-1)

    def padded(values, width):
        return jnp.pad(values, [(0, 0)] * (values.ndim - 1) + [(0, width - values.shape[-1])])

    tokens_f = tokens.reshape(LOCAL, D).astype(F32)
    inv_rms = lax.rsqrt(jnp.mean(tokens_f * tokens_f, axis=1, keepdims=True) + EPS)
    normed = (tokens_f * inv_rms * norm_gain).astype(BF16)
    normed = lax.dynamic_slice_in_dim(
        jnp.concatenate([normed, normed], axis=1), ROWS * x, D, axis=1
    )
    own_seg = lax.dynamic_slice_in_dim(segments, ctx * LOCAL, LOCAL, axis=1)
    seg_row = padded(own_seg.astype(BF16), D)
    payload = jnp.concatenate([normed, jnp.pad(seg_row, ((0, 15), (0, 0)))], axis=0)

    def over_y(value):
        own, below, far, above = ring_gather(value, y_shift)
        mine = [own, below, far, above]
        return mine + [core_swap(part) for part in mine]

    token_parts = over_y(payload)
    normed_all = jnp.concatenate([part[:LOCAL] for part in token_parts], axis=0)
    seg_all = jnp.stack([part[LOCAL, :LOCAL] for part in token_parts]).astype(F32)

    x_part, bc_part = mixer_proj[:, :INNER], mixer_proj[:, INNER:]
    weight_x = jnp.concatenate([slab(x_part), bc_part, padded(slab(step_proj), 128)], axis=1)
    weight_z = slab(gate_proj)

    def over_x(value):
        own, below, far, above = ring_gather(value, x_shift)
        return jnp.concatenate([own, above, far, below], axis=0)

    full_x = over_x(weight_x)
    full_z = over_x(weight_z)
    w_xbc, w_step = full_x[:, :CH], full_x[:, CH:]

    rows_final = lax.dynamic_slice(final_proj, (192 * y, 768 * core), (192, 768))
    own, below, far, above = ring_gather(rows_final, x_shift)
    owners = jnp.stack([own, above, far, below])
    kept = rolled(owners, 2 * core - x + 4, 2).reshape(HP, 768)
    other = core_swap(rolled(owners, 2 - 2 * core - x + 4, 2)).reshape(HP, 768)
    w_final = jnp.where(
        core == 0, jnp.concatenate([kept, other], 1), jnp.concatenate([other, kept], 1)
    )

    cot = cotangent.reshape(LOCAL, D)
    cot_all = jnp.concatenate(over_y(cot), axis=0)

    seg = seg_all[:, :, None]
    shifted = [
        jnp.concatenate([seg[:, :k], seg[:, : LOCAL - k]], axis=1) == seg for k in range(1, 4)
    ]
    enter = (seg == seg[:, :1]) & (ctx == 1)
    tail = seg == seg[:, LOCAL - 1 :]
    cols = jnp.concatenate([m.astype(F32) for m in shifted + [enter, tail]] + [seg, seg, seg], -1)
    seg_rows = jnp.broadcast_to(seg_all[:, None, :], (GROUP, 8, LOCAL))
    par = jnp.concatenate(
        [slab(conv_kernel[:, :INNER]), conv_kernel[:, INNER:]], axis=1
    )
    bias = jnp.concatenate([slab(conv_bias[:INNER]), conv_bias[INNER:]])
    par = jnp.concatenate([par, bias[None], jnp.zeros((3, CH), F32)], axis=0)
    hp = jnp.stack([slab(step_offset), -jnp.exp(slab(log_rates)), slab(skip_gain)])
    hp = jnp.pad(hp, ((0, 5), (0, 128 - OWN)))
    gain = jnp.broadcast_to(slab(gating_gain)[None], (8, HP))

    def grouped(values):
        return values.reshape((GROUP, LOCAL) + values.shape[1:])

    xbc = grouped(dot(normed_all, w_xbc, NN, BF16))
    last = lax.ppermute(xbc[:, LOCAL - 3 :], "ctx", [(0, 1)])
    halo = jnp.pad(last.astype(F32), ((0, 0), (5, 0), (0, 0)))
    raw = grouped(dot(normed_all, w_step, NN))
    z = grouped(dot(normed_all, full_z, NN))

    token = (GROUP, LOCAL, 128)
    u, xc, dt, cum, state = call(
        conv_kernel_fn,
        "conv_states",
        [(flag, 0), (xbc, 1), (halo, 1), (raw, 1), (cols, 1), (par, 0), (hp, 0)],
        [
            ((GROUP, LOCAL, CH), F32, 1),
            ((GROUP, LOCAL, CH), BF16, 1),
            (token, F32, 1),
            (token, F32, 1),
            ((GROUP, HP, STATE), BF16, 1),
        ],
    )
    state_in = lax.ppermute(state, "ctx", [(0, 1)])
    dmix = grouped(dot(cot_all, w_final, NT))
    wide = (GROUP, LOCAL, HP)
    (y_local,) = call(
        scan_kernel_fn,
        "scan",
        [(xc, 1), (dt, 1), (cum, 1), (cols, 1), (seg_rows, 1), (hp, 0)],
        [(wide, F32, 1)],
    )
    y_all, sums = call(
        gate_kernel_fn,
        "gate",
        [
            (flag, 0), (y_local, 1), (state_in, 1), (z, 1), (dmix, 1), (xc, 1), (cum, 1),
            (cols, 1), (gain, 0),
        ],
        [(wide, F32, 1), ((GROUP, 8, LOCAL), F32, 1)],
    )

    swapped = core_swap(sums)
    sums = sums + jnp.concatenate([swapped[4:], swapped[:4]], axis=0)
    total = sums
    for steps in (1, 2, 3):
        got = y_shift(sums, steps).reshape(2, 4, 8, LOCAL)
        got = jnp.concatenate([got[:, 4 - steps :], got[:, : 4 - steps]], axis=1)
        total = total + got.reshape(GROUP, 8, LOCAL)

    mixed, dy, dz, dstate, dgain = call(
        ungate_kernel_fn,
        "ungate",
        [
            (flag, 0), (y_all, 1), (z, 1), (dmix, 1), (total, 1), (xc, 1), (cum, 1), (cols, 1),
            (gain, 0),
        ],
        [
            (wide, BF16, 1),
            (wide, BF16, 1),
            (wide, BF16, 1),
            ((GROUP, HP, STATE), BF16, 1),
            ((8, HP), F32, 0),
        ],
    )
    dstate_in = lax.ppermute(dstate, "ctx", [(1, 0)])

    def back_over_y(partial):
        mine, theirs = partial[: 4 * LOCAL], partial[4 * LOCAL :]
        both = (mine.astype(F32) + core_swap(theirs).astype(F32)).astype(BF16)
        blocks = both.reshape(4, LOCAL, D)
        return ring_scatter(blocks[0], blocks[3], blocks[2], blocks[1], y_shift)

    mixed_rows = mixed.reshape(GROUP * LOCAL, HP)
    layer_out = tokens_f + back_over_y(dot(mixed_rows, w_final, NN, BF16))

    g_final = dot(mixed_rows, cot_all, TN, BF16)
    kept = lax.dynamic_slice_in_dim(g_final, 768 * core, 768, axis=1).reshape(2, 192, 768)
    other = lax.dynamic_slice_in_dim(g_final, 768 - 768 * core, 768, axis=1)
    other = core_swap(other).reshape(2, 192, 768)
    owners = jnp.where(
        core == 0, jnp.concatenate([kept, other], 0), jnp.concatenate([other, kept], 0)
    )
    owners = rolled(owners, x, 4)
    piece = ring_scatter(owners[0], owners[1], owners[2], owners[3], x_shift).astype(BF16)
    piece = sum_z(piece)
    own, below, far, above = ring_gather(piece, y_shift)
    lines = rolled(jnp.stack([own, above, far, below]), 4 - y, 4)
    others = core_swap(lines)
    grad_final = jnp.where(
        core == 0, jnp.concatenate([lines, others], 2), jnp.concatenate([others, lines], 2)
    ).reshape(768, D).astype(F32)

    dxs, dbc, dcum, ddt, dskip = call(
        back_scan_kernel_fn,
        "back_scan",
        [
            (flag, 0), (dy, 1), (xc, 1), (dt, 1), (cum, 1), (cols, 1), (seg_rows, 1), (hp, 0),
            (state_in, 1),
        ],
        [
            (wide, F32, 1),
            ((GROUP, LOCAL, 2 * STATE), F32, 1),
            (token, F32, 1),
            (token, F32, 1),
            ((8, HP), F32, 0),
        ],
        [pltpu.VMEM((128, LOCAL), F32)],
    )
    dxbc, dhalo, draw, dpar, dhead = call(
        back_conv_kernel_fn,
        "back_conv",
        [
            (flag, 0), (dxs, 1), (dbc, 1), (dcum, 1), (ddt, 1), (xc, 1), (u, 1), (xbc, 1),
            (halo, 1), (dt, 1), (cum, 1), (raw, 1), (cols, 1), (par, 0), (hp, 0), (dstate_in, 1),
        ],
        [
            ((GROUP, LOCAL, CH), BF16, 1),
            ((GROUP, 8, CH), F32, 1),
            (token, BF16, 1),
            ((8, CH), F32, 0),
            ((8, 128), F32, 0),
        ],
        [
            pltpu.VMEM((LOCAL, CH), F32),
            pltpu.VMEM((LOCAL, 128), F32),
            pltpu.VMEM((LOCAL, 128), F32),
        ],
    )
    returned = lax.ppermute(dhalo[:, 5:].astype(BF16), "ctx", [(1, 0)])

    dz_rows = dz.reshape(GROUP * LOCAL, HP)
    g_gate = dot(normed_all, dz_rows, TN)
    d_normed = dot(dz_rows, full_z, NT)

    dxbc = jnp.concatenate(
        [
            dxbc[:, : LOCAL - 3],
            (dxbc[:, LOCAL - 3 :].astype(F32) + returned.astype(F32)).astype(BF16),
        ],
        axis=1,
    ).reshape(GROUP * LOCAL, CH)
    draw_rows = draw.reshape(GROUP * LOCAL, 128)
    d_normed = d_normed + dot(dxbc, w_xbc, NT) + dot(draw_rows, w_step, NT)
    d_normed = back_over_y(d_normed.astype(BF16))
    d_normed = lax.dynamic_slice_in_dim(
        jnp.concatenate([d_normed, d_normed], axis=1), D - ROWS * x, D, axis=1
    )
    w = tokens_f * inv_rms
    e1 = d_normed * norm_gain
    grad_tokens = cot.astype(F32) + inv_rms * (
        e1 - w * jnp.mean(e1 * w, axis=1, keepdims=True)
    )

    g_mixer = dot(normed_all, dxbc, TN)
    g_step = dot(draw_rows, normed_all, TN)
    norm_rows = (
        jnp.sum(g_gate * full_z.astype(F32), axis=1)
        + jnp.sum(g_mixer * w_xbc.astype(F32), axis=1)
        + jnp.sum(g_step.T * w_step.astype(F32), axis=1)
    )

    where = jnp.stack([y, core]).astype(jnp.int32)

    def slab_sum(slabs):
        blocks = slabs.reshape(4, ROWS, slabs.shape[1])
        piece = ring_scatter(blocks[0], blocks[1], blocks[2], blocks[3], x_shift)
        piece = sum_z(piece.astype(BF16))
        own, below, far, above = ring_gather(piece, y_shift)
        stack = jnp.stack([own, below, far, above])
        return stack, core_swap(stack)

    grad_gate = place(where, *slab_sum(g_gate.astype(BF16)), INNER)

    low = g_mixer.astype(BF16)
    parts = low[:, HP : HP + STATE], low[:, HP + STATE :]
    keep_bc = jnp.where(core == 0, parts[0], parts[1])
    send_bc = jnp.where(core == 0, parts[1], parts[0])
    low = jnp.concatenate([low[:, :HP], keep_bc + core_swap(send_bc)], axis=1)
    grad_mixer = place(where, *slab_sum(low), CONV_CH)

    top = jnp.concatenate([g_step[:OWN], norm_rows[None] / 1.0], axis=0)
    top = lax.dynamic_slice_in_dim(jnp.concatenate([top, top], axis=1), D - ROWS * x, D, axis=1)
    heads = jnp.sum(dskip[0].reshape(OWN, HEAD_DIM), axis=1)
    flat = jnp.concatenate(
        [dpar[:5].reshape(-1), dgain[0], heads, dhead[0, :OWN], dhead[1, :OWN]]
    )
    flat = jnp.pad(flat, (0, 9 * D - flat.shape[0])).reshape(9, D)
    small = jnp.concatenate([top, flat], axis=0)
    small = small + x_shift(small, 1) + x_shift(small, 2) + x_shift(small, 3)
    small = small + z_swap(small, 0)
    small = small + z_swap(small, 1)
    slots = jnp.stack([small, y_shift(small, -1), y_shift(small, 2), y_shift(small, 1)])
    lines = rolled(slots, 4 - y, 4)
    others = core_swap(lines)
    every = jnp.where(
        core == 0, jnp.stack([lines, others], 1), jnp.stack([others, lines], 1)
    )

    def whole(values):
        rows = values.shape[2]
        values = values.reshape(4, 2, rows, 2, -1)
        return values.transpose(2, 1, 3, 0, 4).reshape(rows, -1)

    mine = lax.dynamic_slice_in_dim(every[:, :, :OWN], ROWS * x, ROWS, axis=3)
    grad_step = whole(mine.transpose(0, 1, 3, 2))
    grad_norm = jnp.sum(every[:, :, OWN], axis=(0, 1)) / norm_gain
    flat = every[:, :, 7:].reshape(4, 2, 9 * D)
    conv = flat[:, :, : 5 * CH].reshape(4, 2, 5, CH)
    conv = jnp.concatenate([whole(conv[..., :HP]), jnp.sum(conv[..., HP:], axis=(0, 1))], axis=1)
    at = 5 * CH
    grad_gating = whole(flat[:, :, None, at : at + HP])[0]
    at += HP
    grad_skip, grad_rates, grad_offset = [
        whole(flat[:, :, None, at + OWN * i : at + OWN * i + OWN])[0] for i in range(3)
    ]
    shape = (1, LOCAL, D)
    return (
        layer_out.reshape(shape),
        grad_tokens.reshape(shape),
        grad_gate,
        grad_mixer,
        grad_step,
        grad_final,
        grad_norm,
        conv[:4],
        conv[4],
        grad_offset,
        grad_rates,
        grad_skip,
        grad_gating,
    )


def solution(mesh):
    tokens = P(("fsdp", "rep"), "ctx", None)
    rows = P("fsdp", None)
    return jax.shard_map(
        per_device,
        mesh=mesh,
        in_specs=(tokens, P(("fsdp", "rep"), None), tokens, rows, rows, rows, rows) + (P(),) * 7,
        out_specs=(tokens, tokens, rows, rows, rows, rows) + (P(),) * 7,
        check_vma=False,
    )
```

```python
import functools

import jax
import jax.numpy as jnp
from jax import lax
from jax.experimental import pallas as pl
from jax.experimental.pallas import tpu as pltpu
from jax.sharding import PartitionSpec as P

D = 1536
INNER = 3072
STATE = 128
HEADS = 48
HEAD_DIM = 64
CONV_CH = 3328
LOCAL = 256
GROUP = 8
OWN = 6
HP = OWN * HEAD_DIM
CH = HP + 2 * STATE
ROWS = D // 4
EPS = 1e-05
AXES = ("ctx", "fsdp", "y", "low", "core")
F32 = jnp.float32
BF16 = jnp.bfloat16
HIGH = lax.Precision.HIGHEST
MASKED = -1e30
PAY = LOCAL + 16
CUT = 144
WIDE = CH + 128 + HP
MIX = CH + 128
DURATION = {
    "pack": 4, "prep": 3, "params": 2, "forward_own": 21, "forward_sib": 20, "d_mixed": 11, "gate": 9,
    "out_proj": 9, "ungate": 11, "grad_final": 5, "grad_gate": 10, "back": 11, "grad_mixer": 13,
    "back_proj": 10, "split": 3, "lines": 2, "place_early": 7, "place_late": 6, "place_small": 2,
}
VMEM_LIMIT = 60 * 1024 * 1024


def place_of(ctx, x, y, low, core):
    return (ctx * 4 + x) * 16 + (y * 2 + low) * 2 + core


def pairs_of(move):
    pairs = []
    for ctx in range(2):
        for x in range(4):
            for y in range(4):
                for low in range(2):
                    for core in range(2):
                        to = move(ctx, x, y, low, core)
                        if to is not None:
                            pairs.append((place_of(ctx, x, y, low, core), place_of(*to)))
    return pairs


def move(value, to):
    return lax.ppermute(value, AXES, pairs_of(to))


def x_shift(value, steps):
    return lax.ppermute(value, "fsdp", [(i, (i + steps) % 4) for i in range(4)])


def y_shift(value, steps):
    return lax.ppermute(value, "y", [(i, (i + steps) % 4) for i in range(4)])


def core_swap(value):
    return lax.ppermute(value, "core", [(0, 1), (1, 0)])


def z_shift(value, steps):
    def to(ctx, x, y, low, core):
        z = (2 * ctx + low + steps) % 4
        return (z // 2, x, y, z % 2, core)

    return move(value, to)


def after(value, *others):
    return lax.optimization_barrier((value,) + others)[0]


def add(*values):
    total = values[0].astype(F32)
    for value in values[1:]:
        total = total + value.astype(F32)
    return total.astype(BF16)


def mm(a, b, dims, precision=None):
    return lax.dot_general(a, b, (dims, ((), ())), precision=precision, preferred_element_type=F32)


NN = ((1,), (0,))
NT = ((1,), (1,))
TN = ((0,), (0,))
SMEM = object()
HBM = object()


def call(fn, name, inputs, outputs, steps=GROUP, scratch=(), aliases=None, ahead=(), wait=()):
    us = DURATION[name]
    first = len(ahead) + len(inputs)
    inputs = inputs + [(value, HBM) for value in wait]

    def kernel(*refs):
        fn(*refs[:first], *refs[first + len(wait) :])

    def block(shape, how):
        if how is SMEM:
            return pl.BlockSpec(memory_space=pltpu.SMEM)
        if how is HBM:
            return pl.BlockSpec(memory_space=pl.ANY)
        if how is None:
            return pl.BlockSpec(tuple(shape), lambda i, *s: (0,) * len(shape))
        return pl.BlockSpec(*how)

    return pl.pallas_call(
        kernel,
        name=name,
        grid_spec=pltpu.PrefetchScalarGridSpec(
            num_scalar_prefetch=len(ahead),
            grid=(steps,),
            in_specs=[block(value.shape, how) for value, how in inputs],
            out_specs=[block(shape, how) for shape, _, how in outputs],
            scratch_shapes=list(scratch),
        ),
        out_shape=[jax.ShapeDtypeStruct(shape, dtype) for shape, dtype, _ in outputs],
        input_output_aliases=aliases or {},
        cost_estimate=pl.CostEstimate(
            flops=int(us * 1.15e9), bytes_accessed=int(us * 3.6e6), transcendentals=0
        ),
        compiler_params=pltpu.CompilerParams(
            dimension_semantics=("arbitrary",), vmem_limit_bytes=VMEM_LIMIT
        ),
    )(*ahead, *[value for value, _ in inputs])


def seq(*rest, first=0, low=0, high=GROUP):
    def at(i, *s):
        return (jnp.clip(i + first, low, high - 1) - low,) + (0,) * len(rest)

    return ((1,) + rest, at)


def by_device(*rest):
    def at(i, at):
        y, core = (at[0] + 4 - i % 4) % 4, (at[1] + i // 4) % 2
        return (2 * y + core,) + (0,) * len(rest)

    return ((1,) + rest, at)


def lane_ids(rows, cols):
    return lax.broadcasted_iota(jnp.int32, (rows, cols), 1)


def pair(values, p, left):
    return jnp.where(left, values[:, 2 * p : 2 * p + 1], values[:, 2 * p + 1 : 2 * p + 2])


def triangle():
    row = lax.broadcasted_iota(jnp.int32, (LOCAL, LOCAL), 0)
    col = lax.broadcasted_iota(jnp.int32, (LOCAL, LOCAL), 1)
    return row >= col


def seg_columns(row):
    return jnp.broadcast_to(row, (128, LOCAL)).T


def same_before(seg, k):
    return jnp.concatenate([seg[:k], seg[: LOCAL - k]], axis=0) == seg


def mask_bias(seg, row):
    wide = jnp.concatenate([seg, seg], axis=1)
    return jnp.where((wide == row) & triangle(), 0.0, MASKED)


def prep_kernel_fn(at_ref, tok_ref, ahead_ref, gain_ref, seg_ref, out_ref, buf_ref):
    def normed(values):
        values = values.astype(F32)
        inv = lax.rsqrt(jnp.mean(values * values, axis=1, keepdims=True) + EPS)
        return (values * inv * gain_ref[...]).astype(BF16)

    buf_ref[0:LOCAL] = normed(tok_ref[...])
    seg = seg_ref[...].astype(F32)
    seg = jnp.where(at_ref[1] == 0, seg[:, :LOCAL], seg[:, LOCAL:])
    part = jnp.concatenate([seg, jnp.zeros((1, ROWS - LOCAL), F32)], axis=1)
    row = jnp.concatenate([part] * 4, axis=1)
    number = lax.broadcasted_iota(jnp.int32, (16, D), 0)
    extra = jnp.where(number >= 8, normed(ahead_ref[...]).astype(F32), 0.0)
    buf_ref[LOCAL:PAY] = jnp.where(number == 0, row, extra).astype(BF16)
    for r in range(4):
        start = pl.multiple_of(ROWS * lax.rem(at_ref[0] + r, 4), 128)
        out_ref[:, ROWS * r : ROWS * r + ROWS] = buf_ref[:, pl.ds(start, ROWS)]


def pack_kernel_fn(
    at_ref, gate_ref, mixer_ref, final_ref, step_ref, slab_ref, rows_ref, buf_ref, wide_ref, sem
):
    y, core = at_ref[0], at_ref[1]
    copies = []
    for i, src in enumerate((mixer_ref, gate_ref)):
        for a in range(2):
            first = (2 * core + a) * 768 + 384 * lax.div(y, 2) + 128 * lax.rem(y, 2)
            where = pl.ds(pl.multiple_of(first, 128), 256)
            copies.append((src.at[:, where], buf_ref.at[2 * i + a]))
    copies.append((mixer_ref.at[:, pl.ds(INNER, 2 * STATE)], buf_ref.at[4]))
    copies.append((final_ref.at[pl.ds(pl.multiple_of(192 * y, 64), 192)], rows_ref))
    copies = [pltpu.make_async_copy(a, b, sem.at[i]) for i, (a, b) in enumerate(copies)]
    for copy in copies:
        copy.start()
    wide_ref[:, CH:MIX] = jnp.zeros((ROWS, 128), F32)
    step = step_ref[...].astype(F32)
    for line in range(4):
        for c in range(2):

            @pl.when((y == line) & (core == c))
            def _(line=line, c=c):
                for a in range(2):
                    at = 12 * (2 * c + a) + 3 * line
                    wide_ref[:, CH + 3 * a : CH + 3 * a + 3] = step[:, at : at + 3]

    for copy in copies:
        copy.wait()
    for odd in range(2):

        @pl.when(lax.rem(y, 2) == odd)
        def _(odd=odd):
            for i, base in enumerate((0, MIX)):
                for a in range(2):
                    block = buf_ref[2 * i + a].astype(F32)
                    to = base + 192 * a
                    wide_ref[:, to : to + 192] = block[:, 64 * odd : 64 * odd + 192]

    slab_ref[...] = wide_ref[...].astype(BF16)
    slab_ref[:, HP:CH] = buf_ref[4]


def params_kernel_fn(
    at_ref, taps_ref, bias_ref, offset_ref, rates_ref, skip_ref, gating_ref,
    par_ref, hp_ref, gain_ref,
):
    par_ref[...] = jnp.zeros_like(par_ref)
    hp_ref[...] = jnp.zeros_like(hp_ref)
    for line in range(4):
        for c in range(2):

            @pl.when((at_ref[0] == line) & (at_ref[1] == c))
            def _(line=line, c=c):
                for a in range(2):
                    at = slice((2 * c + a) * 768 + 192 * line, (2 * c + a) * 768 + 192 * line + 192)
                    to = slice(192 * a, 192 * a + 192)
                    par_ref[0:4, to] = taps_ref[:, at]
                    par_ref[4:5, to] = bias_ref[:, at]
                    gain_ref[0:1, to] = gating_ref[:, at]
                    at = slice(12 * (2 * c + a) + 3 * line, 12 * (2 * c + a) + 3 * line + 3)
                    to = slice(3 * a, 3 * a + 3)
                    hp_ref[0:1, to] = offset_ref[:, at]
                    hp_ref[1:2, to] = -jnp.exp(rates_ref[:, at])
                    hp_ref[2:3, to] = skip_ref[:, at]

    par_ref[0:4, HP:] = taps_ref[:, INNER:]
    par_ref[4:5, HP:] = bias_ref[:, INNER:]


class Pieces:
    def __init__(self, refs, buf, sem, cut):
        own, below, far_a, far_b, above = refs
        self.buf, self.sem, self.whole = buf, sem, own
        self.cut = cut
        self.parts = [[own], [below], [far_a, far_b], [above]]

    def fetch(self, step, slot):
        for k, refs in enumerate(self.parts):

            @pl.when(step == k)
            def _(refs=refs):
                if len(refs) == 1:
                    pltpu.make_async_copy(refs[0], self.buf.at[slot], self.sem.at[slot]).start()
                else:
                    to = self.buf.at[slot]
                    ends = (to.at[0 : self.cut], to.at[self.cut :])
                    for ref, end in zip(refs, ends, strict=True):
                        pltpu.make_async_copy(ref, end, self.sem.at[slot]).start()

    def next(self):
        step = pl.program_id(0)
        slot = lax.rem(step, 2)

        @pl.when(step == 0)
        def _():
            self.fetch(step, slot)

        @pl.when(step < 3)
        def _():
            self.fetch(step + 1, 1 - slot)

        pltpu.make_async_copy(self.whole, self.buf.at[slot], self.sem.at[slot]).wait()
        return slot


def forward_body(
    ctx_ref, par_ref, hp_ref, n, wall_ref,
    nall_ref, xbc_ref, u_ref, xc_ref, dt_ref, cum_ref, raw_ref, z_ref, seg_ref, y_ref, state_ref,
):
    par = par_ref[...]
    hp = hp_ref[...]
    nall_ref[0] = n
    row = n[LOCAL:PAY, 0:LOCAL].astype(F32)[0:1]
    seg_ref[0] = jnp.broadcast_to(row, (8, LOCAL))
    seg = seg_columns(row)
    keeps = [same_before(seg, k) for k in range(1, 4)]
    z_ref[0] = mm(n[0:LOCAL], wall_ref[:, MIX:], NN)
    for j in range(3):
        prod = mm(n, wall_ref[:, 256 * j : 256 * j + 256], NN)
        for half in range(2):
            first = 256 * j + 128 * half
            at = slice(first, first + 128)
            x = prod[:, 128 * half : 128 * half + 128]
            if first == CH:
                raw = x[0:LOCAL] + hp[0:1]
                continue
            low = x.astype(BF16)
            xbc_ref[0, :, at] = low
            x = low.astype(F32)
            ext = jnp.concatenate([x[LOCAL + 8 :], x[:LOCAL]], axis=0)
            u = par[4:5, at] + par[0:1, at] * x[:LOCAL]
            for k in range(1, 4):
                moved = ext[8 - k : 8 - k + LOCAL]
                u = u + par[k : k + 1, at] * jnp.where(keeps[k - 1], moved, 0.0)
            u_ref[0, :, at] = u
            xc_ref[0, :, at] = (u * jax.nn.sigmoid(u)).astype(BF16)
    raw_ref[0] = raw
    dt = jnp.maximum(raw, 0.0) + jnp.log1p(jnp.exp(-jnp.abs(raw)))
    dt_ref[0] = dt
    cum = mm(triangle().astype(F32), dt * hp[1:2], NN, HIGH)
    cum_ref[0] = cum
    left = lane_ids(LOCAL, 128) < HEAD_DIM
    left1 = lane_ids(1, 128) < HEAD_DIM
    basis, out_basis = xc_ref[0, :, HP : HP + STATE], xc_ref[0, :, HP + STATE :]

    @pl.when(ctx_ref[0] == 0)
    def _():
        tail = jnp.where(seg == seg[LOCAL - 1 :], jnp.exp(cum[LOCAL - 1 :] - cum) * dt, 0.0)
        for p in range(3):
            at = slice(128 * p, 128 * p + 128)
            part = xc_ref[0, :, at].astype(F32) * pair(tail, p, left)
            state_ref[0, at] = mm(part.astype(BF16), basis, TN).astype(BF16)

    @pl.when(ctx_ref[0] != 0)
    def _():
        state_ref[0] = jnp.zeros((HP, STATE), BF16)

    cum_t = cum.T
    scores = mm(out_basis, basis, NT)
    bias = mask_bias(seg, row)
    for p in range(3):
        at = slice(128 * p, 128 * p + 128)
        x = xc_ref[0, :, at].astype(F32)
        scaled = (x * pair(dt, p, left)).astype(BF16)
        halves = []
        for h in (2 * p, 2 * p + 1):
            mix = jnp.exp(cum[:, h : h + 1] - cum_t[h : h + 1] + bias) * scores
            halves.append(mm(mix.astype(BF16), scaled, NN))
        y_ref[0, :, at] = jnp.where(left, halves[0], halves[1]) + pair(hp[2:3], p, left1) * x


def forward_own_fn(*refs):
    ctx_ref, par_ref, hp_ref = refs[:3]
    own, above, far_a, far_b, below = refs[8:13]
    wall_ref, buf, sem, wsem = refs[13], refs[-3], refs[-2], refs[-1]
    copies = []
    first = 0
    for i, ref in enumerate((own, above, far_a, far_b, below)):
        rows = ref.shape[0]
        copies.append(pltpu.make_async_copy(ref, wall_ref.at[first : first + rows], wsem.at[i]))
        first += rows

    @pl.when(pl.program_id(0) == 0)
    def _():
        for copy in copies:
            copy.start()

    slot = Pieces(refs[3:8], buf, sem, CUT).next()

    @pl.when(pl.program_id(0) == 0)
    def _():
        for copy in copies:
            copy.wait()

    forward_body(ctx_ref, par_ref, hp_ref, buf[slot], wall_ref, *refs[14:25])


def forward_sib_fn(*refs):
    ctx_ref, par_ref, hp_ref = refs[:3]
    wall_ref, buf, sem = refs[8], refs[-2], refs[-1]
    slot = Pieces(refs[3:8], buf, sem, CUT).next()
    forward_body(ctx_ref, par_ref, hp_ref, buf[slot], wall_ref, *refs[19:30])


def dmix_kernel_fn(at_ref, g_ref, own, near, far, away, dmix_ref, wf_ref, sem):
    step = pl.program_id(0)
    up, down = wf_ref.at[0:192], wf_ref.at[192:HP]

    @pl.when(step == 0)
    def _():
        for r, (a, b) in enumerate(((own, near), (near, own), (away, far), (far, away))):

            @pl.when(at_ref[2] == r)
            def _(a=a, b=b):
                pltpu.make_async_copy(a, up, sem.at[0]).start()
                pltpu.make_async_copy(b, down, sem.at[1]).start()

        pltpu.make_async_copy(own, up, sem.at[0]).wait()
        pltpu.make_async_copy(own, down, sem.at[1]).wait()

    dmix_ref[0] = mm(g_ref[0], wf_ref[...], NT)


def gate_kernel_fn(
    ctx_ref, y_ref, state_a_ref, state_b_ref, z_ref, dmix_ref, xc_ref, cum_ref, seg_ref, gain_ref,
    yall_ref, low_ref, sums_ref,
):
    yall_ref[0] = y_ref[0]

    @pl.when(ctx_ref[0] != 0)
    def _():
        out_basis = xc_ref[0][:, HP + STATE :]
        seg = seg_columns(seg_ref[0, 0:1])
        enter = jnp.where(seg == seg[0:1], jnp.exp(cum_ref[0]), 0.0)
        left = lane_ids(LOCAL, 128) < HEAD_DIM
        for p in range(3):
            at = slice(128 * p, 128 * p + 128)
            state = jnp.where(pl.program_id(0) < 4, state_a_ref[0, at], state_b_ref[0, at])
            yall_ref[0, :, at] += pair(enter, p, left) * mm(out_basis, state, NT)

    z = z_ref[0]
    gated = yall_ref[0] * (z * jax.nn.sigmoid(z))
    raised = gated * gain_ref[0:1]
    low_ref[0] = raised.astype(BF16)
    first = jnp.sum(gated * gated, axis=1, keepdims=True)
    second = jnp.sum(dmix_ref[0] * raised, axis=1, keepdims=True)
    lane = lane_ids(LOCAL, 128)
    both = jnp.where(lane == 0, first, jnp.where(lane == 1, second, 0.0))
    sums_ref[0] = both.T[0:8]


def product_kernel_fn(at_ref, a_ref, w_ref, out_ref):
    out_ref[0] = mm(a_ref[0], w_ref[...], NN).astype(BF16)


def ungate_kernel_fn(
    at_ref, ctx_ref, y_ref, z_ref, dmix_ref, sums_ref, xc_ref, cum_ref, seg_ref, gain_ref,
    mixed_ref, dy_ref, dz_ref, dstate_ref, dgain_ref,
):
    step = pl.program_id(0)
    pad = jnp.concatenate([sums_ref[0], jnp.zeros((120, LOCAL), F32)], axis=0).T
    inv = lax.rsqrt(pad[:, 0:1] / INNER + EPS)
    mean_ev = inv * pad[:, 1:2] / INNER
    y = y_ref[0]
    z = z_ref[0]
    dmix = dmix_ref[0]
    gain = gain_ref[0:1]
    sig = jax.nn.sigmoid(z)
    act = z * sig
    v = y * act * inv
    mixed_ref[0] = (v * gain).astype(BF16)
    d_gated = inv * (dmix * gain - v * mean_ev)
    dy = (d_gated * act).astype(BF16)
    dy_ref[0] = dy
    dz_ref[0, 0:LOCAL] = (d_gated * y * sig * (1.0 + z * (1.0 - sig))).astype(BF16)
    dz_ref[0, LOCAL:PAY] = jnp.zeros((16, HP), BF16)
    part = jnp.sum(dmix * v, axis=0, keepdims=True)

    @pl.when(step == 0)
    def _():
        dgain_ref[...] = jnp.zeros_like(dgain_ref)

    dgain_ref[0:1] += part

    @pl.when(ctx_ref[0] != 0)
    def _():
        out_basis = xc_ref[0][:, HP + STATE :]
        seg = seg_columns(seg_ref[0, 0:1])
        enter = jnp.where(seg == seg[0:1], jnp.exp(cum_ref[0]), 0.0)
        left = lane_ids(LOCAL, 128) < HEAD_DIM
        for p in range(3):
            at = slice(128 * p, 128 * p + 128)
            part = (dy[:, at].astype(F32) * pair(enter, p, left)).astype(BF16)
            dstate_ref[0, at] = mm(part, out_basis, TN).astype(BF16)

    @pl.when(ctx_ref[0] == 0)
    def _():
        dstate_ref[0] = jnp.zeros((HP, STATE), BF16)


def back_kernel_fn(
    ctx_ref, dy_ref, xc_ref, u_ref, xbc_ref, dt_ref, cum_ref, raw_ref, seg_ref, par_ref, hp_ref,
    state_ref, dstate_ref, skip0_ref, par0_ref, head0_ref, _,
    dx_ref, dskip_ref, dpar_ref, dhead_ref, turn_ref, dxc_ref, dc_ref, dd_ref,
):
    step = pl.program_id(0)
    dt = dt_ref[0]
    cum = cum_ref[0]
    hp = hp_ref[...]
    par = par_ref[...]
    cum_t = cum.T
    dt_t = dt.T
    basis, out_basis = xc_ref[0, :, HP : HP + STATE], xc_ref[0, :, HP + STATE :]
    scores = mm(out_basis, basis, NT)
    row = seg_ref[0, 0:1]
    seg = seg_columns(row)
    bias = mask_bias(seg, row)
    lane = lane_ids(LOCAL, 128)
    left = lane < HEAD_DIM
    left1 = lane_ids(1, 128) < HEAD_DIM

    @pl.when(step == 0)
    def _():
        dskip_ref[...] = skip0_ref[...]
        dpar_ref[...] = par0_ref[...]
        dhead_ref[...] = head0_ref[...]
        turn_ref[...] = jnp.zeros_like(turn_ref)

    d_scores = jnp.zeros((LOCAL, LOCAL), F32)
    row_sums = jnp.zeros((LOCAL, 128), F32)
    for p in range(3):
        at = slice(128 * p, 128 * p + 128)
        x = xc_ref[0, :, at]
        g = dy_ref[0, :, at]
        halves = []
        for h in (2 * p, 2 * p + 1):
            mine = left if h % 2 == 0 else ~left
            prod = mm(jnp.where(mine, g, jnp.zeros_like(g)), x, NT)
            mix = jnp.exp(cum[:, h : h + 1] - cum_t[h : h + 1] + bias)
            weighed = mix * prod
            d_scores = d_scores + weighed * dt_t[h : h + 1]
            kp = weighed * scores
            turn_ref[h : h + 1] = jnp.sum(kp, axis=0, keepdims=True)
            rows = jnp.sum(kp * dt_t[h : h + 1], axis=1, keepdims=True)
            row_sums = jnp.where(lane == h, rows, row_sums)
            halves.append(mm((mix * scores).astype(BF16), g, TN))
        gf = g.astype(F32)
        skip = pair(hp[2:3], p, left1)
        dxc_ref[:, at] = pair(dt, p, left) * jnp.where(left, halves[0], halves[1]) + skip * gf
        dskip_ref[0:1, at] += jnp.sum(gf * x.astype(F32), axis=0, keepdims=True)
    ddt = turn_ref[...].T
    dd_ref[...] = ddt
    dc_ref[...] = row_sums - dt * ddt
    low = d_scores.astype(BF16)
    dxc_ref[:, HP : HP + STATE] = mm(low, out_basis, TN)
    dxc_ref[:, HP + STATE :] = mm(low, basis, NN)

    @pl.when(ctx_ref[0] != 0)
    def _():
        enter = jnp.where(seg == seg[0:1], jnp.exp(cum), 0.0)
        d_out = jnp.zeros((LOCAL, STATE), F32)
        extra = jnp.zeros((LOCAL, 128), F32)
        for p in range(3):
            at = slice(128 * p, 128 * p + 128)
            state = state_ref[0, at]
            scaled = dy_ref[0, :, at].astype(F32) * pair(enter, p, left)
            d_out = d_out + mm(scaled.astype(BF16), state, NN)
            both = scaled * mm(out_basis, state, NT)
            for h, mine in ((2 * p, left), (2 * p + 1, ~left)):
                total = jnp.sum(jnp.where(mine, both, 0.0), axis=1, keepdims=True)
                extra = jnp.where(lane == h, total, extra)
        dxc_ref[:, HP + STATE :] += d_out
        dc_ref[...] += extra

    @pl.when(ctx_ref[0] == 0)
    def _():
        tail = jnp.where(seg == seg[LOCAL - 1 :], jnp.exp(cum[LOCAL - 1 :] - cum), 0.0)
        weight = tail * dt
        d_basis = jnp.zeros((LOCAL, STATE), F32)
        d_weight = jnp.zeros((LOCAL, 128), F32)
        for p in range(3):
            at = slice(128 * p, 128 * p + 128)
            x = xc_ref[0, :, at].astype(F32)
            w = pair(weight, p, left)
            ds = dstate_ref[0, at]
            seen = mm(basis, ds, NT)
            dxc_ref[:, at] += w * seen
            d_basis = d_basis + mm((x * w).astype(BF16), ds, NN)
            both = x * seen
            for h, mine in ((2 * p, left), (2 * p + 1, ~left)):
                total = jnp.sum(jnp.where(mine, both, 0.0), axis=1, keepdims=True)
                d_weight = jnp.where(lane == h, total, d_weight)
        dxc_ref[:, HP : HP + STATE] += d_basis
        dd_ref[...] += tail * d_weight
        moved = weight * d_weight
        dc_ref[...] -= moved
        dc_ref[LOCAL - 1 : LOCAL] += jnp.sum(moved, axis=0, keepdims=True)

    d_decay = mm(triangle().astype(F32), dc_ref[...], TN, HIGH)
    rate = hp[1:2]
    d_raw = (dd_ref[...] + d_decay * rate) * jax.nn.sigmoid(raw_ref[0])
    dhead_ref[0:1] += jnp.sum(d_decay * dt, axis=0, keepdims=True) * rate
    dhead_ref[1:2] += jnp.sum(d_raw, axis=0, keepdims=True)
    low = jnp.where(lane < OWN, d_raw, 0.0).astype(BF16)
    dx_ref[0, 0:LOCAL, CH:MIX] = low
    dx_ref[0, LOCAL:PAY, CH:MIX] = jnp.zeros((16, 128), BF16)

    keeps = [same_before(seg, k) for k in range(1, 4)]
    zeros = jnp.zeros((8, 128), F32)
    for j in range(5):
        at = slice(128 * j, 128 * j + 128)
        x = xbc_ref[0, :, at].astype(F32)
        ext = jnp.concatenate([x[LOCAL + 8 :], x[:LOCAL]], axis=0)
        u = u_ref[0, :, at]
        sig = jax.nn.sigmoid(u)
        du = dxc_ref[:, at] * sig * (1.0 + u * (1.0 - sig))
        dpar_ref[4:5, at] += jnp.sum(du, axis=0, keepdims=True)
        dpar_ref[0:1, at] += jnp.sum(du * x[:LOCAL], axis=0, keepdims=True)
        total = par[0:1, at] * du
        before = zeros
        for k in range(1, 4):
            kept = jnp.where(keeps[k - 1], du, 0.0)
            moved = ext[8 - k : 8 - k + LOCAL]
            dpar_ref[k : k + 1, at] += jnp.sum(kept * moved, axis=0, keepdims=True)
            back = jnp.concatenate([zeros, kept * par[k : k + 1, at], zeros], axis=0)
            total = total + back[8 + k : 8 + k + LOCAL]
            before = before + back[k : k + 8]
        dx_ref[0, 0:LOCAL, at] = total.astype(BF16)
        dx_ref[0, LOCAL:PAY, at] = jnp.concatenate([zeros, before], axis=0).astype(BF16)


def norm_row(grad, weight):
    column = jnp.sum(grad * weight.astype(F32), axis=1, keepdims=True)
    return jnp.broadcast_to(column, (ROWS, 128)).T[0:1]


def early_grad_fn(at_ref, n_ref, d_ref, wall_ref, keep_ref, got_ref, out_ref, norm_ref):
    step = pl.program_id(0)
    grad = mm(n_ref[...], d_ref[...], TN)

    @pl.when(step == 0)
    def _():
        norm_ref[...] = jnp.zeros_like(norm_ref)

    norm_ref[pl.ds(step, 1)] = norm_row(grad, wall_ref[:, MIX:])
    low = grad.astype(BF16)
    owner = lax.rem(at_ref[0] + step, 4)
    for mine, src in ((True, keep_ref), (False, got_ref)):

        @pl.when((lax.div(owner, 2) == at_ref[1]) == mine)
        def _(src=src):
            for q in range(4):
                first = pl.multiple_of(192 * lax.rem(owner, 2) + 48 * q, 16)
                out_ref[0, q, 0:96] = low[96 * q : 96 * q + 96]
                out_ref[0, q, 96:144] = src[pl.ds(first, 48), 0:ROWS]
                out_ref[0, q, 144:192] = src[pl.ds(first, 48), ROWS:]


def late_grad_fn(at_ref, n_ref, d_ref, wall_ref, norm_ref, par_ref, gain_ref, skip_ref, head_ref, *refs):
    step = pl.program_id(0)
    outs, small_ref = refs[:4], refs[4]
    grad = mm(n_ref[...], d_ref[:, 0:CH], TN)
    heads = mm(d_ref[:, CH:], n_ref[...], TN)

    @pl.when(step == 0)
    def _():
        small_ref[...] = jnp.zeros_like(small_ref)
        small_ref[4:9] = par_ref[0:5]
        small_ref[9:10, 0:HP] = gain_ref[0:1]
        small_ref[10:11, 0:HP] = skip_ref[0:1]
        small_ref[11:13, 0:128] = head_ref[0:2]

    owner = lax.rem(at_ref[0] + step, 4)
    row = norm_row(grad, wall_ref[:, 0:CH]) + norm_ref[pl.ds(step, 1)]
    weights = wall_ref[:, CH:MIX].astype(F32).T[0:8]
    row = row + jnp.sum(heads[0:8] * weights, axis=0, keepdims=True)
    small_ref[pl.ds(owner, 1), 0:ROWS] = row
    for r in range(4):

        @pl.when(step == r)
        def _(out=outs[r]):
            out[0:ROWS] = grad.astype(BF16)
            out[ROWS + 16 :, 0:ROWS] = heads[0:16].astype(BF16)
            out[ROWS + 16 :, ROWS:] = jnp.zeros((16, CH - ROWS), BF16)

    @pl.when(step == 3)
    def _():
        for out in outs:
            out[ROWS : ROWS + 16] = small_ref[...].astype(BF16)


def lines_fn(a_ref, b_ref, c_ref, d_ref, lines_ref, small_ref):
    total = jnp.zeros((96, 2 * STATE), F32)
    for line, ref in enumerate((a_ref, b_ref, c_ref, d_ref)):
        lines_ref[line] = ref[0:96, 0:HP]
        total = total + ref[0:96, HP:].astype(F32)
        small_ref[line] = ref[96:]
    lines_ref[4, :, 0 : 2 * STATE] = total.astype(BF16)
    lines_ref[4, :, 2 * STATE :] = jnp.zeros((96, 128), BF16)


def final_grad_fn(at_ref, m_ref, g_ref, out_ref):
    out_ref[...] = mm(m_ref[...], g_ref[...], TN).astype(BF16)


def split_fn(parts, at_ref, a_ref, b_ref, c_ref, d_ref, *refs):
    outs, sum_ref = refs[:4], refs[4]
    total = a_ref[...].astype(F32) + b_ref[...].astype(F32)
    sum_ref[...] = (total + c_ref[...].astype(F32) + d_ref[...].astype(F32)).astype(BF16)
    for k, out in enumerate(outs):
        quarter = lax.rem(at_ref[0] + k, 4)
        to = 0
        for first, rows in parts:
            if rows:
                start = pl.multiple_of(first + rows * quarter, 16)
                out[to : to + rows] = sum_ref[pl.ds(start, rows)]
                to += rows
            else:
                out[to:] = sum_ref[first:]


def back_proj_fn(dx_ref, dz_ref, wall_ref, out_ref):
    dx, dz = dx_ref[...].reshape(2 * PAY, MIX), dz_ref[...].reshape(2 * PAY, HP)
    for r in range(4):
        at = slice(ROWS * r, ROWS * r + ROWS)
        part = mm(dx, wall_ref[at, 0:MIX], NT) + mm(dz, wall_ref[at, MIX:], NT)
        out_ref[:, :, at] = part.astype(BF16).reshape(2, PAY, ROWS)


def place_early_fn(at_ref, mine_ref, sib_ref, out_ref, final_ref):
    def fill(refs):
        for c in range(2):
            for line in range(4):
                block = refs[c][line, 0].astype(F32)
                for a in range(2):
                    first = (2 * c + a) * 768 + 192 * line
                    out_ref[:, first : first + 192] = block[0:96, 192 * a : 192 * a + 192]
                    first = 768 * c + 384 * a
                    final_ref[line, :, first : first + 384] = block[96 + 48 * a : 144 + 48 * a]

    for mine, refs in ((0, (mine_ref, sib_ref)), (1, (sib_ref, mine_ref))):

        @pl.when(at_ref[1] == mine)
        def _(refs=refs):
            fill(refs)


def place_late_fn(at_ref, *refs):
    arrays, (out_ref, buf, sem) = refs[:8], refs[8:]
    y, core = at_ref[0], at_ref[1]
    step = pl.program_id(0)

    def fetch(number, slot):
        for k in range(4):

            @pl.when(number == k)
            def _(k=k):
                for i in range(2):
                    to = buf.at[slot, lax.rem(core + i, 2)]
                    pltpu.make_async_copy(arrays[4 * i + k], to, sem.at[slot, i]).start()

    slot = lax.rem(step, 2)

    @pl.when(step == 0)
    def _():
        fetch(step, slot)

    @pl.when(step < 3)
    def _():
        fetch(step + 1, 1 - slot)

    for i in range(2):
        pltpu.make_async_copy(arrays[0], buf.at[slot, i], sem.at[slot, i]).wait()
    for c in range(2):
        for line in range(4):
            block = buf[slot, c, lax.rem(y - line + 4, 4)].astype(F32)
            for a in range(2):
                first = (2 * c + a) * 768 + 192 * line
                out_ref[:, first : first + 192] = block[:, 192 * a : 192 * a + 192]
    total = buf[slot, 0, 4].astype(F32) + buf[slot, 1, 4].astype(F32)
    out_ref[:, INNER:] = total[:, 0 : 2 * STATE]


def place_small_fn(
    at_ref, own_ref, sib_ref, gain_ref,
    taps_ref, bias_ref, gating_ref, skip_ref, heads_ref, norm_ref, step_ref, buf_ref,
):
    y, core = at_ref[0], at_ref[1]
    buf_ref[...] = jnp.zeros_like(buf_ref)
    taps = jnp.zeros((8, 2 * STATE), F32)
    norm = jnp.zeros((4, ROWS), F32)
    for mine, sets in ((0, (own_ref, sib_ref)), (1, (sib_ref, own_ref))):

        @pl.when(core == mine)
        def _(sets=sets):
            for c in range(2):
                for line in range(4):
                    rows = sets[c][lax.rem(y - line + 4, 4)].astype(F32)
                    for a in range(2):
                        at = (2 * c + a) * 768 + 192 * line
                        at = slice(at, at + 192)
                        part = rows[:, 192 * a : 192 * a + 192]
                        taps_ref[:, at] = part[4:8]
                        bias_ref[:, at] = part[8:9]
                        gating_ref[:, at] = part[9:10]
                        skip_ref[:, at] = part[10:11]
                        at = 12 * (2 * c + a) + 3 * line
                        heads_ref[0:2, at : at + 3] = rows[11:13, 3 * a : 3 * a + 3]
                        buf_ref[at : at + 3] = rows[16 + 3 * a : 19 + 3 * a, 0:ROWS]

    for ref in (own_ref, sib_ref):
        for slot in range(4):
            rows = ref[slot].astype(F32)
            taps = taps + rows[4:12, HP:CH]
            norm = norm + rows[0:4, 0:ROWS]
    taps_ref[:, INNER:] = taps[0:4]
    bias_ref[:, INNER:] = taps[4:5]
    norm_ref[...] = norm / gain_ref[...]
    step_ref[...] = buf_ref[...].T[:, 0:HEADS]


def per_device(
    tokens,
    segments,
    cotangent,
    gate_proj,
    mixer_proj,
    step_proj,
    final_proj,
    norm_gain,
    conv_kernel,
    conv_bias,
    step_offset,
    log_rates,
    skip_gain,
    gating_gain,
):
    ctx = lax.axis_index("ctx")
    x = lax.axis_index("fsdp")
    y = lax.axis_index("y")
    core = lax.axis_index("core")
    turn = (x - 2 * core + 4) % 4

    def scalars(*values):
        return jnp.stack([jnp.asarray(v, jnp.int32) for v in values])

    z = ctx * 2 + lax.axis_index("low")
    flag, where = scalars(ctx), scalars(y, core)

    tokens = tokens.reshape(LOCAL, D)
    cot = cotangent.reshape(LOCAL, D)
    slab, final_rows = call(
        pack_kernel_fn,
        "pack",
        [
            (where, SMEM), (gate_proj, HBM), (mixer_proj, HBM), (final_proj, HBM),
            (step_proj, None),
        ],
        [((ROWS, WIDE), BF16, None), ((192, D), BF16, None)],
        steps=1,
        scratch=[
            pltpu.VMEM((5, ROWS, 256), BF16),
            pltpu.VMEM((ROWS, WIDE), F32),
            pltpu.SemaphoreType.DMA((6,)),
        ],
    )

    def first_hop(own, shift):
        return [own, shift(own, 1), shift(own, -1)]

    def far_hop(hop, shift, cut):
        own, below, above = hop
        ends = below[:cut], above[cut:]
        return ends, [own, below, shift(ends[0], 1), shift(ends[1], -1), above]

    slabs = first_hop(slab, x_shift)
    ahead = lax.ppermute(after(tokens, slab)[LOCAL - 16 :], "ctx", [(0, 1)])
    (payload,) = call(
        prep_kernel_fn,
        "prep",
        [
            (scalars(x, ctx), SMEM), (tokens, None), (ahead, None), (norm_gain[None], None),
            (segments, None),
        ],
        [((PAY, D), BF16, None)],
        steps=1,
        scratch=[pltpu.VMEM((PAY, D), BF16)],
    )
    mine = first_hop(payload, y_shift)
    par, hp, gain = call(
        params_kernel_fn,
        "params",
        [
            (where, SMEM), (conv_kernel, None), (conv_bias[None], None),
            (step_offset[None], None), (log_rates[None], None), (skip_gain[None], None),
            (gating_gain[None], None),
        ],
        [((8, CH), F32, None), ((8, 128), F32, None), ((8, HP), F32, None)],
        steps=1,
        wait=[payload],
    )
    _, slabs = far_hop(slabs, x_shift, 192)
    mine = list(after(tuple(mine), slabs[1], slabs[4]))
    _, mine = far_hop(mine, y_shift, CUT)
    theirs = [core_swap(part) for part in mine]
    cot_all = lax.all_gather(after(cot, mine[2], mine[3]), ("y", "core"), axis=0)

    def owner(r, c):
        return (2 * c + r) % 4

    def from_owners(steps):
        def to(ctx, x, y, low, core):
            r = (x - 2 * core) % 4
            return (ctx, owner(steps[r], core), y, low, core) if r in steps else None

        return to

    def token_outputs(first):
        def spot(*rest):
            return seq(*rest, first=first)

        outs = [
            ((GROUP, PAY, D), BF16),
            ((GROUP, PAY, CH), BF16),
            ((GROUP, LOCAL, CH), F32),
            ((GROUP, LOCAL, CH), BF16),
            ((GROUP, LOCAL, 128), F32),
            ((GROUP, LOCAL, 128), F32),
            ((GROUP, LOCAL, 128), F32),
            ((GROUP, LOCAL, HP), F32),
            ((GROUP, 8, LOCAL), F32),
            ((GROUP, LOCAL, HP), F32),
        ]
        outs = [(shape, dtype, spot(*shape[1:])) for shape, dtype in outs]
        return outs + [((4, HP, STATE), BF16, seq(HP, STATE))]

    block = [pltpu.VMEM((2, PAY, D), BF16), pltpu.SemaphoreType.DMA((2,))]
    own, below, far_a, far_b, above = slabs
    wall, *kept, state_a = call(
        forward_own_fn,
        "forward_own",
        [(flag, SMEM), (par, None), (hp, None)]
        + [(part, HBM) for part in mine]
        + [(part, HBM) for part in (own, above, far_a, far_b, below)],
        [((D, WIDE), BF16, None)] + token_outputs(0),
        steps=4,
        scratch=block + [pltpu.SemaphoreType.DMA((5,))],
    )
    state_in_a = lax.ppermute(state_a, "ctx", [(0, 1)])
    final_rows = after(final_rows, state_a)
    near = move(final_rows, from_owners({0: 1, 1: 0}))
    far = move(final_rows, from_owners({0: 3, 1: 2}))
    away = move(final_rows, from_owners({0: 2, 1: 3}))
    *kept, state_b = call(
        forward_sib_fn,
        "forward_sib",
        [(flag, SMEM), (par, None), (hp, None)]
        + [(part, HBM) for part in theirs]
        + [(wall, None)]
        + [(part, HBM) for part in kept],
        token_outputs(4),
        steps=4,
        scratch=block,
        aliases={9 + i: i for i in range(10)},
        wait=[final_rows],
    )
    nall, xbc, u, xc, dt, cum, raw, gate, segs, y_local = kept
    state_in_b = lax.ppermute(state_b, "ctx", [(0, 1)])
    states = [
        (state_in_a, seq(HP, STATE, low=0, high=4)),
        (state_in_b, seq(HP, STATE, low=4, high=8)),
    ]
    rows = (GROUP, LOCAL, HP)
    wide = seq(LOCAL, HP)
    token = seq(LOCAL, 128)
    line = seq(8, LOCAL)
    conv = seq(LOCAL, CH)
    dmix, w_final = call(
        dmix_kernel_fn,
        "d_mixed",
        [(cot_all, by_device(LOCAL, D))]
        + [(part, HBM) for part in [final_rows, near, far, away]],
        [(rows, F32, wide), ((HP, D), BF16, None)],
        scratch=[pltpu.SemaphoreType.DMA((2,))],
        ahead=[scalars(y, core, turn)],
    )
    y_all, gated, sums = call(
        gate_kernel_fn,
        "gate",
        [(flag, SMEM), (y_local, wide)]
        + states
        + [(gate, wide), (dmix, wide), (xc, conv), (cum, token), (segs, line), (gain, None)],
        [(rows, F32, wide), (rows, BF16, wide), ((GROUP, 8, LOCAL), F32, line)],
    )

    (out,) = call(
        product_kernel_fn,
        "out_proj",
        [(gated, wide), (w_final, None)],
        [((GROUP, LOCAL, D), BF16, by_device(LOCAL, D))],
        ahead=[where],
    )
    swapped = core_swap(sums)
    sums = sums + jnp.concatenate([swapped[4:], swapped[:4]], axis=0)
    shifted = [y_shift(sums, steps) for steps in (1, 2, 3)]
    shifted = after(tuple(shifted), out)
    total = sums
    for steps, got in zip((1, 2, 3), shifted, strict=True):
        got = got.reshape(2, 4, 8, LOCAL)
        got = jnp.concatenate([got[:, 4 - steps :], got[:, : 4 - steps]], axis=1)
        total = total + got.reshape(GROUP, 8, LOCAL)
    out = lax.psum_scatter(out, ("y", "core"), scatter_dimension=0, tiled=True)

    mixed, dy, dz, dstate, dgain = call(
        ungate_kernel_fn,
        "ungate",
        [(flag, SMEM), (y_all, wide), (gate, wide), (dmix, wide), (total, line), (xc, conv)]
        + [(cum, token), (segs, line), (gain, None)],
        [
            (rows, BF16, by_device(LOCAL, HP)),
            (rows, BF16, wide),
            ((GROUP, PAY, HP), BF16, seq(PAY, HP)),
            ((GROUP, HP, STATE), BF16, seq(HP, STATE)),
            ((8, HP), F32, None),
        ],
        ahead=[where],
    )
    dstate_in = lax.ppermute(dstate, "ctx", [(1, 0)])

    def ring_start(mine, theirs, cut):
        far, near = add(mine[2, :cut], theirs[2, :cut]), add(mine[2, cut:], theirs[2, cut:])
        return (far, near), (y_shift(far, 1), y_shift(near, -1))

    def ring_next(mine, theirs, cut, up, down):
        tail = jnp.zeros((mine.shape[1] - cut, D), BF16)
        ahead = add(mine[3], theirs[3], jnp.concatenate([up, tail], axis=0))
        head = jnp.zeros((cut, D), BF16)
        behind = add(mine[1], theirs[1], jnp.concatenate([head, down], axis=0))
        return (ahead, behind), (y_shift(ahead, 1), y_shift(behind, -1))

    def ring_end(mine, theirs, got):
        return sum(v.astype(F32) for v in (mine[0], theirs[0]) + tuple(got))

    mixed_rows = mixed.reshape(GROUP * LOCAL, HP)

    def final_half(half):
        return call(
            final_grad_fn,
            "grad_final",
            [
                (mixed_rows, None),
                (
                    cot_all.reshape(GROUP * LOCAL, D),
                    ((GROUP * LOCAL, ROWS), lambda i, s: (0, 2 * s[0] + i)),
                ),
            ],
            [((HP, 768), BF16, ((HP, ROWS), lambda i, s: (0, i)))],
            steps=2,
            ahead=[scalars(half)],
        )[0]

    final_got = core_swap(final_half(1 - core))
    final_kept = final_half(core)

    normed_rows = nall.reshape(GROUP * PAY, D)

    def grad_inputs(grads):
        return [
            (scalars(x, core), SMEM),
            (normed_rows, ((GROUP * PAY, ROWS), lambda i, *s: (0, i))),
            (grads, None),
            (wall, ((ROWS, WIDE), lambda i, *s: (i, 0))),
        ]

    def over_x(blocks):
        own, ahead, far, behind = blocks
        return own, x_shift(far, 2), x_shift(ahead, 1), x_shift(behind, -1)

    def over_z(blocks, parts, rows):
        shape = blocks[0].shape
        quarters = call(
            functools.partial(split_fn, parts),
            "split",
            [(scalars(z), SMEM)] + [(block, None) for block in blocks],
            [((rows, shape[1]), BF16, None)] * 4,
            steps=1,
            scratch=[pltpu.VMEM(shape, BF16)],
        )
        return quarters, [quarters[0]] + [z_shift(quarters[k], k) for k in (2, 1, 3)]

    def over_y(piece):
        return [piece] + [y_shift(piece, s) for s in (1, 2, 3)]

    def gathered(lines):
        own, small = call(
            lines_fn,
            "lines",
            [(line, None) for line in lines],
            [((5, 96, HP), BF16, None), ((4, 32, CH), BF16, None)],
            steps=1,
        )
        mine = [own] + [z_shift(own, k) for k in (2, 1, 3)]
        mine = [mine[0], mine[2], mine[1], mine[3]]
        small = small, core_swap(small)
        return small, mine + [core_swap(part) for part in mine]

    early, norm_gate = call(
        early_grad_fn,
        "grad_gate",
        grad_inputs(dz.reshape(GROUP * PAY, HP))[1:] + [(final_kept, None), (final_got, None)],
        [
            (
                (4, 4, 192, HP),
                BF16,
                ((1, 4, 192, HP), lambda i, at: ((at[0] + i) % 4, 0, 0, 0)),
            ),
            ((8, HP), F32, None),
        ],
        steps=4,
        ahead=[scalars(x, core)],
    )
    early = after(early, out)
    early_block = early
    early = lax.psum_scatter(early, "fsdp", scatter_dimension=0, tiled=True)
    early = lax.psum(early[0], ("ctx", "low"))
    early = lax.all_gather(early, "y", axis=0)

    def back(first, sums, wait):
        def spot(*rest):
            return seq(*rest, first=first)

        state = states[0][0] if first < 4 else states[1][0]
        return call(
            back_kernel_fn,
            "back",
            [
                (flag, SMEM), (dy, spot(LOCAL, HP)), (xc, spot(LOCAL, CH)), (u, spot(LOCAL, CH)),
                (xbc, spot(PAY, CH)), (dt, spot(LOCAL, 128)), (cum, spot(LOCAL, 128)),
                (raw, spot(LOCAL, 128)), (segs, spot(8, LOCAL)), (par, None), (hp, None),
                (state, seq(HP, STATE, first=first % 4, high=4)), (dstate_in, spot(HP, STATE)),
            ]
            + [(value, None) for value in sums[1:]]
            + [(sums[0], HBM)],
            [
                ((GROUP, PAY, MIX), BF16, spot(PAY, MIX)),
                ((8, HP), F32, None),
                ((8, CH), F32, None),
                ((8, 128), F32, None),
            ],
            steps=2,
            scratch=[
                pltpu.VMEM((128, LOCAL), F32),
                pltpu.VMEM((LOCAL, CH), F32),
                pltpu.VMEM((LOCAL, 128), F32),
                pltpu.VMEM((LOCAL, 128), F32),
            ],
            aliases={16: 0},
            wait=wait,
        )

    sums = [
        jnp.zeros((GROUP, PAY, MIX), BF16),
        jnp.zeros((8, HP), F32),
        jnp.zeros((8, CH), F32),
        jnp.zeros((8, 128), F32),
    ]
    sums = back(0, sums, [early_block])
    for first in (2, 4, 6):
        sums = back(first, sums, [])
    dx, dskip, dpar, dhead = sums

    late = call(
        late_grad_fn,
        "grad_mixer",
        grad_inputs(dx.reshape(GROUP * PAY, MIX))
        + [(value, None) for value in (norm_gate, dpar, dgain, dskip, dhead)],
        [((ROWS + 32, CH), BF16, None)] * 4,
        steps=4,
        scratch=[pltpu.VMEM((16, CH), F32)],
    )
    blocks = late
    late = over_x(late)

    def back_projected(first, wait):
        return call(
            back_proj_fn,
            "back_proj",
            [
                (dx, ((2, PAY, MIX), lambda i: (i + first // 2, 0, 0))),
                (dz, ((2, PAY, HP), lambda i: (i + first // 2, 0, 0))),
                (wall, None),
            ],
            [((4, PAY, D), BF16, ((2, PAY, D), lambda i: (i, 0, 0)))],
            steps=2,
            wait=wait,
        )[0]

    back_theirs = back_projected(4, [blocks[1]])
    back_swapped = core_swap(back_theirs)
    back_mine = back_projected(0, [back_theirs])
    ends, (back_up, back_down) = ring_start(back_mine, back_swapped, CUT)
    quarters, late = over_z(after(late, ends[0], ends[1]), ((0, 96), (ROWS, 0)), 128)
    factor = lax.rsqrt(total[0, 0] / INNER + EPS)[:, None]
    layer_out = tokens.astype(F32) + factor * out[0].astype(F32)
    back_up, back_down = after((back_up, back_down), quarters[1])
    ends, back_got = ring_next(back_mine, back_swapped, CUT, back_up, back_down)
    piece = add(*after(tuple(late), *ends))
    late = over_y(piece)
    small, late = gathered(late)
    quarter = ((4, 1, 192, HP), lambda i: (0, i, 0, 0))
    grad_gate, grad_final = call(
        place_early_fn,
        "place_early",
        [(where, SMEM), (early, quarter)]
        + [(core_swap(early), quarter)],
        [
            ((ROWS, INNER), F32, ((96, INNER), lambda i: (i, 0))),
            ((4, 192, D), F32, ((4, 48, D), lambda i: (0, i, 0))),
        ],
        steps=4,
    )
    d_normed = ring_end(back_mine, back_swapped, after(back_got, late[0]))
    ahead = lax.ppermute(d_normed[LOCAL:].astype(BF16), "ctx", [(1, 0)])

    taps, bias, gating, skip, heads, norm, grad_step = call(
        place_small_fn,
        "place_small",
        [(where, SMEM), (small[0], None), (small[1], None), (norm_gain.reshape(4, ROWS), None)],
        [((4, CONV_CH), F32, None), ((1, CONV_CH), F32, None)]
        + [((1, INNER), F32, None)] * 2
        + [((8, HEADS), F32, None), ((4, ROWS), F32, None), ((ROWS, HEADS), F32, None)],
        steps=1,
        scratch=[pltpu.VMEM((128, ROWS), F32)],
    )
    d_normed = jnp.concatenate(
        [d_normed[: LOCAL - 8], d_normed[LOCAL - 8 : LOCAL] + ahead[8:].astype(F32)], axis=0
    )
    d_normed = lax.dynamic_slice_in_dim(
        jnp.concatenate([d_normed, d_normed], axis=1), D - ROWS * x, D, axis=1
    )
    tokens_f = tokens.astype(F32)
    inv_rms = lax.rsqrt(jnp.mean(tokens_f * tokens_f, axis=1, keepdims=True) + EPS)
    w = tokens_f * inv_rms
    e1 = d_normed * norm_gain
    grad_tokens = cotangent.reshape(LOCAL, D).astype(F32) + inv_rms * (
        e1 - w * jnp.mean(e1 * w, axis=1, keepdims=True)
    )
    (grad_mixer,) = call(
        place_late_fn,
        "place_late",
        [(value, HBM) for value in late],
        [((ROWS, CONV_CH), F32, ((96, CONV_CH), lambda i, at: ((at[2] - i + 4) % 4, 0)))],
        steps=4,
        scratch=[pltpu.VMEM((2, 2, 5, 96, HP), BF16), pltpu.SemaphoreType.DMA((2, 2))],
        ahead=[scalars(y, core, z)],
    )
    shape = (1, LOCAL, D)
    return (
        layer_out.reshape(shape),
        grad_tokens.reshape(shape),
        grad_gate,
        grad_mixer,
        grad_step,
        grad_final.reshape(2 * 384, D),
        norm.reshape(D),
        taps,
        bias[0],
        heads[1],
        heads[0],
        jnp.sum(skip.reshape(HEADS, HEAD_DIM), axis=1),
        gating[0],
    )


def solution(mesh):
    apart = jax.sharding.Mesh(mesh.devices.reshape(2, 4, 4, 2, 2), AXES)
    batch = ("fsdp", "y", "low", "core")
    tokens = P(batch, "ctx", None)
    rows = P("fsdp", None)
    return jax.shard_map(
        per_device,
        mesh=apart,
        in_specs=(tokens, P(batch, None), tokens, rows, rows, rows, rows) + (P(),) * 7,
        out_specs=(tokens, tokens, rows, rows, rows, rows) + (P(),) * 7,
        check_vma=False,
    )
```

```python
import functools

import jax
import jax.numpy as jnp
from jax import lax
from jax.experimental import pallas as pl
from jax.experimental.pallas import tpu as pltpu
from jax.sharding import PartitionSpec as P

D = 1536
INNER = 3072
STATE = 128
HEADS = 48
HEAD_DIM = 64
CONV_CH = 3328
LOCAL = 256
GROUP = 8
OWN = 6
HP = OWN * HEAD_DIM
CH = HP + 2 * STATE
ROWS = D // 4
EPS = 1e-05
AXES = ("ctx", "fsdp", "y", "low", "core")
F32 = jnp.float32
BF16 = jnp.bfloat16
HIGH = lax.Precision.HIGHEST
MASKED = -1e30
PAY = LOCAL + 16
CUT = 144
WIDE = CH + 128 + HP
HALF = 208
MIX = CH + 128
SCALE = 1.0
DURATION = {
    "pack": 4, "prep": 3, "params": 2, "forward_first": 10, "forward_near": 18, "forward_far": 10, "d_mixed": 7, "gate": 7,
    "out_proj": 7, "ungate": 8, "grad_final": 0.1, "grad_gate": 0.1, "back": 17, "grad_mixer": 13,
    "back_proj": 6, "split": 3, "patch": 1, "finish": 3, "lines": 2, "place_early": 7, "place_late": 6, "place_small": 2,
}
VMEM_LIMIT = 63 * 1024 * 1024


def place_of(ctx, x, y, low, core):
    return (ctx * 4 + x) * 16 + (y * 2 + low) * 2 + core


def pairs_of(move):
    pairs = []
    for ctx in range(2):
        for x in range(4):
            for y in range(4):
                for low in range(2):
                    for core in range(2):
                        to = move(ctx, x, y, low, core)
                        if to is not None:
                            pairs.append((place_of(ctx, x, y, low, core), place_of(*to)))
    return pairs


def move(value, to):
    return lax.ppermute(value, AXES, pairs_of(to))


def x_shift(value, steps):
    return lax.ppermute(value, "fsdp", [(i, (i + steps) % 4) for i in range(4)])


def y_shift(value, steps):
    return lax.ppermute(value, "y", [(i, (i + steps) % 4) for i in range(4)])


def core_swap(value):
    return lax.ppermute(value, "core", [(0, 1), (1, 0)])


def z_shift(value, steps):
    def to(ctx, x, y, low, core):
        z = (2 * ctx + low + steps) % 4
        return (z // 2, x, y, z % 2, core)

    return move(value, to)


def after(value, *others):
    return lax.optimization_barrier((value,) + others)[0]


def add(*values):
    total = values[0].astype(F32)
    for value in values[1:]:
        total = total + value.astype(F32)
    return total.astype(BF16)


def mm(a, b, dims, precision=None):
    return lax.dot_general(a, b, (dims, ((), ())), precision=precision, preferred_element_type=F32)


NN = ((1,), (0,))
NT = ((1,), (1,))
TN = ((0,), (0,))
SMEM = object()
HBM = object()


def call(fn, name, inputs, outputs, steps=GROUP, scratch=(), aliases=None, ahead=(), wait=()):
    us = DURATION[name] * SCALE
    first = len(ahead) + len(inputs)
    inputs = inputs + [(value, HBM) for value in wait]

    def kernel(*refs):
        fn(*refs[:first], *refs[first + len(wait) :])

    def block(shape, how):
        if how is SMEM:
            return pl.BlockSpec(memory_space=pltpu.SMEM)
        if how is HBM:
            return pl.BlockSpec(memory_space=pl.ANY)
        if how is None:
            return pl.BlockSpec(tuple(shape), lambda i, *s: (0,) * len(shape))
        return pl.BlockSpec(*how)

    return pl.pallas_call(
        kernel,
        name=name,
        grid_spec=pltpu.PrefetchScalarGridSpec(
            num_scalar_prefetch=len(ahead),
            grid=(steps,),
            in_specs=[block(value.shape, how) for value, how in inputs],
            out_specs=[block(shape, how) for shape, _, how in outputs],
            scratch_shapes=list(scratch),
        ),
        out_shape=[jax.ShapeDtypeStruct(shape, dtype) for shape, dtype, _ in outputs],
        input_output_aliases=aliases or {},
        cost_estimate=pl.CostEstimate(
            flops=int(us * 1.15e9), bytes_accessed=int(us * 3.6e6), transcendentals=0
        ),
        compiler_params=pltpu.CompilerParams(
            dimension_semantics=("arbitrary",), vmem_limit_bytes=VMEM_LIMIT
        ),
    )(*ahead, *[value for value, _ in inputs])


def seq(*rest, first=0, low=0, high=GROUP):
    def at(i, *s):
        return (jnp.clip(i + first, low, high - 1) - low,) + (0,) * len(rest)

    return ((1,) + rest, at)


def by_device(*rest, steps=1, first=0):
    def at(i, at):
        i = i * steps + first
        y, core = (at[0] + 4 - i % 4) % 4, (at[1] + i // 4) % 2
        return (2 * y + core,) + (0,) * len(rest)

    return ((1,) + rest, at)


def lane_ids(rows, cols):
    return lax.broadcasted_iota(jnp.int32, (rows, cols), 1)


def pair(values, p, left):
    return jnp.where(left, values[:, 2 * p : 2 * p + 1], values[:, 2 * p + 1 : 2 * p + 2])


def small_parts(small):
    mine = lane_ids(LOCAL, 128) < OWN
    parts = small, pltpu.roll(small, 120, 1), pltpu.roll(small, 112, 1)
    return [jnp.where(mine, part, 0.0) for part in parts]


def summed_rows(values, dims):
    lane = lane_ids(LOCAL, 128)
    high = values.astype(BF16).astype(F32)
    rest = values - high
    middle = rest.astype(BF16).astype(F32)
    parts = jnp.where(lane < 8, high, jnp.where(lane < 16, middle, rest - middle))
    got = mm(triangle().astype(BF16), parts.astype(BF16), dims)
    return got + pltpu.roll(got, 120, 1) + pltpu.roll(got, 112, 1)


def head_sums(values, p):
    lane, row = lane_ids(128, 128), lax.broadcasted_iota(jnp.int32, (128, 128), 0)
    ones = jnp.where(lane == 2 * p + row // HEAD_DIM, 1.0, 0.0).astype(BF16)
    return mm(values.astype(BF16), ones, NN)


def triangle():
    row = lax.broadcasted_iota(jnp.int32, (LOCAL, LOCAL), 0)
    col = lax.broadcasted_iota(jnp.int32, (LOCAL, LOCAL), 1)
    return row >= col


def seg_columns(row):
    return jnp.broadcast_to(row, (128, LOCAL)).T


def same_before(seg, k):
    return jnp.concatenate([seg[:k], seg[: LOCAL - k]], axis=0) == seg


def mask_bias(seg, row):
    wide = jnp.concatenate([seg, seg], axis=1)
    return jnp.where((wide == row) & triangle(), 0.0, MASKED)


def prep_kernel_fn(at_ref, tok_ref, ahead_ref, gain_ref, seg_ref, out_ref, buf_ref):
    def normed(values):
        values = values.astype(F32)
        inv = lax.rsqrt(jnp.mean(values * values, axis=1, keepdims=True) + EPS)
        return (values * inv * gain_ref[...]).astype(BF16)

    buf_ref[0:LOCAL] = normed(tok_ref[...])
    seg = seg_ref[...].astype(F32)
    seg = jnp.where(at_ref[1] == 0, seg[:, :LOCAL], seg[:, LOCAL:])
    part = jnp.concatenate([seg, jnp.zeros((1, ROWS - LOCAL), F32)], axis=1)
    row = jnp.concatenate([part] * 4, axis=1)
    number = lax.broadcasted_iota(jnp.int32, (16, D), 0)
    extra = jnp.where(number >= 8, normed(ahead_ref[...]).astype(F32), 0.0)
    buf_ref[LOCAL:PAY] = jnp.where(number == 0, row, extra).astype(BF16)
    for r in range(4):
        start = pl.multiple_of(ROWS * lax.rem(at_ref[0] + r, 4), 128)
        out_ref[:, ROWS * r : ROWS * r + ROWS] = buf_ref[:, pl.ds(start, ROWS)]


def pack_kernel_fn(
    at_ref, gate_ref, mixer_ref, final_ref, step_ref, slab_ref, rows_ref, buf_ref, wide_ref, sem
):
    y, core = at_ref[0], at_ref[1]
    copies = []
    for i, src in enumerate((mixer_ref, gate_ref)):
        for a in range(2):
            first = (2 * core + a) * 768 + 384 * lax.div(y, 2) + 128 * lax.rem(y, 2)
            where = pl.ds(pl.multiple_of(first, 128), 256)
            copies.append((src.at[:, where], buf_ref.at[2 * i + a]))
    copies.append((mixer_ref.at[:, pl.ds(INNER, 2 * STATE)], buf_ref.at[4]))
    copies.append((final_ref.at[pl.ds(pl.multiple_of(192 * y, 64), 192)], rows_ref))
    copies = [pltpu.make_async_copy(a, b, sem.at[i]) for i, (a, b) in enumerate(copies)]
    for copy in copies:
        copy.start()
    wide_ref[:, CH:MIX] = jnp.zeros((ROWS, 128), F32)
    step = step_ref[...].astype(F32)
    for line in range(4):
        for c in range(2):

            @pl.when((y == line) & (core == c))
            def _(line=line, c=c):
                for a in range(2):
                    at = 12 * (2 * c + a) + 3 * line
                    for to in range(CH + 3 * a, CH + 24, 8):
                        wide_ref[:, to : to + 3] = step[:, at : at + 3]

    for copy in copies:
        copy.wait()
    for odd in range(2):

        @pl.when(lax.rem(y, 2) == odd)
        def _(odd=odd):
            for i, base in enumerate((0, MIX)):
                for a in range(2):
                    block = buf_ref[2 * i + a].astype(F32)
                    to = base + 192 * a
                    wide_ref[:, to : to + 192] = block[:, 64 * odd : 64 * odd + 192]

    slab_ref[...] = wide_ref[...].astype(BF16)
    slab_ref[:, HP:CH] = buf_ref[4]


def params_kernel_fn(
    at_ref, taps_ref, bias_ref, offset_ref, rates_ref, skip_ref, gating_ref,
    par_ref, hp_ref, gain_ref,
):
    par_ref[...] = jnp.zeros_like(par_ref)
    hp_ref[...] = jnp.zeros_like(hp_ref)
    for line in range(4):
        for c in range(2):

            @pl.when((at_ref[0] == line) & (at_ref[1] == c))
            def _(line=line, c=c):
                for a in range(2):
                    at = slice((2 * c + a) * 768 + 192 * line, (2 * c + a) * 768 + 192 * line + 192)
                    to = slice(192 * a, 192 * a + 192)
                    par_ref[0:4, to] = taps_ref[:, at]
                    par_ref[4:5, to] = bias_ref[:, at]
                    gain_ref[0:1, to] = gating_ref[:, at]
                    at = slice(12 * (2 * c + a) + 3 * line, 12 * (2 * c + a) + 3 * line + 3)
                    for first in range(3 * a, 24, 8):
                        to = slice(first, first + 3)
                        hp_ref[0:1, to] = offset_ref[:, at]
                        hp_ref[1:2, to] = -jnp.exp(rates_ref[:, at])
                        hp_ref[2:3, to] = skip_ref[:, at]

    par_ref[0:4, HP:] = taps_ref[:, INNER:]
    par_ref[4:5, HP:] = bias_ref[:, INNER:]


class Pieces:
    def __init__(self, parts, buf, sem):
        self.parts, self.buf, self.sem = parts, buf, sem

    def fetch(self, step, slot):
        for k, refs in enumerate(self.parts):

            @pl.when(step == k)
            def _(refs=refs):
                first = 0
                for ref in refs:
                    to = self.buf.at[slot, first : first + ref.shape[0]]
                    pltpu.make_async_copy(ref, to, self.sem.at[slot]).start()
                    first += ref.shape[0]

    def next(self):
        step = pl.program_id(0)
        slot = lax.rem(step, 2)

        @pl.when(step == 0)
        def _():
            self.fetch(step, slot)

        @pl.when(step < len(self.parts) - 1)
        def _():
            self.fetch(step + 1, 1 - slot)

        pltpu.make_async_copy(self.buf.at[slot], self.buf.at[slot], self.sem.at[slot]).wait()
        return slot


def forward_body(
    ctx_ref, par_ref, hp_ref, n, wall_ref,
    nall_ref, xbc_ref, u_ref, out_ref, small_ref, z_ref, seg_ref, y_ref, state_ref, xc_ref,
):
    par = par_ref[...]
    hp = hp_ref[...]
    nall_ref[0] = n
    row = n[LOCAL:PAY, 0:LOCAL].astype(F32)[0:1]
    seg_ref[0] = jnp.broadcast_to(row, (8, LOCAL))
    seg = seg_columns(row)
    keeps = [same_before(seg, k) for k in range(1, 4)]
    z_ref[0] = mm(n[0:LOCAL], wall_ref[:, MIX:], NN).astype(BF16)
    for j in range(3):
        prod = mm(n, wall_ref[:, 256 * j : 256 * j + 256], NN)
        for half in range(2):
            first = 256 * j + 128 * half
            at = slice(first, first + 128)
            x = prod[:, 128 * half : 128 * half + 128]
            if first == CH:
                raw = x[0:LOCAL] + hp[0:1]
                continue
            low = x.astype(BF16)
            xbc_ref[0, :, at] = low
            x = low.astype(F32)
            ext = jnp.concatenate([x[LOCAL + 8 :], x[:LOCAL]], axis=0)
            u = par[4:5, at] + par[0:1, at] * x[:LOCAL]
            for k in range(1, 4):
                moved = ext[8 - k : 8 - k + LOCAL]
                u = u + par[k : k + 1, at] * jnp.where(keeps[k - 1], moved, 0.0)
            u_ref[0, :, at] = u.astype(BF16)
            xc_ref[:, at] = (u * jax.nn.sigmoid(u)).astype(BF16)
    dt = jnp.maximum(raw, 0.0) + jnp.log1p(jnp.exp(-jnp.abs(raw)))
    cum = summed_rows(dt * hp[1:2], NN)
    lane = lane_ids(LOCAL, 128)
    small_ref[0] = jnp.where(lane < 8, dt, jnp.where(lane < 16, pltpu.roll(cum, 8, 1), raw))
    left = lane < HEAD_DIM
    left1 = lane_ids(1, 128) < HEAD_DIM
    basis, out_basis = xc_ref[:, HP : HP + STATE], xc_ref[:, HP + STATE :]
    out_ref[0] = out_basis

    @pl.when(ctx_ref[0] == 0)
    def _():
        tail = jnp.where(seg == seg[LOCAL - 1 :], jnp.exp(cum[LOCAL - 1 :] - cum) * dt, 0.0)
        for p in range(3):
            at = slice(128 * p, 128 * p + 128)
            part = xc_ref[:, at].astype(F32) * pair(tail, p, left)
            state_ref[0, at] = mm(part.astype(BF16), basis, TN).astype(BF16)

    @pl.when(ctx_ref[0] != 0)
    def _():
        state_ref[0] = jnp.zeros((HP, STATE), BF16)

    cum_t = cum.T
    scores = mm(out_basis, basis, NT)
    bias = mask_bias(seg, row)
    for p in range(3):
        at = slice(128 * p, 128 * p + 128)
        x = xc_ref[:, at].astype(F32)
        scaled = (x * pair(dt, p, left)).astype(BF16)
        halves = []
        for h in (2 * p, 2 * p + 1):
            mix = jnp.exp(cum[:, h : h + 1] - cum_t[h : h + 1] + bias) * scores
            halves.append(mm(mix.astype(BF16), scaled, NN))
        y = jnp.where(left, halves[0], halves[1]) + pair(hp[2:3], p, left1) * x
        y_ref[0, :, at] = y.astype(BF16)


def forward_first_fn(ctx_ref, par_ref, hp_ref, mine, theirs, *refs):
    slabs, wall_ref, outs, (xc, buf, sem, wsem) = refs[:5], refs[5], refs[6:15], refs[15:]
    copies = []
    first = 0
    for i, ref in enumerate(slabs):
        rows = ref.shape[0]
        copies.append(pltpu.make_async_copy(ref, wall_ref.at[first : first + rows], wsem.at[i]))
        first += rows

    @pl.when(pl.program_id(0) == 0)
    def _():
        for copy in copies:
            copy.start()

    slot = Pieces([[mine], [theirs]], buf, sem).next()

    @pl.when(pl.program_id(0) == 0)
    def _():
        for copy in copies:
            copy.wait()

    forward_body(ctx_ref, par_ref, hp_ref, buf[slot], wall_ref, *outs, xc)


def forward_near_fn(ctx_ref, par_ref, hp_ref, wall_ref, *refs):
    parts, outs, (xc, buf, sem) = refs[:4], refs[13:22], refs[22:]
    slot = Pieces([[part] for part in parts], buf, sem).next()
    forward_body(ctx_ref, par_ref, hp_ref, buf[slot], wall_ref, *outs, xc)


def forward_far_fn(ctx_ref, par_ref, hp_ref, wall_ref, *refs):
    parts, outs, (xc, buf, sem) = refs[:4], refs[12:21], refs[21:]
    slot = Pieces([parts[:2], parts[2:]], buf, sem).next()
    forward_body(ctx_ref, par_ref, hp_ref, buf[slot], wall_ref, *outs, xc)


def dmix_kernel_fn(at_ref, *refs):
    g_refs, (own, near, far, away, dmix_ref, wf_ref, sem) = refs[:4], refs[4:]
    step = pl.program_id(0)
    up, down = wf_ref.at[0:192], wf_ref.at[192:HP]

    @pl.when(step == 0)
    def _():
        for r, (a, b) in enumerate(((own, near), (near, own), (away, far), (far, away))):

            @pl.when(at_ref[2] == r)
            def _(a=a, b=b):
                pltpu.make_async_copy(a, up, sem.at[0]).start()
                pltpu.make_async_copy(b, down, sem.at[1]).start()

        pltpu.make_async_copy(own, up, sem.at[0]).wait()
        pltpu.make_async_copy(own, down, sem.at[1]).wait()

    for k, ref in enumerate(g_refs):
        dmix_ref[k] = mm(ref[0], wf_ref[...], NT).astype(BF16)


def gate_kernel_fn(
    ctx_ref, y_ref, state_a_ref, state_b_ref, z_ref, dmix_ref, basis_ref, small_ref, seg_ref,
    gain_ref, yall_ref, low_ref, sums_ref, sum_ref,
):
    sum_ref[...] = y_ref[0].astype(F32)

    @pl.when(ctx_ref[0] != 0)
    def _():
        out_basis = basis_ref[0]
        seg = seg_columns(seg_ref[0, 0:1])
        enter = jnp.where(seg == seg[0:1], jnp.exp(small_parts(small_ref[0])[1]), 0.0)
        left = lane_ids(LOCAL, 128) < HEAD_DIM
        for p in range(3):
            at = slice(128 * p, 128 * p + 128)
            far = lax.rem(pl.program_id(0), 4) == 2
            state = jnp.where(far, state_b_ref[0, at], state_a_ref[0, at])
            sum_ref[:, at] += pair(enter, p, left) * mm(out_basis, state, NT)

    y = sum_ref[...]
    yall_ref[0] = y.astype(BF16)
    z = z_ref[0].astype(F32)
    gated = y * (z * jax.nn.sigmoid(z))
    raised = gated * gain_ref[0:1]
    low_ref[0] = raised.astype(BF16)
    first = jnp.sum(gated * gated, axis=1, keepdims=True)
    second = jnp.sum(dmix_ref[0].astype(F32) * raised, axis=1, keepdims=True)
    lane = lane_ids(LOCAL, 128)
    both = jnp.where(lane == 0, first, jnp.where(lane == 1, second, 0.0))
    sums_ref[0] = both.T[0:8]


def product_kernel_fn(at_ref, a_ref, w_ref, out_ref, buf, sem):
    step = pl.program_id(0)

    def copies(number):
        found = []
        for k in range(4):
            place = 2 * lax.rem(at_ref[0] + 4 - k, 4) + lax.rem(at_ref[1] + number, 2)
            found.append(pltpu.make_async_copy(buf.at[number, k], out_ref.at[place], sem.at[number, k]))
        return found

    for number in range(2):

        @pl.when(step == number)
        def _(number=number):
            for k, copy in enumerate(copies(number)):
                buf[number, k] = mm(a_ref[k], w_ref[...], NN).astype(BF16)
                copy.start()

    @pl.when(step == 1)
    def _():
        for number in range(2):
            for copy in copies(number):
                copy.wait()


def ungate_kernel_fn(
    at_ref, ctx_ref, y_ref, z_ref, dmix_ref, sums_ref, basis_ref, small_ref, seg_ref, gain_ref,
    mixed_ref, dy_ref, dz_ref, dstate_ref, dgain_ref,
):
    step = pl.program_id(0)
    pad = jnp.concatenate([sums_ref[0], jnp.zeros((120, LOCAL), F32)], axis=0).T
    inv = lax.rsqrt(pad[:, 0:1] / INNER + EPS)
    mean_ev = inv * pad[:, 1:2] / INNER
    y = y_ref[0].astype(F32)
    z = z_ref[0].astype(F32)
    dmix = dmix_ref[0].astype(F32)
    gain = gain_ref[0:1]
    sig = jax.nn.sigmoid(z)
    act = z * sig
    v = y * act * inv
    mixed_ref[0] = (v * gain).astype(BF16)
    d_gated = inv * (dmix * gain - v * mean_ev)
    dy = (d_gated * act).astype(BF16)
    dy_ref[0] = dy
    dz_ref[0, 0:LOCAL] = (d_gated * y * sig * (1.0 + z * (1.0 - sig))).astype(BF16)
    dz_ref[0, LOCAL:PAY] = jnp.zeros((16, HP), BF16)
    part = jnp.sum(dmix * v, axis=0, keepdims=True)

    @pl.when(step == 0)
    def _():
        dgain_ref[...] = jnp.zeros_like(dgain_ref)

    dgain_ref[0:1] += part

    @pl.when(ctx_ref[0] != 0)
    def _():
        out_basis = basis_ref[0]
        seg = seg_columns(seg_ref[0, 0:1])
        enter = jnp.where(seg == seg[0:1], jnp.exp(small_parts(small_ref[0])[1]), 0.0)
        left = lane_ids(LOCAL, 128) < HEAD_DIM
        for p in range(3):
            at = slice(128 * p, 128 * p + 128)
            part = (dy[:, at].astype(F32) * pair(enter, p, left)).astype(BF16)
            dstate_ref[0, at] = mm(part, out_basis, TN).astype(BF16)

    @pl.when(ctx_ref[0] == 0)
    def _():
        dstate_ref[0] = jnp.zeros((HP, STATE), BF16)


def back_kernel_fn(
    ctx_ref, dy_ref, u_ref, xbc_ref, small_ref, seg_ref, par_ref, hp_ref, state_a_ref, state_b_ref,
    dstate_ref, skip0_ref, par0_ref, head0_ref,
    dx_ref, dskip_ref, dpar_ref, dhead_ref, turn_ref, dxc_ref, dc_ref, dd_ref, xc_ref, slope_ref,
):
    step = pl.program_id(0)
    hp = hp_ref[...]
    par = par_ref[...]
    dt, cum, raw = small_parts(small_ref[0])
    cum_t = cum.T
    for j in range(5):
        at = slice(128 * j, 128 * j + 128)
        u = u_ref[0, :, at].astype(F32)
        sig = jax.nn.sigmoid(u)
        xc_ref[:, at] = (u * sig).astype(BF16)
        slope_ref[:, at] = sig * (1.0 + u * (1.0 - sig))
    basis, out_basis = xc_ref[:, HP : HP + STATE], xc_ref[:, HP + STATE :]
    scores = mm(basis, out_basis, NT)
    row = seg_ref[0, 0:1]
    seg = seg_columns(row)
    same = jnp.concatenate([seg, seg], axis=1) == row
    first = lax.broadcasted_iota(jnp.int32, (LOCAL, LOCAL), 0)
    bias = jnp.where(same & (first <= lane_ids(LOCAL, LOCAL)), 0.0, MASKED)
    lane = lane_ids(LOCAL, 128)
    left = lane < HEAD_DIM
    left1 = lane_ids(1, 128) < HEAD_DIM

    @pl.when(step == 0)
    def _():
        dskip_ref[...] = skip0_ref[...]
        dpar_ref[...] = par0_ref[...]
        dhead_ref[...] = head0_ref[...]
        turn_ref[...] = jnp.zeros_like(turn_ref)

    d_scores = jnp.zeros((LOCAL, LOCAL), F32)
    sums = jnp.zeros((LOCAL, 128), F32)
    for p in range(3):
        at = slice(128 * p, 128 * p + 128)
        x = xc_ref[:, at].astype(F32)
        g = dy_ref[0, :, at]
        steps = pair(dt, p, left)
        scaled = (x * steps).astype(BF16)
        halves = []
        for h in (2 * p, 2 * p + 1):
            mine = left if h % 2 == 0 else ~left
            prod = mm(scaled, jnp.where(mine, g, jnp.zeros_like(g)), NT)
            mix = jnp.exp(cum_t[h : h + 1] - cum[:, h : h + 1] + bias)
            weighed = mix * prod
            d_scores = d_scores + weighed
            pulled = weighed * scores
            turn_ref[h : h + 1] = jnp.sum(pulled, axis=0, keepdims=True)
            sums = jnp.where(lane == h, jnp.sum(pulled, axis=1, keepdims=True), sums)
            halves.append(mm((mix * scores).astype(BF16), g, NN))
        gf = g.astype(F32)
        skip = pair(hp[2:3], p, left1)
        dxc_ref[:, at] = steps * jnp.where(left, halves[0], halves[1]) + skip * gf
        dskip_ref[0:1, at] += jnp.sum(gf * x, axis=0, keepdims=True)
    dd_ref[...] = jnp.where(dt > 1e-37, sums / jnp.maximum(dt, 1e-37), 0.0)
    dc_ref[...] = turn_ref[...].T - sums
    low = d_scores.astype(BF16)
    dxc_ref[:, HP : HP + STATE] = mm(low, out_basis, NN)
    dxc_ref[:, HP + STATE :] = mm(low, basis, TN)

    @pl.when(ctx_ref[0] != 0)
    def _():
        enter = jnp.where(seg == seg[0:1], jnp.exp(cum), 0.0)
        d_out = jnp.zeros((LOCAL, STATE), F32)
        extra = jnp.zeros((LOCAL, 128), F32)
        for p in range(3):
            at = slice(128 * p, 128 * p + 128)
            state = jnp.where(lax.rem(step, 4) == 2, state_b_ref[0, at], state_a_ref[0, at])
            scaled = dy_ref[0, :, at].astype(F32) * pair(enter, p, left)
            d_out = d_out + mm(scaled.astype(BF16), state, NN)
            extra = extra + head_sums(scaled * mm(out_basis, state, NT), p)
        dxc_ref[:, HP + STATE :] += d_out
        dc_ref[...] += extra

    @pl.when(ctx_ref[0] == 0)
    def _():
        tail = jnp.where(seg == seg[LOCAL - 1 :], jnp.exp(cum[LOCAL - 1 :] - cum), 0.0)
        weight = tail * dt
        d_basis = jnp.zeros((LOCAL, STATE), F32)
        d_weight = jnp.zeros((LOCAL, 128), F32)
        for p in range(3):
            at = slice(128 * p, 128 * p + 128)
            x = xc_ref[:, at].astype(F32)
            w = pair(weight, p, left)
            ds = dstate_ref[0, at]
            seen = mm(basis, ds, NT)
            dxc_ref[:, at] += w * seen
            d_basis = d_basis + mm((x * w).astype(BF16), ds, NN)
            d_weight = d_weight + head_sums(x * seen, p)
        dxc_ref[:, HP : HP + STATE] += d_basis
        dd_ref[...] += tail * d_weight
        moved = weight * d_weight
        dc_ref[...] -= moved
        dc_ref[LOCAL - 1 : LOCAL] += jnp.sum(moved, axis=0, keepdims=True)

    dc = jnp.where(lane < OWN, dc_ref[...], 0.0)
    dc = dc + pltpu.roll(dc, 8, 1) + pltpu.roll(dc, 16, 1)
    d_decay = summed_rows(dc, TN)
    rate = hp[1:2]
    d_raw = (dd_ref[...] + d_decay * rate) * jax.nn.sigmoid(raw)
    d_raw = jnp.where(lane < OWN, d_raw, 0.0)
    dhead_ref[0:1] += jnp.sum(d_decay * dt, axis=0, keepdims=True) * rate
    dhead_ref[1:2] += jnp.sum(d_raw, axis=0, keepdims=True)
    dx_ref[0, 0:LOCAL, CH:MIX] = d_raw.astype(BF16)
    dx_ref[0, LOCAL:PAY, CH:MIX] = jnp.zeros((16, 128), BF16)

    keeps = [same_before(seg, k) for k in range(1, 4)]
    zeros = jnp.zeros((8, 128), F32)
    for j in range(5):
        at = slice(128 * j, 128 * j + 128)
        x = xbc_ref[0, :, at].astype(F32)
        ext = jnp.concatenate([x[LOCAL + 8 :], x[:LOCAL]], axis=0)
        du = dxc_ref[:, at] * slope_ref[:, at]
        dpar_ref[4:5, at] += jnp.sum(du, axis=0, keepdims=True)
        dpar_ref[0:1, at] += jnp.sum(du * x[:LOCAL], axis=0, keepdims=True)
        total = par[0:1, at] * du
        before = zeros
        for k in range(1, 4):
            kept = jnp.where(keeps[k - 1], du, 0.0)
            moved = ext[8 - k : 8 - k + LOCAL]
            dpar_ref[k : k + 1, at] += jnp.sum(kept * moved, axis=0, keepdims=True)
            back = jnp.concatenate([zeros, kept * par[k : k + 1, at], zeros], axis=0)
            total = total + back[8 + k : 8 + k + LOCAL]
            before = before + back[k : k + 8]
        dx_ref[0, 0:LOCAL, at] = total.astype(BF16)
        dx_ref[0, LOCAL:PAY, at] = jnp.concatenate([zeros, before], axis=0).astype(BF16)


def norm_row(grad, weight):
    column = jnp.sum(grad * weight.astype(F32), axis=1, keepdims=True)
    return jnp.broadcast_to(column, (ROWS, 128)).T[0:1]


def early_grad_fn(at_ref, n_ref, d_ref, wall_ref, keep_ref, got_ref, *refs):
    step = pl.program_id(0)
    outs, norm_ref = refs[:4], refs[4]
    grad = mm(n_ref[...], d_ref[...], TN)

    @pl.when(step == 0)
    def _():
        norm_ref[...] = jnp.zeros_like(norm_ref)

    norm_ref[pl.ds(step, 1)] = norm_row(grad, wall_ref[:, MIX:])
    low = grad.astype(BF16)
    owner = lax.rem(at_ref[0] + step, 4)
    for r in range(4):
        for mine, src in ((True, keep_ref), (False, got_ref)):

            @pl.when((step == r) & ((lax.div(owner, 2) == at_ref[1]) == mine))
            def _(src=src, out=outs[r]):
                for q in range(4):
                    first = pl.multiple_of(192 * lax.rem(owner, 2) + 48 * q, 16)
                    out[192 * q : 192 * q + 96] = low[96 * q : 96 * q + 96]
                    out[192 * q + 96 : 192 * q + 144] = src[pl.ds(first, 48), 0:ROWS]
                    out[192 * q + 144 : 192 * q + 192] = src[pl.ds(first, 48), ROWS:]


def late_grad_fn(
    at_ref, n_ref, a_ref, wall_ref, b_ref, norm_ref, par_ref, gain_ref, skip_ref, head_ref, *refs
):
    step = pl.program_id(0)
    outs, small_ref = refs[:5], refs[5]
    half = 4 * PAY
    grad = mm(n_ref[0:half], a_ref[:, 0:CH], TN) + mm(n_ref[half:], b_ref[:, 0:CH], TN)
    heads = mm(a_ref[:, CH:], n_ref[0:half], TN) + mm(b_ref[:, CH:], n_ref[half:], TN)

    @pl.when(step == 0)
    def _():
        small_ref[...] = jnp.zeros_like(small_ref)
        small_ref[4:9] = par_ref[0:5]
        small_ref[9:10, 0:HP] = gain_ref[0:1]
        small_ref[10:11, 0:HP] = skip_ref[0:1]
        small_ref[11:13, 0:128] = head_ref[0:2]

    owner = lax.rem(at_ref[0] + step, 4)
    row = norm_row(grad, wall_ref[:, 0:CH]) + norm_ref[pl.ds(step, 1)]
    weights = wall_ref[:, CH:MIX].astype(F32).T[0:8]
    row = row + jnp.sum(heads[0:8] * weights, axis=0, keepdims=True)
    small_ref[pl.ds(owner, 1), 0:ROWS] = row
    low = grad.astype(BF16)
    rows = heads[0:16].astype(BF16)
    for r, out in enumerate((outs[0], outs[1], outs[3], outs[4])):

        @pl.when(step == (0, 1, 2, 3)[r])
        def _(out=out, r=r):
            if r == 2:
                outs[2][...] = low[0:HALF]
                out[0 : ROWS - HALF] = low[HALF:]
            else:
                out[0:ROWS] = low
            out[-16:, 0:ROWS] = rows
            out[-16:, ROWS:] = jnp.zeros((16, CH - ROWS), BF16)

    @pl.when(step == 3)
    def _():
        for out in (outs[0], outs[1], outs[3], outs[4]):
            out[-32:-16] = small_ref[...].astype(BF16)


def patch_fn(first, a_ref, b_ref, out_ref):
    out_ref[...] = a_ref[...]
    at = slice(first, first + b_ref.shape[0])
    out_ref[at] = (a_ref[at].astype(F32) + b_ref[...].astype(F32)).astype(BF16)


def lines_fn(a_ref, b_ref, c_ref, d_ref, lines_ref, small_ref):
    total = jnp.zeros((96, 2 * STATE), F32)
    for line, ref in enumerate((a_ref, b_ref, c_ref, d_ref)):
        lines_ref[line] = ref[0:96, 0:HP]
        total = total + ref[0:96, HP:].astype(F32)
        small_ref[line] = ref[96:]
    lines_ref[4, :, 0 : 2 * STATE] = total.astype(BF16)
    lines_ref[4, :, 2 * STATE :] = jnp.zeros((96, 128), BF16)


def final_grad_fn(at_ref, m_ref, g_ref, send_ref, keep_ref):
    low = mm(m_ref[...], g_ref[...], TN).astype(BF16)

    @pl.when(pl.program_id(0) < 2)
    def _():
        send_ref[...] = low

    @pl.when(pl.program_id(0) >= 2)
    def _():
        keep_ref[...] = low


def split_fn(parts, at_ref, *refs):
    blocks, outs, sum_ref = refs[:-5], refs[-5:-1], refs[-1]
    total = blocks[0][...].astype(F32)
    for block in blocks[1:]:
        total = total + block[...].astype(F32)
    sum_ref[...] = total.astype(BF16)
    for k, out in enumerate(outs):
        quarter = lax.rem(at_ref[0] + k, 4)
        to = 0
        for first, rows in parts:
            if rows:
                start = pl.multiple_of(first + rows * quarter, 16)
                out[to : to + rows] = sum_ref[pl.ds(start, rows)]
                to += rows
            else:
                out[to:] = sum_ref[first:]


def back_proj_fn(ax_ref, bx_ref, az_ref, bz_ref, wall_ref, a_ref, b_ref):
    dx = jnp.concatenate([ax_ref[0], bx_ref[0]], axis=0)
    dz = jnp.concatenate([az_ref[0], bz_ref[0]], axis=0)
    for r in range(4):
        at = slice(ROWS * r, ROWS * r + ROWS)
        part = mm(dx, wall_ref[at, 0:MIX], NT) + mm(dz, wall_ref[at, MIX:], NT)
        low = part.astype(BF16)
        a_ref[0, :, at] = low[:PAY]
        b_ref[0, :, at] = low[PAY:]


def finish_fn(at_ref, a_ref, b_ref, c_ref, d_ref, ahead_ref, tok_ref, cot_ref, gain_ref, out_ref):
    values = tok_ref[...].astype(F32)
    inv = lax.rsqrt(jnp.mean(values * values, axis=1, keepdims=True) + EPS)
    mean = jnp.zeros((LOCAL, 1), F32)
    spots = [pl.multiple_of(ROWS * lax.rem(at_ref[0] + r, 4), 128) for r in range(4)]
    for r, spot in enumerate(spots):
        at, to = slice(ROWS * r, ROWS * r + ROWS), pl.ds(spot, ROWS)
        total = a_ref[0:LOCAL, at].astype(F32) + b_ref[0:LOCAL, at].astype(F32)
        total = total + c_ref[0:LOCAL, at].astype(F32) + d_ref[0:LOCAL, at].astype(F32)
        last = jnp.concatenate([jnp.zeros((LOCAL - 8, ROWS), F32), ahead_ref[8:16, at].astype(F32)], axis=0)
        e1 = (total + last) * gain_ref[:, to]
        out_ref[:, to] = e1
        w = tok_ref[:, to].astype(F32) * inv
        mean = mean + jnp.sum(e1 * w, axis=1, keepdims=True)
    mean = mean / D
    for r in range(4):
        to = slice(ROWS * r, ROWS * r + ROWS)
        w = tok_ref[:, to].astype(F32) * inv
        out_ref[:, to] = cot_ref[:, to].astype(F32) + inv * (out_ref[:, to] - w * mean)


def place_early_fn(at_ref, mine_ref, sib_ref, out_ref, final_ref):
    def fill(refs):
        for c in range(2):
            for line in range(4):
                block = refs[c][0, lax.rem(at_ref[0] - line + 4, 4)].astype(F32)
                for a in range(2):
                    first = (2 * c + a) * 768 + 192 * line
                    out_ref[:, first : first + 192] = block[0:96, 192 * a : 192 * a + 192]
                    first = 768 * c + 384 * a
                    final_ref[line, :, first : first + 384] = block[96 + 48 * a : 144 + 48 * a]

    for mine, refs in ((0, (mine_ref, sib_ref)), (1, (sib_ref, mine_ref))):

        @pl.when(at_ref[1] == mine)
        def _(refs=refs):
            fill(refs)


def place_late_fn(at_ref, *refs):
    arrays, (out_ref, buf, sem) = refs[:8], refs[8:]
    y, core = at_ref[0], at_ref[1]
    step = pl.program_id(0)

    def fetch(number, slot):
        for k in range(4):

            @pl.when(number == k)
            def _(k=k):
                for i in range(2):
                    to = buf.at[slot, lax.rem(core + i, 2)]
                    pltpu.make_async_copy(arrays[4 * i + k], to, sem.at[slot, i]).start()

    slot = lax.rem(step, 2)

    @pl.when(step == 0)
    def _():
        fetch(step, slot)

    @pl.when(step < 3)
    def _():
        fetch(step + 1, 1 - slot)

    for i in range(2):
        pltpu.make_async_copy(arrays[0], buf.at[slot, i], sem.at[slot, i]).wait()
    for c in range(2):
        for line in range(4):
            block = buf[slot, c, lax.rem(y - line + 4, 4)].astype(F32)
            for a in range(2):
                first = (2 * c + a) * 768 + 192 * line
                out_ref[:, first : first + 192] = block[:, 192 * a : 192 * a + 192]
    total = buf[slot, 0, 4].astype(F32) + buf[slot, 1, 4].astype(F32)
    out_ref[:, INNER:] = total[:, 0 : 2 * STATE]


def place_small_fn(
    at_ref, own_ref, sib_ref, gain_ref,
    taps_ref, bias_ref, gating_ref, skip_ref, heads_ref, norm_ref, step_ref, buf_ref,
):
    y, core = at_ref[0], at_ref[1]
    buf_ref[...] = jnp.zeros_like(buf_ref)
    taps = jnp.zeros((8, 2 * STATE), F32)
    norm = jnp.zeros((4, ROWS), F32)
    for mine, sets in ((0, (own_ref, sib_ref)), (1, (sib_ref, own_ref))):

        @pl.when(core == mine)
        def _(sets=sets):
            for c in range(2):
                for line in range(4):
                    rows = sets[c][lax.rem(y - line + 4, 4)].astype(F32)
                    for a in range(2):
                        at = (2 * c + a) * 768 + 192 * line
                        at = slice(at, at + 192)
                        part = rows[:, 192 * a : 192 * a + 192]
                        taps_ref[:, at] = part[4:8]
                        bias_ref[:, at] = part[8:9]
                        gating_ref[:, at] = part[9:10]
                        skip_ref[:, at] = part[10:11]
                        at = 12 * (2 * c + a) + 3 * line
                        heads_ref[0:2, at : at + 3] = rows[11:13, 3 * a : 3 * a + 3]
                        buf_ref[at : at + 3] = rows[16 + 3 * a : 19 + 3 * a, 0:ROWS]

    for ref in (own_ref, sib_ref):
        for slot in range(4):
            rows = ref[slot].astype(F32)
            taps = taps + rows[4:12, HP:CH]
            norm = norm + rows[0:4, 0:ROWS]
    taps_ref[:, INNER:] = taps[0:4]
    bias_ref[:, INNER:] = taps[4:5]
    norm_ref[...] = norm / gain_ref[...]
    step_ref[...] = buf_ref[...].T[:, 0:HEADS]


def per_device(
    tokens,
    segments,
    cotangent,
    gate_proj,
    mixer_proj,
    step_proj,
    final_proj,
    norm_gain,
    conv_kernel,
    conv_bias,
    step_offset,
    log_rates,
    skip_gain,
    gating_gain,
):
    ctx = lax.axis_index("ctx")
    x = lax.axis_index("fsdp")
    y = lax.axis_index("y")
    core = lax.axis_index("core")
    turn = (x - 2 * core + 4) % 4

    def scalars(*values):
        return jnp.stack([jnp.asarray(v, jnp.int32) for v in values])

    z = ctx * 2 + lax.axis_index("low")
    flag, where = scalars(ctx), scalars(y, core)

    tokens = tokens.reshape(LOCAL, D)
    cot = cotangent.reshape(LOCAL, D)
    slab, final_rows = call(
        pack_kernel_fn,
        "pack",
        [
            (where, SMEM), (gate_proj, HBM), (mixer_proj, HBM), (final_proj, HBM),
            (step_proj, None),
        ],
        [((ROWS, WIDE), BF16, None), ((192, D), BF16, None)],
        steps=1,
        scratch=[
            pltpu.VMEM((5, ROWS, 256), BF16),
            pltpu.VMEM((ROWS, WIDE), F32),
            pltpu.SemaphoreType.DMA((6,)),
        ],
    )

    def first_hop(own, shift):
        return [own, shift(own, 1), shift(own, -1)]

    def far_hop(hop, shift, cut):
        own, below, above = hop
        ends = below[:cut], above[cut:]
        return ends, [own, below, shift(ends[0], 1), shift(ends[1], -1), above]

    slabs = first_hop(slab, x_shift)
    ahead = lax.ppermute(after(tokens, slab)[LOCAL - 16 :], "ctx", [(0, 1)])
    (payload,) = call(
        prep_kernel_fn,
        "prep",
        [
            (scalars(x, ctx), SMEM), (tokens, None), (ahead, None), (norm_gain[None], None),
            (segments, None),
        ],
        [((PAY, D), BF16, None)],
        steps=1,
        scratch=[pltpu.VMEM((PAY, D), BF16)],
    )
    mine = first_hop(payload, y_shift)
    par, hp, gain = call(
        params_kernel_fn,
        "params",
        [
            (where, SMEM), (conv_kernel, None), (conv_bias[None], None),
            (step_offset[None], None), (log_rates[None], None), (skip_gain[None], None),
            (gating_gain[None], None),
        ],
        [((8, CH), F32, None), ((8, 128), F32, None), ((8, HP), F32, None)],
        steps=1,
        wait=[payload],
    )
    _, slabs = far_hop(slabs, x_shift, 192)
    own_theirs = core_swap(payload)
    mine = list(after(tuple(mine), own_theirs, slabs[2], slabs[3]))
    cot_all = lax.all_gather(after(cot, mine[1], mine[2]), ("y", "core"), axis=0)

    def owner(r, c):
        return (2 * c + r) % 4

    def from_owners(steps):
        def to(ctx, x, y, low, core):
            r = (x - 2 * core) % 4
            return (ctx, owner(steps[r], core), y, low, core) if r in steps else None

        return to

    def token_outputs(place, count, spot):
        def at(shape):
            return (1,) + shape, lambda i: (place(i),) + (0,) * len(shape)

        outs = [
            ((PAY, D), BF16),
            ((PAY, CH), BF16),
            ((LOCAL, CH), BF16),
            ((LOCAL, STATE), BF16),
            ((LOCAL, 128), F32),
            ((LOCAL, HP), BF16),
            ((8, LOCAL), F32),
            ((LOCAL, HP), BF16),
        ]
        outs = [((GROUP,) + shape, dtype, at(shape)) for shape, dtype in outs]
        state = (1, HP, STATE), lambda i: (spot(i), 0, 0)
        return outs + [((count, HP, STATE), BF16, state)]

    base = [(flag, SMEM), (par, None), (hp, None)]
    scratch = [
        pltpu.VMEM((LOCAL, CH), BF16),
        pltpu.VMEM((2, PAY, D), BF16),
        pltpu.SemaphoreType.DMA((2,)),
    ]
    own, below, far_a, far_b, above = slabs
    wall, *kept = call(
        forward_first_fn,
        "forward_first",
        base
        + [(part, HBM) for part in (payload, own_theirs)]
        + [(part, HBM) for part in (own, above, far_a, far_b, below)],
        [((D, WIDE), BF16, None)] + token_outputs(lambda i: 4 * i, 6, lambda i: i),
        steps=2,
        scratch=scratch + [pltpu.SemaphoreType.DMA((5,))],
    )
    _, below, above = mine
    theirs = [core_swap(below), core_swap(above)]
    below, above, *theirs = after((below, above, *theirs), kept[-1])
    far = y_shift(below[:CUT], 1), y_shift(above[CUT:], -1)
    final_rows = after(final_rows, kept[-1])
    near = move(final_rows, from_owners({0: 1, 1: 0}))
    kept = call(
        forward_near_fn,
        "forward_near",
        base
        + [(wall, None)]
        + [(part, HBM) for part in [below, above, *theirs]]
        + [(part, HBM) for part in kept],
        token_outputs(lambda i: 4 * (i // 2) + 1 + 2 * (i % 2), 6, lambda i: 2 + i),
        steps=4,
        scratch=scratch,
        aliases={8 + i: i for i in range(9)},
    )
    *kept, state_a = kept
    state_in_a = lax.ppermute(state_a, "ctx", [(0, 1)])
    final_rows, *far = after((final_rows, *far), state_a)
    theirs = [core_swap(part) for part in far]
    far_rows = move(final_rows, from_owners({0: 3, 1: 2}))
    away = move(final_rows, from_owners({0: 2, 1: 3}))
    *kept, state_b = call(
        forward_far_fn,
        "forward_far",
        base
        + [(wall, None)]
        + [(part, HBM) for part in [*far, *theirs]]
        + [(part, HBM) for part in kept],
        token_outputs(lambda i: 4 * i + 2, 2, lambda i: i),
        steps=2,
        scratch=scratch,
        aliases={8 + i: i for i in range(8)},
    )
    nall, xbc, u, out_basis, small, gate, segs, y_local = kept
    state_in_b = lax.ppermute(state_b, "ctx", [(0, 1)])

    def state_blocks(first=0):
        def near_at(i, *s):
            line, core = (i + first) % 4, (i + first) // 4
            return (jnp.where(line == 0, core, 2 + 2 * core + line // 2), 0, 0)

        def far_at(i, *s):
            return ((i + first) // 4, 0, 0)

        return [(state_in_a, ((1, HP, STATE), near_at)), (state_in_b, ((1, HP, STATE), far_at))]

    rows = (GROUP, LOCAL, HP)
    wide = seq(LOCAL, HP)
    token = seq(LOCAL, 128)
    line = seq(8, LOCAL)
    dmix, w_final = call(
        dmix_kernel_fn,
        "d_mixed",
        [(cot_all, by_device(LOCAL, D, steps=4, first=k)) for k in range(4)]
        + [(part, HBM) for part in [final_rows, near, far_rows, away]],
        [(rows, BF16, ((4, LOCAL, HP), lambda i, at: (i, 0, 0))), ((HP, D), BF16, None)],
        steps=2,
        scratch=[pltpu.SemaphoreType.DMA((2,))],
        ahead=[scalars(y, core, turn)],
    )
    y_all, gated, sums = call(
        gate_kernel_fn,
        "gate",
        [(flag, SMEM), (y_local, wide)]
        + state_blocks()
        + [(gate, wide), (dmix, wide), (out_basis, token), (small, token), (segs, line)]
        + [(gain, None)],
        [(rows, BF16, wide), (rows, BF16, wide), ((GROUP, 8, LOCAL), F32, line)],
        scratch=[pltpu.VMEM((LOCAL, HP), F32)],
    )

    (out,) = call(
        product_kernel_fn,
        "out_proj",
        [(where, SMEM), (gated, ((4, LOCAL, HP), lambda i: (i, 0, 0))), (w_final, None)],
        [((GROUP, LOCAL, D), BF16, HBM)],
        steps=2,
        scratch=[pltpu.VMEM((2, 4, LOCAL, D), BF16), pltpu.SemaphoreType.DMA((2, 4))],
    )
    swapped = core_swap(sums)
    sums = sums + jnp.concatenate([swapped[4:], swapped[:4]], axis=0)
    shifted = [y_shift(sums, steps) for steps in (1, 2, 3)]
    shifted = after(tuple(shifted), out)
    total = sums
    for steps, got in zip((1, 2, 3), shifted, strict=True):
        got = got.reshape(2, 4, 8, LOCAL)
        got = jnp.concatenate([got[:, 4 - steps :], got[:, : 4 - steps]], axis=1)
        total = total + got.reshape(GROUP, 8, LOCAL)
    out = lax.psum_scatter(out, ("y", "core"), scatter_dimension=0, tiled=True)
    mixed, dy, dz, dstate, dgain = call(
        ungate_kernel_fn,
        "ungate",
        [(flag, SMEM), (y_all, wide), (gate, wide), (dmix, wide), (total, line)]
        + [(out_basis, token), (small, token), (segs, line), (gain, None)],
        [
            (rows, BF16, by_device(LOCAL, HP)),
            (rows, BF16, wide),
            ((GROUP, PAY, HP), BF16, seq(PAY, HP)),
            ((GROUP, HP, STATE), BF16, seq(HP, STATE)),
            ((8, HP), F32, None),
        ],
        ahead=[where],
    )
    dstate_in = lax.ppermute(dstate, "ctx", [(1, 0)])

    mixed_rows = mixed.reshape(GROUP * LOCAL, HP)

    half = lambda i, at: (0, 2 * ((at[1] + 1 + i // 2) % 2) + i % 2)
    final_send, final_kept = call(
        final_grad_fn,
        "grad_final",
        [
            (mixed_rows, None),
            (cot_all.reshape(GROUP * LOCAL, D), ((GROUP * LOCAL, ROWS), half)),
        ],
        [
            ((HP, 768), BF16, ((HP, ROWS), lambda i, at: (0, jnp.minimum(i, 1)))),
            ((HP, 768), BF16, ((HP, ROWS), lambda i, at: (0, jnp.maximum(i - 2, 0)))),
        ],
        steps=4,
        ahead=[where],
    )
    final_got = core_swap(final_send)

    normed_rows = nall.reshape(GROUP * PAY, D)

    def grad_inputs(grads):
        return [
            (scalars(x, core), SMEM),
            (normed_rows, ((GROUP * PAY, ROWS), lambda i, *s: (0, i))),
            (grads, None),
            (wall, ((ROWS, WIDE), lambda i, *s: (i, 0))),
        ]

    def over_x(blocks):
        own, ahead, far, behind = blocks
        return own, x_shift(far, 2), x_shift(ahead, 1), x_shift(behind, -1)

    def over_z(blocks, parts, rows):
        shape = blocks[0].shape
        quarters = call(
            functools.partial(split_fn, parts),
            "split",
            [(scalars(z), SMEM)] + [(block, None) for block in blocks],
            [((rows, shape[1]), BF16, None)] * 4,
            steps=1,
            scratch=[pltpu.VMEM(shape, BF16)],
        )
        return quarters, [quarters[0]] + [z_shift(quarters[k], k) for k in (2, 1, 3)]

    def over_y(piece):
        return [piece] + [y_shift(piece, s) for s in (1, 2, 3)]

    def gathered(lines):
        own, small = call(
            lines_fn,
            "lines",
            [(line, None) for line in lines],
            [((5, 96, HP), BF16, None), ((4, 32, CH), BF16, None)],
            steps=1,
        )
        mine = [own] + [z_shift(own, k) for k in (2, 1, 3)]
        mine = [mine[0], mine[2], mine[1], mine[3]]
        return (small, core_swap(small)), mine

    *early, norm_gate = call(
        early_grad_fn,
        "grad_gate",
        grad_inputs(dz.reshape(GROUP * PAY, HP)) + [(final_kept, None), (final_got, None)],
        [((2 * ROWS, HP), BF16, None)] * 4 + [((8, HP), F32, None)],
        steps=4,
    )
    early_block = early[0]
    early = over_x(early)

    def back(first, sums, wait):
        def spot(*rest):
            return seq(*rest, first=first)

        return call(
            back_kernel_fn,
            "back",
            [
                (flag, SMEM), (dy, spot(LOCAL, HP)), (u, spot(LOCAL, CH)), (xbc, spot(PAY, CH)),
                (small, spot(LOCAL, 128)), (segs, spot(8, LOCAL)), (par, None), (hp, None),
            ]
            + state_blocks(first)
            + [(dstate_in, spot(HP, STATE))]
            + [(value, None) for value in sums],
            [
                ((4, PAY, MIX), BF16, seq(PAY, MIX, high=4)),
                ((8, HP), F32, None),
                ((8, CH), F32, None),
                ((8, 128), F32, None),
            ],
            steps=4,
            scratch=[
                pltpu.VMEM((128, LOCAL), F32),
                pltpu.VMEM((LOCAL, CH), F32),
                pltpu.VMEM((LOCAL, 128), F32),
                pltpu.VMEM((LOCAL, 128), F32),
                pltpu.VMEM((LOCAL, CH), BF16),
                pltpu.VMEM((LOCAL, CH), F32),
            ],
            wait=wait,
        )

    sums = [jnp.zeros((8, HP), F32), jnp.zeros((8, CH), F32), jnp.zeros((8, 128), F32)]
    dx_mine, *sums = back(0, sums, [early_block])
    quarters, early = over_z(after(tuple(early), sums[0]), ((0, 192),), 192)
    factor = lax.rsqrt(total[0, 0] / INNER + EPS)[:, None]
    layer_out = tokens.astype(F32) + factor * out[0].astype(F32)
    dx_theirs, *sums = back(4, sums, [*quarters[1:], layer_out])
    dskip, dpar, dhead = sums
    piece = add(*after(tuple(early), dpar))
    early = over_y(piece)

    def back_projected(first, count, wait):
        mine = lambda i: (first + 2 * i, 0, 0)
        theirs = lambda i: (4 + first + 2 * i, 0, 0)
        block, out = (1, PAY, MIX), ((1, PAY, D), lambda i: (i, 0, 0))
        a, b = call(
            back_proj_fn,
            "back_proj",
            [
                (dx_mine, (block, mine)), (dx_theirs, (block, mine)),
                (dz, ((1, PAY, HP), mine)), (dz, ((1, PAY, HP), theirs)), (wall, None),
            ],
            [((count, PAY, D), BF16, out)] * 2,
            steps=count,
            wait=wait,
        )
        return a, b

    far_mine, far_theirs = back_projected(2, 1, [piece])
    far_theirs = core_swap(far_theirs)
    blocks = call(
        late_grad_fn,
        "grad_mixer",
        grad_inputs(dx_mine.reshape(4 * PAY, MIX))
        + [(dx_theirs.reshape(4 * PAY, MIX), None)]
        + [(value, None) for value in (norm_gate, dpar, dgain, dskip, dhead)],
        [((rows, CH), BF16, None) for rows in (ROWS + 32, ROWS + 32, HALF, HALF, ROWS + 32)],
        steps=4,
        wait=[far_mine],
        scratch=[pltpu.VMEM((16, CH), F32)],
    )
    stack = jnp.stack(after(tuple(early), blocks[0]))
    early = lax.all_gather(stack, ("ctx", "low"), axis=0)

    def patched(a, b, first):
        return call(
            functools.partial(patch_fn, first),
            "patch",
            [(a, None), (b, None)],
            [(a.shape, BF16, None)],
            steps=1,
        )[0]

    far_mine, far_theirs = after((far_mine, far_theirs), blocks[0])
    ends = (
        add(far_mine[0, :CUT], far_theirs[0, :CUT]),
        add(far_mine[0, CUT:], far_theirs[0, CUT:]),
    )
    x_up, x_down = x_shift(blocks[2], 1), x_shift(blocks[3], -1)
    up, down = y_shift(ends[0], 1), y_shift(ends[1], -1)
    mine, theirs = back_projected(1, 2, [*ends, stack])
    x_up, x_down = after((x_up, x_down), mine)
    late = blocks[0], patched(blocks[1], x_up, 0), patched(blocks[4], x_down, HALF)
    ends = late[1:]
    theirs, up, down = after((theirs, up, down), *ends)
    theirs = core_swap(theirs)
    late = late[0], x_shift(late[1], 1), x_shift(late[2], -1)
    tail = jnp.zeros((PAY - CUT, D), BF16)
    above = add(mine[1], theirs[1], jnp.concatenate([up, tail], axis=0))
    head = jnp.zeros((CUT, D), BF16)
    below = add(mine[0], theirs[0], jnp.concatenate([head, down], axis=0))
    back_got = y_shift(above, 1), y_shift(below, -1)
    back_own = back_projected(0, 1, [*ends, above, below])
    late = after(tuple(late), back_own[0], *back_got)
    quarters, late = over_z(late, ((0, 96), (ROWS, 0)), 128)
    back_own = back_own[0], core_swap(back_own[1])
    piece = add(*late)
    late = over_y(piece)
    parts = [value.reshape(PAY, D) for value in back_own] + list(back_got)
    ahead = add(*[part[LOCAL:] for part in parts])
    ahead = lax.ppermute(ahead, "ctx", [(1, 0)])
    (grad_tokens,) = call(
        finish_fn,
        "finish",
        [(scalars(x), SMEM)]
        + [(part, None) for part in parts + [ahead, tokens, cot, norm_gain[None]]],
        [((LOCAL, D), F32, None)],
        steps=1,
    )
    rest, late = gathered(after(tuple(late), grad_tokens))

    early = after(early, rest[1])
    quarter = ((1, 4, 192, HP), lambda i: (i, 0, 0, 0))
    grad_gate, grad_final = call(
        place_early_fn,
        "place_early",
        [(where, SMEM), (early, quarter), (core_swap(early), quarter)],
        [
            ((ROWS, INNER), F32, ((96, INNER), lambda i: (i, 0))),
            ((4, 192, D), F32, ((4, 48, D), lambda i: (0, i, 0))),
        ],
        steps=4,
        wait=[rest[1]],
    )
    taps, bias, gating, skip, heads, norm, grad_step = call(
        place_small_fn,
        "place_small",
        [(where, SMEM), (rest[0], None), (rest[1], None), (norm_gain.reshape(4, ROWS), None)],
        [((4, CONV_CH), F32, None), ((1, CONV_CH), F32, None)]
        + [((1, INNER), F32, None)] * 2
        + [((8, HEADS), F32, None), ((4, ROWS), F32, None), ((ROWS, HEADS), F32, None)],
        steps=1,
        scratch=[pltpu.VMEM((128, ROWS), F32)],
    )
    late = list(after(tuple(late), grad_gate, taps))
    late = late + [core_swap(part) for part in late]
    (grad_mixer,) = call(
        place_late_fn,
        "place_late",
        [(value, HBM) for value in late],
        [((ROWS, CONV_CH), F32, ((96, CONV_CH), lambda i, at: ((at[2] - i + 4) % 4, 0)))],
        steps=4,
        scratch=[pltpu.VMEM((2, 2, 5, 96, HP), BF16), pltpu.SemaphoreType.DMA((2, 2))],
        ahead=[scalars(y, core, z)],
    )
    shape = (1, LOCAL, D)
    return (
        layer_out.reshape(shape),
        grad_tokens.reshape(shape),
        grad_gate,
        grad_mixer,
        grad_step,
        grad_final.reshape(2 * 384, D),
        norm.reshape(D),
        taps,
        bias[0],
        heads[1],
        heads[0],
        jnp.sum(skip.reshape(HEADS, HEAD_DIM), axis=1),
        gating[0],
    )


def solution(mesh):
    apart = jax.sharding.Mesh(mesh.devices.reshape(2, 4, 4, 2, 2), AXES)
    batch = ("fsdp", "y", "low", "core")
    tokens = P(batch, "ctx", None)
    rows = P("fsdp", None)
    return jax.shard_map(
        per_device,
        mesh=apart,
        in_specs=(tokens, P(batch, None), tokens, rows, rows, rows, rows) + (P(),) * 7,
        out_specs=(tokens, tokens, rows, rows, rows, rows) + (P(),) * 7,
        check_vma=False,
    )
```

```python
import functools

import jax
import jax.numpy as jnp
from jax import lax
from jax.experimental import pallas as pl
from jax.experimental.pallas import tpu as pltpu
from jax.sharding import PartitionSpec as P

D = 1536
INNER = 3072
STATE = 128
HEADS = 48
HEAD_DIM = 64
CONV_CH = 3328
LOCAL = 256
GROUP = 8
OWN = 6
HP = OWN * HEAD_DIM
CH = HP + 2 * STATE
ROWS = D // 4
EPS = 1e-05
AXES = ("ctx", "fsdp", "y", "low", "core")
F32 = jnp.float32
BF16 = jnp.bfloat16
HIGH = lax.Precision.HIGHEST
MASKED = -1e30
PAY = LOCAL + 16
CUT = 144
WIDE = CH + 128 + HP
HALF = 208
MIX = CH + 128
SCALE = 1.0
DURATION = {
    "pack": 4, "prep": 3, "params": 2, "forward_first": 10, "forward_near": 18, "forward_far": 10, "d_mixed": 7, "gate": 7,
    "out_proj": 7, "ungate": 8, "grad_final": 0.1, "grad_gate": 0.1, "back": 38, "grad_mixer": 13,
    "back_proj": 6, "split": 3, "patch": 2, "ends": 1, "finish": 3, "layer_out": 2, "lines": 2, "place_early": 7, "place_late": 6, "place_small": 2,
}
VMEM_LIMIT = 63 * 1024 * 1024


def place_of(ctx, x, y, low, core):
    return (ctx * 4 + x) * 16 + (y * 2 + low) * 2 + core


def pairs_of(move):
    pairs = []
    for ctx in range(2):
        for x in range(4):
            for y in range(4):
                for low in range(2):
                    for core in range(2):
                        to = move(ctx, x, y, low, core)
                        if to is not None:
                            pairs.append((place_of(ctx, x, y, low, core), place_of(*to)))
    return pairs


def move(value, to):
    return lax.ppermute(value, AXES, pairs_of(to))


def x_shift(value, steps):
    return lax.ppermute(value, "fsdp", [(i, (i + steps) % 4) for i in range(4)])


def y_shift(value, steps):
    return lax.ppermute(value, "y", [(i, (i + steps) % 4) for i in range(4)])


def core_swap(value):
    return lax.ppermute(value, "core", [(0, 1), (1, 0)])


def z_shift(value, steps):
    def to(ctx, x, y, low, core):
        z = (2 * ctx + low + steps) % 4
        return (z // 2, x, y, z % 2, core)

    return move(value, to)


def after(value, *others):
    return lax.optimization_barrier((value,) + others)[0]


def add(*values):
    total = values[0].astype(F32)
    for value in values[1:]:
        total = total + value.astype(F32)
    return total.astype(BF16)


def mm(a, b, dims, precision=None):
    return lax.dot_general(a, b, (dims, ((), ())), precision=precision, preferred_element_type=F32)


NN = ((1,), (0,))
NT = ((1,), (1,))
TN = ((0,), (0,))
SMEM = object()
HBM = object()


def call(fn, name, inputs, outputs, steps=GROUP, scratch=(), aliases=None, ahead=(), wait=()):
    us = DURATION[name] * SCALE
    first = len(ahead) + len(inputs)
    inputs = inputs + [(value, HBM) for value in wait]

    def kernel(*refs):
        fn(*refs[:first], *refs[first + len(wait) :])

    def block(shape, how):
        if how is SMEM:
            return pl.BlockSpec(memory_space=pltpu.SMEM)
        if how is HBM:
            return pl.BlockSpec(memory_space=pl.ANY)
        if how is None:
            return pl.BlockSpec(tuple(shape), lambda i, *s: (0,) * len(shape))
        return pl.BlockSpec(*how)

    return pl.pallas_call(
        kernel,
        name=name,
        grid_spec=pltpu.PrefetchScalarGridSpec(
            num_scalar_prefetch=len(ahead),
            grid=(steps,),
            in_specs=[block(value.shape, how) for value, how in inputs],
            out_specs=[block(shape, how) for shape, _, how in outputs],
            scratch_shapes=list(scratch),
        ),
        out_shape=[jax.ShapeDtypeStruct(shape, dtype) for shape, dtype, _ in outputs],
        input_output_aliases=aliases or {},
        cost_estimate=pl.CostEstimate(
            flops=int(us * 1.15e9), bytes_accessed=int(us * 3.6e6), transcendentals=0
        ),
        compiler_params=pltpu.CompilerParams(
            dimension_semantics=("arbitrary",), vmem_limit_bytes=VMEM_LIMIT
        ),
    )(*ahead, *[value for value, _ in inputs])


def seq(*rest, first=0, low=0, high=GROUP):
    def at(i, *s):
        return (jnp.clip(i + first, low, high - 1) - low,) + (0,) * len(rest)

    return ((1,) + rest, at)


def by_device(*rest, steps=1, first=0):
    def at(i, at):
        i = i * steps + first
        y, core = (at[0] + 4 - i % 4) % 4, (at[1] + i // 4) % 2
        return (2 * y + core,) + (0,) * len(rest)

    return ((1,) + rest, at)


def lane_ids(rows, cols):
    return lax.broadcasted_iota(jnp.int32, (rows, cols), 1)


def pair(values, p, left):
    return jnp.where(left, values[:, 2 * p : 2 * p + 1], values[:, 2 * p + 1 : 2 * p + 2])


def small_parts(small):
    mine = lane_ids(LOCAL, 128) < OWN
    parts = small, pltpu.roll(small, 120, 1), pltpu.roll(small, 112, 1)
    return [jnp.where(mine, part, 0.0) for part in parts]


def summed_rows(values, dims):
    lane = lane_ids(LOCAL, 128)
    high = values.astype(BF16).astype(F32)
    rest = values - high
    middle = rest.astype(BF16).astype(F32)
    parts = jnp.where(lane < 8, high, jnp.where(lane < 16, middle, rest - middle))
    got = mm(triangle().astype(BF16), parts.astype(BF16), dims)
    return got + pltpu.roll(got, 120, 1) + pltpu.roll(got, 112, 1)


def head_sums(values, p):
    lane, row = lane_ids(128, 128), lax.broadcasted_iota(jnp.int32, (128, 128), 0)
    ones = jnp.where(lane == 2 * p + row // HEAD_DIM, 1.0, 0.0).astype(BF16)
    return mm(values.astype(BF16), ones, NN)


def triangle():
    row = lax.broadcasted_iota(jnp.int32, (LOCAL, LOCAL), 0)
    col = lax.broadcasted_iota(jnp.int32, (LOCAL, LOCAL), 1)
    return row >= col


def seg_columns(row):
    return jnp.broadcast_to(row, (128, LOCAL)).T


def same_before(seg, k):
    return jnp.concatenate([seg[:k], seg[: LOCAL - k]], axis=0) == seg


def mask_bias(seg, row):
    wide = jnp.concatenate([seg, seg], axis=1)
    return jnp.where((wide == row) & triangle(), 0.0, MASKED)


def prep_kernel_fn(at_ref, tok_ref, ahead_ref, gain_ref, seg_ref, out_ref, buf_ref):
    def normed(values):
        values = values.astype(F32)
        inv = lax.rsqrt(jnp.mean(values * values, axis=1, keepdims=True) + EPS)
        return (values * inv * gain_ref[...]).astype(BF16)

    buf_ref[0:LOCAL] = normed(tok_ref[...])
    seg = seg_ref[...].astype(F32)
    seg = jnp.where(at_ref[1] == 0, seg[:, :LOCAL], seg[:, LOCAL:])
    part = jnp.concatenate([seg, jnp.zeros((1, ROWS - LOCAL), F32)], axis=1)
    row = jnp.concatenate([part] * 4, axis=1)
    number = lax.broadcasted_iota(jnp.int32, (16, D), 0)
    extra = jnp.where(number >= 8, normed(ahead_ref[...]).astype(F32), 0.0)
    buf_ref[LOCAL:PAY] = jnp.where(number == 0, row, extra).astype(BF16)
    for r in range(4):
        start = pl.multiple_of(ROWS * lax.rem(at_ref[0] + r, 4), 128)
        out_ref[:, ROWS * r : ROWS * r + ROWS] = buf_ref[:, pl.ds(start, ROWS)]


def pack_kernel_fn(
    at_ref, gate_ref, mixer_ref, final_ref, step_ref,
    slab_ref, rows_ref, buf_ref, wide_ref, turn_ref, sem,
):
    y, core = at_ref[0], at_ref[1]
    copies = []
    for i, src in enumerate((mixer_ref, gate_ref)):
        for a in range(2):
            first = (2 * core + a) * 768 + 384 * lax.div(y, 2) + 128 * lax.rem(y, 2)
            where = pl.ds(pl.multiple_of(first, 128), 256)
            copies.append((src.at[:, where], buf_ref.at[2 * i + a]))
    copies.append((mixer_ref.at[:, pl.ds(INNER, 2 * STATE)], buf_ref.at[4]))
    copies.append((final_ref.at[pl.ds(pl.multiple_of(192 * y, 64), 192)], rows_ref))
    copies = [pltpu.make_async_copy(a, b, sem.at[i]) for i, (a, b) in enumerate(copies)]
    for copy in copies:
        copy.start()
    turn_ref[...] = jnp.zeros_like(turn_ref)
    step = step_ref[...].astype(F32)
    for line in range(4):
        for c in range(2):

            @pl.when((y == line) & (core == c))
            def _(line=line, c=c):
                for a in range(2):
                    at = 12 * (2 * c + a) + 3 * line
                    for to in range(3 * a, 24, 8):
                        turn_ref[to : to + 3] = step[at : at + 3]

    wide_ref[:, CH:MIX] = turn_ref[...].T
    for copy in copies:
        copy.wait()
    for odd in range(2):

        @pl.when(lax.rem(y, 2) == odd)
        def _(odd=odd):
            for i, base in enumerate((0, MIX)):
                for a in range(2):
                    block = buf_ref[2 * i + a].astype(F32)
                    to = base + 192 * a
                    wide_ref[:, to : to + 192] = block[:, 64 * odd : 64 * odd + 192]

    slab_ref[...] = wide_ref[...].astype(BF16)
    slab_ref[:, HP:CH] = buf_ref[4]


def params_kernel_fn(
    at_ref, taps_ref, bias_ref, offset_ref, rates_ref, skip_ref, gating_ref,
    par_ref, hp_ref, gain_ref,
):
    par_ref[...] = jnp.zeros_like(par_ref)
    hp_ref[...] = jnp.zeros_like(hp_ref)
    for line in range(4):
        for c in range(2):

            @pl.when((at_ref[0] == line) & (at_ref[1] == c))
            def _(line=line, c=c):
                for a in range(2):
                    at = slice((2 * c + a) * 768 + 192 * line, (2 * c + a) * 768 + 192 * line + 192)
                    to = slice(192 * a, 192 * a + 192)
                    par_ref[0:4, to] = taps_ref[:, at]
                    par_ref[4:5, to] = bias_ref[:, at]
                    gain_ref[0:1, to] = gating_ref[:, at]
                    at = slice(12 * (2 * c + a) + 3 * line, 12 * (2 * c + a) + 3 * line + 3)
                    for first in range(3 * a, 24, 8):
                        to = slice(first, first + 3)
                        hp_ref[0:1, to] = offset_ref[:, at]
                        hp_ref[1:2, to] = -jnp.exp(rates_ref[:, at])
                        hp_ref[2:3, to] = skip_ref[:, at]

    par_ref[0:4, HP:] = taps_ref[:, INNER:]
    par_ref[4:5, HP:] = bias_ref[:, INNER:]


class Pieces:
    def __init__(self, parts, buf, sem):
        self.parts, self.buf, self.sem = parts, buf, sem

    def fetch(self, step, slot):
        for k, refs in enumerate(self.parts):

            @pl.when(step == k)
            def _(refs=refs):
                first = 0
                for ref in refs:
                    to = self.buf.at[slot, first : first + ref.shape[0]]
                    pltpu.make_async_copy(ref, to, self.sem.at[slot]).start()
                    first += ref.shape[0]

    def next(self):
        step = pl.program_id(0)
        slot = lax.rem(step, 2)

        @pl.when(step == 0)
        def _():
            self.fetch(step, slot)

        @pl.when(step < len(self.parts) - 1)
        def _():
            self.fetch(step + 1, 1 - slot)

        pltpu.make_async_copy(self.buf.at[slot], self.buf.at[slot], self.sem.at[slot]).wait()
        return slot


def forward_body(
    ctx_ref, par_ref, hp_ref, n, wall_ref,
    nall_ref, xbc_ref, u_ref, out_ref, small_ref, z_ref, seg_ref, y_ref, state_ref, xc_ref,
):
    par = par_ref[...]
    hp = hp_ref[...]
    nall_ref[0] = n
    row = n[LOCAL:PAY, 0:LOCAL].astype(F32)[0:1]
    seg_ref[0] = jnp.broadcast_to(row, (8, LOCAL))
    seg = seg_columns(row)
    keeps = [same_before(seg, k) for k in range(1, 4)]
    z_ref[0] = mm(n[0:LOCAL], wall_ref[:, MIX:], NN).astype(BF16)
    for j in range(3):
        prod = mm(n, wall_ref[:, 256 * j : 256 * j + 256], NN)
        for half in range(2):
            first = 256 * j + 128 * half
            at = slice(first, first + 128)
            x = prod[:, 128 * half : 128 * half + 128]
            if first == CH:
                raw = x[0:LOCAL] + hp[0:1]
                continue
            low = x.astype(BF16)
            xbc_ref[0, :, at] = low
            x = low.astype(F32)
            ext = jnp.concatenate([x[LOCAL + 8 :], x[:LOCAL]], axis=0)
            u = par[4:5, at] + par[0:1, at] * x[:LOCAL]
            for k in range(1, 4):
                moved = ext[8 - k : 8 - k + LOCAL]
                u = u + par[k : k + 1, at] * jnp.where(keeps[k - 1], moved, 0.0)
            u_ref[0, :, at] = u.astype(BF16)
            xc_ref[:, at] = (u * jax.nn.sigmoid(u)).astype(BF16)
    dt = jnp.maximum(raw, 0.0) + jnp.log1p(jnp.exp(-jnp.abs(raw)))
    cum = summed_rows(dt * hp[1:2], NN)
    lane = lane_ids(LOCAL, 128)
    small_ref[0] = jnp.where(lane < 8, dt, jnp.where(lane < 16, pltpu.roll(cum, 8, 1), raw))
    left = lane < HEAD_DIM
    left1 = lane_ids(1, 128) < HEAD_DIM
    basis, out_basis = xc_ref[:, HP : HP + STATE], xc_ref[:, HP + STATE :]
    out_ref[0] = out_basis

    @pl.when(ctx_ref[0] == 0)
    def _():
        tail = jnp.where(seg == seg[LOCAL - 1 :], jnp.exp(cum[LOCAL - 1 :] - cum) * dt, 0.0)
        for p in range(3):
            at = slice(128 * p, 128 * p + 128)
            part = xc_ref[:, at].astype(F32) * pair(tail, p, left)
            state_ref[0, at] = mm(part.astype(BF16), basis, TN).astype(BF16)

    @pl.when(ctx_ref[0] != 0)
    def _():
        state_ref[0] = jnp.zeros((HP, STATE), BF16)

    cum_t = cum.T
    scores = mm(out_basis, basis, NT)
    bias = mask_bias(seg, row)
    for p in range(3):
        at = slice(128 * p, 128 * p + 128)
        x = xc_ref[:, at].astype(F32)
        scaled = (x * pair(dt, p, left)).astype(BF16)
        halves = []
        for h in (2 * p, 2 * p + 1):
            mix = jnp.exp(cum[:, h : h + 1] - cum_t[h : h + 1] + bias) * scores
            halves.append(mm(mix.astype(BF16), scaled, NN))
        y = jnp.where(left, halves[0], halves[1]) + pair(hp[2:3], p, left1) * x
        y_ref[0, :, at] = y.astype(BF16)


def forward_first_fn(ctx_ref, par_ref, hp_ref, mine, theirs, *refs):
    slabs, wall_ref, outs, (xc, buf, sem, wsem) = refs[:5], refs[5], refs[6:15], refs[15:]
    copies = []
    first = 0
    for i, ref in enumerate(slabs):
        rows = ref.shape[0]
        copies.append(pltpu.make_async_copy(ref, wall_ref.at[first : first + rows], wsem.at[i]))
        first += rows

    @pl.when(pl.program_id(0) == 0)
    def _():
        for copy in copies:
            copy.start()

    slot = Pieces([[mine], [theirs]], buf, sem).next()

    @pl.when(pl.program_id(0) == 0)
    def _():
        for copy in copies:
            copy.wait()

    forward_body(ctx_ref, par_ref, hp_ref, buf[slot], wall_ref, *outs, xc)


def forward_near_fn(ctx_ref, par_ref, hp_ref, wall_ref, *refs):
    parts, outs, (xc, buf, sem) = refs[:4], refs[13:22], refs[22:]
    slot = Pieces([[part] for part in parts], buf, sem).next()
    forward_body(ctx_ref, par_ref, hp_ref, buf[slot], wall_ref, *outs, xc)


def forward_far_fn(ctx_ref, par_ref, hp_ref, wall_ref, *refs):
    parts, outs, (xc, buf, sem) = refs[:4], refs[12:21], refs[21:]
    slot = Pieces([parts[:2], parts[2:]], buf, sem).next()
    forward_body(ctx_ref, par_ref, hp_ref, buf[slot], wall_ref, *outs, xc)


def dmix_kernel_fn(at_ref, *refs):
    g_refs, (own, near, far, away, dmix_ref, wf_ref, sem) = refs[:4], refs[4:]
    step = pl.program_id(0)
    up, down = wf_ref.at[0:192], wf_ref.at[192:HP]

    @pl.when(step == 0)
    def _():
        for r, (a, b) in enumerate(((own, near), (near, own), (away, far), (far, away))):

            @pl.when(at_ref[2] == r)
            def _(a=a, b=b):
                pltpu.make_async_copy(a, up, sem.at[0]).start()
                pltpu.make_async_copy(b, down, sem.at[1]).start()

        pltpu.make_async_copy(own, up, sem.at[0]).wait()
        pltpu.make_async_copy(own, down, sem.at[1]).wait()

    for k, ref in enumerate(g_refs):
        dmix_ref[k] = mm(ref[0], wf_ref[...], NT).astype(BF16)


def entered(k, ctx_ref, state_a_ref, state_b_ref, small_ref, seg_ref, use):
    @pl.when(ctx_ref[0] != 0)
    def _():
        number = 2 * pl.program_id(0) + k
        line, core = lax.rem(number, 4), lax.div(number, 4)
        near = jnp.where(line == 0, core, 2 + 2 * core + lax.div(line, 2))
        seg = seg_columns(seg_ref[k, 0:1])
        enter = jnp.where(seg == seg[0:1], jnp.exp(small_parts(small_ref[k])[1]), 0.0)
        left = lane_ids(LOCAL, 128) < HEAD_DIM
        for p in range(3):
            at = slice(128 * p, 128 * p + 128)
            state = jnp.where(line == 2, state_b_ref[core, at], state_a_ref[near, at])
            use(at, pair(enter, p, left), state)


def gate_kernel_fn(
    ctx_ref, y_ref, state_a_ref, state_b_ref, z_ref, dmix_ref, basis_ref, small_ref, seg_ref,
    gain_ref, yall_ref, low_ref, sums_ref, sum_ref,
):
    for k in range(2):
        sum_ref[...] = y_ref[k].astype(F32)

        def use(at, gate, state, k=k):
            sum_ref[:, at] += gate * mm(basis_ref[k], state, NT)

        entered(k, ctx_ref, state_a_ref, state_b_ref, small_ref, seg_ref, use)
        y = sum_ref[...]
        yall_ref[k] = y.astype(BF16)
        z = z_ref[k].astype(F32)
        gated = y * (z * jax.nn.sigmoid(z))
        raised = gated * gain_ref[0:1]
        low_ref[k] = raised.astype(BF16)
        first = jnp.sum(gated * gated, axis=1, keepdims=True)
        second = jnp.sum(dmix_ref[k].astype(F32) * raised, axis=1, keepdims=True)
        lane = lane_ids(LOCAL, 128)
        both = jnp.where(lane == 0, first, jnp.where(lane == 1, second, 0.0))
        sums_ref[k] = both.T[0:8]


def product_kernel_fn(at_ref, a_ref, w_ref, out_ref, buf, sem):
    step = pl.program_id(0)

    def copies(number):
        found = []
        for k in range(4):
            place = 2 * lax.rem(at_ref[0] + 4 - k, 4) + lax.rem(at_ref[1] + number, 2)
            found.append(pltpu.make_async_copy(buf.at[number, k], out_ref.at[place], sem.at[number, k]))
        return found

    for number in range(2):

        @pl.when(step == number)
        def _(number=number):
            for k, copy in enumerate(copies(number)):
                buf[number, k] = mm(a_ref[k], w_ref[...], NN).astype(BF16)
                copy.start()

    @pl.when(step == 1)
    def _():
        for number in range(2):
            for copy in copies(number):
                copy.wait()


def ungate_kernel_fn(
    at_ref, ctx_ref, y_ref, z_ref, dmix_ref, sums_ref, basis_ref, small_ref, seg_ref, gain_ref,
    mixed_ref, dy_ref, dz_ref, dstate_ref, dgain_ref, buf, sem,
):
    step = pl.program_id(0)
    slot = lax.rem(step, 2)

    def copy(number, k):
        place = 2 * lax.rem(at_ref[0] + 8 - 2 * number - k, 4)
        place = place + lax.rem(at_ref[1] + lax.div(number, 2), 2)
        spot = lax.rem(number, 2)
        return pltpu.make_async_copy(buf.at[spot, k], mixed_ref.at[place], sem.at[spot, k])

    @pl.when(step == 0)
    def _():
        dgain_ref[...] = jnp.zeros_like(dgain_ref)

    @pl.when(step >= 2)
    def _():
        for k in range(2):
            copy(step - 2, k).wait()

    gain = gain_ref[0:1]
    for k in range(2):
        pad = jnp.concatenate([sums_ref[k], jnp.zeros((120, LOCAL), F32)], axis=0).T
        inv = lax.rsqrt(pad[:, 0:1] / INNER + EPS)
        mean_ev = inv * pad[:, 1:2] / INNER
        y = y_ref[k].astype(F32)
        z = z_ref[k].astype(F32)
        dmix = dmix_ref[k].astype(F32)
        sig = jax.nn.sigmoid(z)
        act = z * sig
        v = y * act * inv
        buf[slot, k] = (v * gain).astype(BF16)
        copy(step, k).start()
        d_gated = inv * (dmix * gain - v * mean_ev)
        dy = (d_gated * act).astype(BF16)
        dy_ref[k] = dy
        dz_ref[k, 0:LOCAL] = (d_gated * y * sig * (1.0 + z * (1.0 - sig))).astype(BF16)
        dz_ref[k, LOCAL:PAY] = jnp.zeros((16, HP), BF16)
        dgain_ref[0:1] += jnp.sum(dmix * v, axis=0, keepdims=True)

        @pl.when(ctx_ref[0] != 0)
        def _(k=k, dy=dy):
            seg = seg_columns(seg_ref[k, 0:1])
            enter = jnp.where(seg == seg[0:1], jnp.exp(small_parts(small_ref[k])[1]), 0.0)
            left = lane_ids(LOCAL, 128) < HEAD_DIM
            for p in range(3):
                at = slice(128 * p, 128 * p + 128)
                part = (dy[:, at].astype(F32) * pair(enter, p, left)).astype(BF16)
                dstate_ref[k, at] = mm(part, basis_ref[k], TN).astype(BF16)

        @pl.when(ctx_ref[0] == 0)
        def _(k=k):
            dstate_ref[k] = jnp.zeros((HP, STATE), BF16)

    @pl.when(step == 3)
    def _():
        for number in (2, 3):
            for k in range(2):
                copy(number, k).wait()


def back_kernel_fn(
    ctx_ref, dy_ref, u_ref, xbc_ref, small_ref, seg_ref, par_ref, hp_ref, state_a_ref, state_b_ref,
    dstate_ref, skip0_ref, par0_ref, head0_ref,
    dx_ref, dskip_ref, dpar_ref, dhead_ref, turn_ref, dxc_ref, dc_ref, dd_ref, xc_ref, slope_ref,
):
    step = pl.program_id(0)
    hp = hp_ref[...]
    par = par_ref[...]
    dt, cum, raw = small_parts(small_ref[0])
    cum_t = cum.T
    for j in range(5):
        at = slice(128 * j, 128 * j + 128)
        u = u_ref[0, :, at].astype(F32)
        sig = jax.nn.sigmoid(u)
        xc_ref[:, at] = (u * sig).astype(BF16)
        slope_ref[:, at] = sig * (1.0 + u * (1.0 - sig))
    basis, out_basis = xc_ref[:, HP : HP + STATE], xc_ref[:, HP + STATE :]
    scores = mm(basis, out_basis, NT)
    row = seg_ref[0, 0:1]
    seg = seg_columns(row)
    same = jnp.concatenate([seg, seg], axis=1) == row
    first = lax.broadcasted_iota(jnp.int32, (LOCAL, LOCAL), 0)
    bias = jnp.where(same & (first <= lane_ids(LOCAL, LOCAL)), 0.0, MASKED)
    lane = lane_ids(LOCAL, 128)
    left = lane < HEAD_DIM
    left1 = lane_ids(1, 128) < HEAD_DIM

    @pl.when(step == 0)
    def _():
        dskip_ref[...] = skip0_ref[...]
        dpar_ref[...] = par0_ref[...]
        dhead_ref[...] = head0_ref[...]
        turn_ref[...] = jnp.zeros_like(turn_ref)

    d_scores = jnp.zeros((LOCAL, LOCAL), F32)
    sums = jnp.zeros((LOCAL, 128), F32)
    for p in range(3):
        at = slice(128 * p, 128 * p + 128)
        x = xc_ref[:, at].astype(F32)
        g = dy_ref[0, :, at]
        steps = pair(dt, p, left)
        scaled = (x * steps).astype(BF16)
        halves = []
        for h in (2 * p, 2 * p + 1):
            mine = left if h % 2 == 0 else ~left
            prod = mm(scaled, jnp.where(mine, g, jnp.zeros_like(g)), NT)
            mix = jnp.exp(cum_t[h : h + 1] - cum[:, h : h + 1] + bias)
            weighed = mix * prod
            d_scores = d_scores + weighed
            pulled = weighed * scores
            turn_ref[h : h + 1] = jnp.sum(pulled, axis=0, keepdims=True)
            sums = jnp.where(lane == h, jnp.sum(pulled, axis=1, keepdims=True), sums)
            halves.append(mm((mix * scores).astype(BF16), g, NN))
        gf = g.astype(F32)
        skip = pair(hp[2:3], p, left1)
        dxc_ref[:, at] = steps * jnp.where(left, halves[0], halves[1]) + skip * gf
        dskip_ref[0:1, at] += jnp.sum(gf * x, axis=0, keepdims=True)
    dd_ref[...] = jnp.where(dt > 1e-37, sums / jnp.maximum(dt, 1e-37), 0.0)
    dc_ref[...] = turn_ref[...].T - sums
    low = d_scores.astype(BF16)
    dxc_ref[:, HP : HP + STATE] = mm(low, out_basis, NN)
    dxc_ref[:, HP + STATE :] = mm(low, basis, TN)

    @pl.when(ctx_ref[0] != 0)
    def _():
        enter = jnp.where(seg == seg[0:1], jnp.exp(cum), 0.0)
        d_out = jnp.zeros((LOCAL, STATE), F32)
        extra = jnp.zeros((LOCAL, 128), F32)
        for p in range(3):
            at = slice(128 * p, 128 * p + 128)
            state = jnp.where(lax.rem(step, 4) == 2, state_b_ref[0, at], state_a_ref[0, at])
            scaled = dy_ref[0, :, at].astype(F32) * pair(enter, p, left)
            d_out = d_out + mm(scaled.astype(BF16), state, NN)
            extra = extra + head_sums(scaled * mm(out_basis, state, NT), p)
        dxc_ref[:, HP + STATE :] += d_out
        dc_ref[...] += extra

    @pl.when(ctx_ref[0] == 0)
    def _():
        tail = jnp.where(seg == seg[LOCAL - 1 :], jnp.exp(cum[LOCAL - 1 :] - cum), 0.0)
        weight = tail * dt
        d_basis = jnp.zeros((LOCAL, STATE), F32)
        d_weight = jnp.zeros((LOCAL, 128), F32)
        for p in range(3):
            at = slice(128 * p, 128 * p + 128)
            x = xc_ref[:, at].astype(F32)
            w = pair(weight, p, left)
            ds = dstate_ref[0, at]
            seen = mm(basis, ds, NT)
            dxc_ref[:, at] += w * seen
            d_basis = d_basis + mm((x * w).astype(BF16), ds, NN)
            d_weight = d_weight + head_sums(x * seen, p)
        dxc_ref[:, HP : HP + STATE] += d_basis
        dd_ref[...] += tail * d_weight
        moved = weight * d_weight
        dc_ref[...] -= moved
        dc_ref[LOCAL - 1 : LOCAL] += jnp.sum(moved, axis=0, keepdims=True)

    dc = jnp.where(lane < OWN, dc_ref[...], 0.0)
    dc = dc + pltpu.roll(dc, 8, 1) + pltpu.roll(dc, 16, 1)
    d_decay = summed_rows(dc, TN)
    rate = hp[1:2]
    d_raw = (dd_ref[...] + d_decay * rate) * jax.nn.sigmoid(raw)
    d_raw = jnp.where(lane < OWN, d_raw, 0.0)
    dhead_ref[0:1] += jnp.sum(d_decay * dt, axis=0, keepdims=True) * rate
    dhead_ref[1:2] += jnp.sum(d_raw, axis=0, keepdims=True)
    dx_ref[0, 0:LOCAL, CH:MIX] = d_raw.astype(BF16)
    dx_ref[0, LOCAL:PAY, CH:MIX] = jnp.zeros((16, 128), BF16)

    keeps = [same_before(seg, k) for k in range(1, 4)]
    zeros = jnp.zeros((8, 128), F32)
    for j in range(5):
        at = slice(128 * j, 128 * j + 128)
        x = xbc_ref[0, :, at].astype(F32)
        ext = jnp.concatenate([x[LOCAL + 8 :], x[:LOCAL]], axis=0)
        du = dxc_ref[:, at] * slope_ref[:, at]
        dpar_ref[4:5, at] += jnp.sum(du, axis=0, keepdims=True)
        dpar_ref[0:1, at] += jnp.sum(du * x[:LOCAL], axis=0, keepdims=True)
        total = par[0:1, at] * du
        before = zeros
        for k in range(1, 4):
            kept = jnp.where(keeps[k - 1], du, 0.0)
            moved = ext[8 - k : 8 - k + LOCAL]
            dpar_ref[k : k + 1, at] += jnp.sum(kept * moved, axis=0, keepdims=True)
            back = jnp.concatenate([zeros, kept * par[k : k + 1, at], zeros], axis=0)
            total = total + back[8 + k : 8 + k + LOCAL]
            before = before + back[k : k + 8]
        dx_ref[0, 0:LOCAL, at] = total.astype(BF16)
        dx_ref[0, LOCAL:PAY, at] = jnp.concatenate([zeros, before], axis=0).astype(BF16)


def norm_row(grad, weight):
    column = jnp.sum(grad * weight.astype(F32), axis=1, keepdims=True)
    return jnp.broadcast_to(column, (ROWS, 128)).T[0:1]


def early_grad_fn(at_ref, n_ref, d_ref, wall_ref, keep_ref, got_ref, *refs):
    step = pl.program_id(0)
    outs, norm_ref = refs[:4], refs[4]
    grad = mm(n_ref[...], d_ref[...], TN)

    @pl.when(step == 0)
    def _():
        norm_ref[...] = jnp.zeros_like(norm_ref)

    norm_ref[pl.ds(step, 1)] = norm_row(grad, wall_ref[:, MIX:])
    low = grad.astype(BF16)
    owner = lax.rem(at_ref[0] + step, 4)
    for r in range(4):
        for mine, src in ((True, keep_ref), (False, got_ref)):

            @pl.when((step == r) & ((lax.div(owner, 2) == at_ref[1]) == mine))
            def _(src=src, out=outs[r]):
                for q in range(4):
                    first = pl.multiple_of(192 * lax.rem(owner, 2) + 48 * q, 16)
                    out[192 * q : 192 * q + 96] = low[96 * q : 96 * q + 96]
                    out[192 * q + 96 : 192 * q + 144] = src[pl.ds(first, 48), 0:ROWS]
                    out[192 * q + 144 : 192 * q + 192] = src[pl.ds(first, 48), ROWS:]


def late_grad_fn(
    at_ref, n_ref, d_ref, wall_ref, norm_ref, par_ref, gain_ref, skip_ref, head_ref, *refs
):
    step = pl.program_id(0)
    outs, small_ref = refs[:5], refs[5]
    grad = mm(n_ref[...], d_ref[...], TN)
    rows = grad[:, CH:].T[0:16].astype(BF16)
    low = grad[:, 0:CH].astype(BF16)

    @pl.when(step == 0)
    def _():
        small_ref[...] = jnp.zeros_like(small_ref)
        small_ref[4:9] = par_ref[0:5]
        small_ref[9:10, 0:HP] = gain_ref[0:1]
        small_ref[10:12, 0:128] = head_ref[0:2]
        lane = lane_ids(1, 128)
        skip = jnp.zeros((1, 128), F32)
        for h in range(OWN):
            part = skip_ref[0:1, HEAD_DIM * h : HEAD_DIM * h + HEAD_DIM]
            skip = jnp.where(lane == h, jnp.sum(part, axis=1, keepdims=True), skip)
        small_ref[12:13, 0:128] = skip

    owner = lax.rem(at_ref[0] + step, 4)
    row = norm_row(grad, wall_ref[:, 0:MIX]) + norm_ref[pl.ds(step, 1)]
    small_ref[pl.ds(owner, 1), 0:ROWS] = row
    for r, out in enumerate((outs[0], outs[1], outs[3], outs[4])):

        @pl.when(step == (0, 1, 2, 3)[r])
        def _(out=out, r=r):
            if r == 2:
                outs[2][...] = low[0:HALF]
                out[0 : ROWS - HALF] = low[HALF:]
            else:
                out[0:ROWS] = low
            out[-16:, 0:ROWS] = rows
            out[-16:, ROWS:] = jnp.zeros((16, CH - ROWS), BF16)

    @pl.when(step == 3)
    def _():
        for out in (outs[0], outs[1], outs[3], outs[4]):
            out[-32:-16] = small_ref[...].astype(BF16)


def patch_fn(a_ref, up_ref, b_ref, down_ref, first_ref, second_ref):
    first_ref[...] = a_ref[...]
    first_ref[0:HALF] = (a_ref[0:HALF].astype(F32) + up_ref[...].astype(F32)).astype(BF16)
    second_ref[...] = b_ref[...]
    second_ref[HALF:] = (b_ref[HALF:].astype(F32) + down_ref[...].astype(F32)).astype(BF16)


def ends_fn(a_ref, b_ref, up_ref, down_ref):
    total = a_ref[0].astype(F32) + b_ref[0].astype(F32)
    up_ref[...] = total[:CUT].astype(BF16)
    down_ref[...] = total[CUT:].astype(BF16)


def lines_fn(a_ref, b_ref, c_ref, d_ref, lines_ref, small_ref):
    total = jnp.zeros((96, 2 * STATE), F32)
    for line, ref in enumerate((a_ref, b_ref, c_ref, d_ref)):
        lines_ref[line] = ref[0:96, 0:HP]
        total = total + ref[0:96, HP:].astype(F32)
        small_ref[line] = ref[96:]
    lines_ref[4, :, 0 : 2 * STATE] = total.astype(BF16)
    lines_ref[4, :, 2 * STATE :] = jnp.zeros((96, 128), BF16)


def final_grad_fn(at_ref, m_ref, g_ref, send_ref, keep_ref):
    low = mm(m_ref[...], g_ref[...], TN).astype(BF16)

    @pl.when(pl.program_id(0) < 2)
    def _():
        send_ref[...] = low

    @pl.when(pl.program_id(0) >= 2)
    def _():
        keep_ref[...] = low


def split_fn(parts, at_ref, *refs):
    blocks, outs, sum_ref = refs[:-5], refs[-5:-1], refs[-1]
    total = blocks[0][...].astype(F32)
    for block in blocks[1:]:
        total = total + block[...].astype(F32)
    sum_ref[...] = total.astype(BF16)
    for k, out in enumerate(outs):
        quarter = lax.rem(at_ref[0] + k, 4)
        to = 0
        for first, rows in parts:
            if rows:
                start = pl.multiple_of(first + rows * quarter, 16)
                out[to : to + rows] = sum_ref[pl.ds(start, rows)]
                to += rows
            else:
                out[to:] = sum_ref[first:]


def back_proj_fn(ax_ref, bx_ref, az_ref, bz_ref, wall_ref, a_ref, b_ref):
    dx = jnp.concatenate([ax_ref[0], bx_ref[0]], axis=0)
    dz = jnp.concatenate([az_ref[0], bz_ref[0]], axis=0)
    for r in range(4):
        at = slice(ROWS * r, ROWS * r + ROWS)
        part = mm(dx, wall_ref[at, 0:MIX], NT) + mm(dz, wall_ref[at, MIX:], NT)
        low = part.astype(BF16)
        a_ref[0, :, at] = low[:PAY]
        b_ref[0, :, at] = low[PAY:]


def finish_fn(at_ref, a_ref, b_ref, c_ref, d_ref, ahead_ref, tok_ref, cot_ref, gain_ref, out_ref):
    values = tok_ref[...].astype(F32)
    inv = lax.rsqrt(jnp.mean(values * values, axis=1, keepdims=True) + EPS)
    mean = jnp.zeros((LOCAL, 1), F32)
    spots = [pl.multiple_of(ROWS * lax.rem(at_ref[0] + r, 4), 128) for r in range(4)]
    for r, spot in enumerate(spots):
        at, to = slice(ROWS * r, ROWS * r + ROWS), pl.ds(spot, ROWS)
        total = a_ref[0:LOCAL, at].astype(F32) + b_ref[0:LOCAL, at].astype(F32)
        total = total + c_ref[0:LOCAL, at].astype(F32) + d_ref[0:LOCAL, at].astype(F32)
        last = jnp.concatenate([jnp.zeros((LOCAL - 8, ROWS), F32), ahead_ref[8:16, at].astype(F32)], axis=0)
        e1 = (total + last) * gain_ref[:, to]
        out_ref[:, to] = e1
        w = tok_ref[:, to].astype(F32) * inv
        mean = mean + jnp.sum(e1 * w, axis=1, keepdims=True)
    mean = mean / D
    for r in range(4):
        to = slice(ROWS * r, ROWS * r + ROWS)
        w = tok_ref[:, to].astype(F32) * inv
        out_ref[:, to] = cot_ref[:, to].astype(F32) + inv * (out_ref[:, to] - w * mean)


def layer_out_fn(out_ref, tok_ref, sums_ref, res_ref):
    pad = jnp.concatenate([sums_ref[0], jnp.zeros((120, LOCAL), F32)], axis=0).T
    factor = lax.rsqrt(pad[:, 0:1] / INNER + EPS)
    res_ref[...] = tok_ref[...].astype(F32) + factor * out_ref[...].astype(F32)


def place_early_fn(at_ref, mine_ref, sib_ref, out_ref, final_ref):
    def fill(refs):
        for c in range(2):
            for line in range(4):
                block = refs[c][0, lax.rem(at_ref[0] - line + 4, 4)].astype(F32)
                for a in range(2):
                    first = (2 * c + a) * 768 + 192 * line
                    out_ref[:, first : first + 192] = block[0:96, 192 * a : 192 * a + 192]
                    first = 768 * c + 384 * a
                    final_ref[line, :, first : first + 384] = block[96 + 48 * a : 144 + 48 * a]

    for mine, refs in ((0, (mine_ref, sib_ref)), (1, (sib_ref, mine_ref))):

        @pl.when(at_ref[1] == mine)
        def _(refs=refs):
            fill(refs)


def place_late_fn(at_ref, *refs):
    arrays, (out_ref, buf, sem) = refs[:8], refs[8:]
    y, core = at_ref[0], at_ref[1]
    step = pl.program_id(0)

    def fetch(number, slot):
        for k in range(4):

            @pl.when(number == k)
            def _(k=k):
                for i in range(2):
                    to = buf.at[slot, lax.rem(core + i, 2)]
                    pltpu.make_async_copy(arrays[4 * i + k], to, sem.at[slot, i]).start()

    slot = lax.rem(step, 2)

    @pl.when(step == 0)
    def _():
        fetch(step, slot)

    @pl.when(step < 3)
    def _():
        fetch(step + 1, 1 - slot)

    for i in range(2):
        pltpu.make_async_copy(arrays[0], buf.at[slot, i], sem.at[slot, i]).wait()
    for c in range(2):
        for line in range(4):
            block = buf[slot, c, lax.rem(y - line + 4, 4)].astype(F32)
            for a in range(2):
                first = (2 * c + a) * 768 + 192 * line
                out_ref[:, first : first + 192] = block[:, 192 * a : 192 * a + 192]
    total = buf[slot, 0, 4].astype(F32) + buf[slot, 1, 4].astype(F32)
    out_ref[:, INNER:] = total[:, 0 : 2 * STATE]


def place_small_fn(
    at_ref, own_ref, sib_ref, gain_ref,
    taps_ref, bias_ref, gating_ref, rates_ref, offset_ref, norm_ref, skip_ref, step_ref, buf_ref,
    line_ref, heads_ref,
):
    y, core = at_ref[0], at_ref[1]
    buf_ref[...] = jnp.zeros_like(buf_ref)
    taps = jnp.zeros((8, 2 * STATE), F32)
    norm = jnp.zeros((4, ROWS), F32)
    for mine, sets in ((0, (own_ref, sib_ref)), (1, (sib_ref, own_ref))):

        @pl.when(core == mine)
        def _(sets=sets):
            for c in range(2):
                for line in range(4):
                    rows = sets[c][lax.rem(y - line + 4, 4)].astype(F32)
                    for a in range(2):
                        at = (2 * c + a) * 768 + 192 * line
                        at = slice(at, at + 192)
                        part = rows[:, 192 * a : 192 * a + 192]
                        taps_ref[:, at] = part[4:8]
                        line_ref[0:2, at] = part[8:10]
                        at = 12 * (2 * c + a) + 3 * line
                        heads_ref[0:3, at : at + 3] = rows[10:13, 3 * a : 3 * a + 3]
                        buf_ref[at : at + 3] = rows[16 + 3 * a : 19 + 3 * a, 0:ROWS]

    for ref in (own_ref, sib_ref):
        for slot in range(4):
            rows = ref[slot].astype(F32)
            taps = taps + rows[4:12, HP:CH]
            norm = norm + rows[0:4, 0:ROWS]
    taps_ref[:, INNER:] = taps[0:4]
    line_ref[0:1, INNER:] = taps[4:5]
    norm = norm / gain_ref[...]
    for a in range(4):
        norm_ref[ROWS * a : ROWS * a + ROWS] = norm[a]
    bias_ref[...] = line_ref[0]
    gating_ref[...] = line_ref[1, 0:INNER]
    skip_ref[...] = heads_ref[2, 0:HEADS]
    rates_ref[...] = heads_ref[0, 0:HEADS]
    offset_ref[...] = heads_ref[1, 0:HEADS]
    step_ref[...] = buf_ref[0:HEADS]


def per_device(
    tokens,
    segments,
    cotangent,
    gate_proj,
    mixer_proj,
    step_proj,
    final_proj,
    norm_gain,
    conv_kernel,
    conv_bias,
    step_offset,
    log_rates,
    skip_gain,
    gating_gain,
):
    ctx = lax.axis_index("ctx")
    x = lax.axis_index("fsdp")
    y = lax.axis_index("y")
    core = lax.axis_index("core")
    turn = (x - 2 * core + 4) % 4

    def scalars(*values):
        return jnp.stack([jnp.asarray(v, jnp.int32) for v in values])

    z = ctx * 2 + lax.axis_index("low")
    flag, where = scalars(ctx), scalars(y, core)

    tokens = tokens.reshape(LOCAL, D)
    cot = cotangent.reshape(LOCAL, D)
    slab, final_rows = call(
        pack_kernel_fn,
        "pack",
        [
            (where, SMEM), (gate_proj, HBM), (mixer_proj, HBM), (final_proj, HBM),
            (step_proj.T, None),
        ],
        [((ROWS, WIDE), BF16, None), ((192, D), BF16, None)],
        steps=1,
        scratch=[
            pltpu.VMEM((5, ROWS, 256), BF16),
            pltpu.VMEM((ROWS, WIDE), F32),
            pltpu.VMEM((128, ROWS), F32),
            pltpu.SemaphoreType.DMA((6,)),
        ],
    )

    def first_hop(own, shift):
        return [own, shift(own, 1), shift(own, -1)]

    def far_hop(hop, shift, cut):
        own, below, above = hop
        ends = below[:cut], above[cut:]
        return ends, [own, below, shift(ends[0], 1), shift(ends[1], -1), above]

    slabs = first_hop(slab, x_shift)
    ahead = lax.ppermute(after(tokens, slab)[LOCAL - 16 :], "ctx", [(0, 1)])
    (payload,) = call(
        prep_kernel_fn,
        "prep",
        [
            (scalars(x, ctx), SMEM), (tokens, None), (ahead, None), (norm_gain[None], None),
            (segments, None),
        ],
        [((PAY, D), BF16, None)],
        steps=1,
        scratch=[pltpu.VMEM((PAY, D), BF16)],
    )
    mine = first_hop(payload, y_shift)
    par, hp, gain = call(
        params_kernel_fn,
        "params",
        [
            (where, SMEM), (conv_kernel, None), (conv_bias[None], None),
            (step_offset[None], None), (log_rates[None], None), (skip_gain[None], None),
            (gating_gain[None], None),
        ],
        [((8, CH), F32, None), ((8, 128), F32, None), ((8, HP), F32, None)],
        steps=1,
        wait=[payload],
    )
    _, slabs = far_hop(slabs, x_shift, 192)
    own_theirs = core_swap(payload)
    mine = list(after(tuple(mine), own_theirs, slabs[2], slabs[3]))
    cot_all = lax.all_gather(after(cot, mine[1], mine[2]), ("y", "core"), axis=0)

    def owner(r, c):
        return (2 * c + r) % 4

    def from_owners(steps):
        def to(ctx, x, y, low, core):
            r = (x - 2 * core) % 4
            return (ctx, owner(steps[r], core), y, low, core) if r in steps else None

        return to

    def token_outputs(place, count, spot):
        def at(shape):
            return (1,) + shape, lambda i: (place(i),) + (0,) * len(shape)

        outs = [
            ((PAY, D), BF16),
            ((PAY, CH), BF16),
            ((LOCAL, CH), BF16),
            ((LOCAL, STATE), BF16),
            ((LOCAL, 128), F32),
            ((LOCAL, HP), BF16),
            ((8, LOCAL), F32),
            ((LOCAL, HP), BF16),
        ]
        outs = [((GROUP,) + shape, dtype, at(shape)) for shape, dtype in outs]
        state = (1, HP, STATE), lambda i: (spot(i), 0, 0)
        return outs + [((count, HP, STATE), BF16, state)]

    base = [(flag, SMEM), (par, None), (hp, None)]
    scratch = [
        pltpu.VMEM((LOCAL, CH), BF16),
        pltpu.VMEM((2, PAY, D), BF16),
        pltpu.SemaphoreType.DMA((2,)),
    ]
    own, below, far_a, far_b, above = slabs
    wall, *kept = call(
        forward_first_fn,
        "forward_first",
        base
        + [(part, HBM) for part in (payload, own_theirs)]
        + [(part, HBM) for part in (own, above, far_a, far_b, below)],
        [((D, WIDE), BF16, None)] + token_outputs(lambda i: 4 * i, 6, lambda i: i),
        steps=2,
        scratch=scratch + [pltpu.SemaphoreType.DMA((5,))],
    )
    _, below, above = mine
    theirs = [core_swap(below), core_swap(above)]
    below, above, *theirs = after((below, above, *theirs), kept[-1])
    far = y_shift(below[:CUT], 1), y_shift(above[CUT:], -1)
    final_rows = after(final_rows, kept[-1])
    near = move(final_rows, from_owners({0: 1, 1: 0}))
    kept = call(
        forward_near_fn,
        "forward_near",
        base
        + [(wall, None)]
        + [(part, HBM) for part in [below, above, *theirs]]
        + [(part, HBM) for part in kept],
        token_outputs(lambda i: 4 * (i // 2) + 1 + 2 * (i % 2), 6, lambda i: 2 + i),
        steps=4,
        scratch=scratch,
        aliases={8 + i: i for i in range(9)},
    )
    *kept, state_a = kept
    state_in_a = lax.ppermute(state_a, "ctx", [(0, 1)])
    final_rows, *far = after((final_rows, *far), state_a)
    theirs = [core_swap(part) for part in far]
    far_rows = move(final_rows, from_owners({0: 3, 1: 2}))
    away = move(final_rows, from_owners({0: 2, 1: 3}))
    *kept, state_b = call(
        forward_far_fn,
        "forward_far",
        base
        + [(wall, None)]
        + [(part, HBM) for part in [*far, *theirs]]
        + [(part, HBM) for part in kept],
        token_outputs(lambda i: 4 * i + 2, 2, lambda i: i),
        steps=2,
        scratch=scratch,
        aliases={8 + i: i for i in range(8)},
    )
    nall, xbc, u, out_basis, small, gate, segs, y_local = kept
    state_in_b = lax.ppermute(state_b, "ctx", [(0, 1)])

    def state_blocks(first=0):
        def near_at(i, *s):
            line, core = (i + first) % 4, (i + first) // 4
            return (jnp.where(line == 0, core, 2 + 2 * core + line // 2), 0, 0)

        def far_at(i, *s):
            return ((i + first) // 4, 0, 0)

        return [(state_in_a, ((1, HP, STATE), near_at)), (state_in_b, ((1, HP, STATE), far_at))]

    rows = (GROUP, LOCAL, HP)
    wide = seq(LOCAL, HP)
    token = seq(LOCAL, 128)
    line = seq(8, LOCAL)
    dmix, w_final = call(
        dmix_kernel_fn,
        "d_mixed",
        [(cot_all, by_device(LOCAL, D, steps=4, first=k)) for k in range(4)]
        + [(part, HBM) for part in [final_rows, near, far_rows, away]],
        [(rows, BF16, ((4, LOCAL, HP), lambda i, at: (i, 0, 0))), ((HP, D), BF16, None)],
        steps=2,
        scratch=[pltpu.SemaphoreType.DMA((2,))],
        ahead=[scalars(y, core, turn)],
    )
    two = lambda *rest: ((2,) + rest, lambda i, *s: (i,) + (0,) * len(rest))
    pairs = two(LOCAL, HP)
    tokens_two = two(LOCAL, 128)
    y_all, gated, sums = call(
        gate_kernel_fn,
        "gate",
        [(flag, SMEM), (y_local, pairs), (state_in_a, None), (state_in_b, None), (gate, pairs)]
        + [(dmix, pairs), (out_basis, tokens_two), (small, tokens_two), (segs, two(8, LOCAL))]
        + [(gain, None)],
        [(rows, BF16, pairs), (rows, BF16, pairs), ((GROUP, 8, LOCAL), F32, two(8, LOCAL))],
        steps=4,
        scratch=[pltpu.VMEM((LOCAL, HP), F32)],
    )

    (out,) = call(
        product_kernel_fn,
        "out_proj",
        [(where, SMEM), (gated, ((4, LOCAL, HP), lambda i: (i, 0, 0))), (w_final, None)],
        [((GROUP, LOCAL, D), BF16, HBM)],
        steps=2,
        scratch=[pltpu.VMEM((2, 4, LOCAL, D), BF16), pltpu.SemaphoreType.DMA((2, 4))],
    )
    swapped = core_swap(sums)
    sums = sums + jnp.concatenate([swapped[4:], swapped[:4]], axis=0)
    shifted = [y_shift(sums, steps) for steps in (1, 2, 3)]
    shifted = after(tuple(shifted), out)
    total = sums
    for steps, got in zip((1, 2, 3), shifted, strict=True):
        got = got.reshape(2, 4, 8, LOCAL)
        got = jnp.concatenate([got[:, 4 - steps :], got[:, : 4 - steps]], axis=1)
        total = total + got.reshape(GROUP, 8, LOCAL)
    out = lax.psum_scatter(out, ("y", "core"), scatter_dimension=0, tiled=True)
    mixed, dy, dz, dstate, dgain = call(
        ungate_kernel_fn,
        "ungate",
        [(where, SMEM), (flag, SMEM), (y_all, pairs), (gate, pairs), (dmix, pairs)]
        + [(total, two(8, LOCAL)), (out_basis, tokens_two), (small, tokens_two)]
        + [(segs, two(8, LOCAL)), (gain, None)],
        [
            (rows, BF16, HBM),
            (rows, BF16, pairs),
            ((GROUP, PAY, HP), BF16, two(PAY, HP)),
            ((GROUP, HP, STATE), BF16, two(HP, STATE)),
            ((8, HP), F32, None),
        ],
        steps=4,
        scratch=[pltpu.VMEM((2, 2, LOCAL, HP), BF16), pltpu.SemaphoreType.DMA((2, 2))],
    )
    dstate_in = lax.ppermute(dstate, "ctx", [(1, 0)])

    mixed_rows = mixed.reshape(GROUP * LOCAL, HP)

    half = lambda i, at: (0, 2 * ((at[1] + 1 + i // 2) % 2) + i % 2)
    final_send, final_kept = call(
        final_grad_fn,
        "grad_final",
        [
            (mixed_rows, None),
            (cot_all.reshape(GROUP * LOCAL, D), ((GROUP * LOCAL, ROWS), half)),
        ],
        [
            ((HP, 768), BF16, ((HP, ROWS), lambda i, at: (0, jnp.minimum(i, 1)))),
            ((HP, 768), BF16, ((HP, ROWS), lambda i, at: (0, jnp.maximum(i - 2, 0)))),
        ],
        steps=4,
        ahead=[where],
    )
    final_got = core_swap(final_send)

    normed_rows = nall.reshape(GROUP * PAY, D)

    def grad_inputs(grads):
        return [
            (scalars(x, core), SMEM),
            (normed_rows, ((GROUP * PAY, ROWS), lambda i, *s: (0, i))),
            (grads, None),
            (wall, ((ROWS, WIDE), lambda i, *s: (i, 0))),
        ]

    def over_x(blocks):
        own, ahead, far, behind = blocks
        return own, x_shift(far, 2), x_shift(ahead, 1), x_shift(behind, -1)

    def over_z(blocks, parts, rows, wait=()):
        shape = blocks[0].shape
        quarters = call(
            functools.partial(split_fn, parts),
            "split",
            [(scalars(z), SMEM)] + [(block, None) for block in blocks],
            [((rows, shape[1]), BF16, None)] * 4,
            steps=1,
            scratch=[pltpu.VMEM(shape, BF16)],
            wait=wait,
        )
        return quarters, [quarters[0]] + [z_shift(quarters[k], k) for k in (2, 1, 3)]

    def over_y(piece):
        return [piece] + [y_shift(piece, s) for s in (1, 2, 3)]

    def gathered(lines):
        own, small = call(
            lines_fn,
            "lines",
            [(line, None) for line in lines],
            [((5, 96, HP), BF16, None), ((4, 32, CH), BF16, None)],
            steps=1,
        )
        mine = [own] + [z_shift(own, k) for k in (2, 1, 3)]
        mine = [mine[0], mine[2], mine[1], mine[3]]
        return (small, core_swap(small)), mine

    *early, norm_gate = call(
        early_grad_fn,
        "grad_gate",
        grad_inputs(dz.reshape(GROUP * PAY, HP)) + [(final_kept, None), (final_got, None)],
        [((2 * ROWS, HP), BF16, None)] * 4 + [((8, HP), F32, None)],
        steps=4,
    )
    early_block = early[0]
    early = over_x(early)

    sums = [jnp.zeros((8, HP), F32), jnp.zeros((8, CH), F32), jnp.zeros((8, 128), F32)]
    dx, dskip, dpar, dhead = call(
        back_kernel_fn,
        "back",
        [
            (flag, SMEM), (dy, wide), (u, seq(LOCAL, CH)), (xbc, seq(PAY, CH)), (small, token),
            (segs, line), (par, None), (hp, None),
        ]
        + state_blocks()
        + [(dstate_in, seq(HP, STATE))]
        + [(value, None) for value in sums],
        [
            ((GROUP, PAY, MIX), BF16, seq(PAY, MIX)),
            ((8, HP), F32, None),
            ((8, CH), F32, None),
            ((8, 128), F32, None),
        ],
        scratch=[
            pltpu.VMEM((128, LOCAL), F32),
            pltpu.VMEM((LOCAL, CH), F32),
            pltpu.VMEM((LOCAL, 128), F32),
            pltpu.VMEM((LOCAL, 128), F32),
            pltpu.VMEM((LOCAL, CH), BF16),
            pltpu.VMEM((LOCAL, CH), F32),
        ],
        wait=[early_block],
    )
    quarters, early = over_z(after(tuple(early), dpar), ((0, 192),), 192)

    def back_projected(first, count, wait):
        mine = lambda i: (first + 2 * i, 0, 0)
        theirs = lambda i: (4 + first + 2 * i, 0, 0)
        block, out = (1, PAY, MIX), ((1, PAY, D), lambda i: (i, 0, 0))
        a, b = call(
            back_proj_fn,
            "back_proj",
            [
                (dx, (block, mine)), (dx, (block, theirs)),
                (dz, ((1, PAY, HP), mine)), (dz, ((1, PAY, HP), theirs)), (wall, None),
            ],
            [((count, PAY, D), BF16, out)] * 2,
            steps=count,
            wait=wait,
        )
        return a, b

    far_mine, far_theirs = back_projected(2, 1, [*quarters[1:], out])
    piece = add(*after(tuple(early), far_mine))
    early = over_y(piece)
    far_theirs = core_swap(far_theirs)
    blocks = call(
        late_grad_fn,
        "grad_mixer",
        grad_inputs(dx.reshape(GROUP * PAY, MIX))
        + [(value, None) for value in (norm_gate, dpar, dgain, dskip, dhead)],
        [((rows, CH), BF16, None) for rows in (ROWS + 32, ROWS + 32, HALF, HALF, ROWS + 32)],
        steps=4,
        wait=[far_mine, piece],
        scratch=[pltpu.VMEM((16, CH), F32)],
    )
    stack = jnp.stack(after(tuple(early), blocks[0]))
    early = lax.all_gather(stack, ("ctx", "low"), axis=0)

    far_mine, far_theirs = after((far_mine, far_theirs), blocks[0])
    ends = call(
        ends_fn,
        "ends",
        [(far_mine, None), (far_theirs, None)],
        [((CUT, D), BF16, None), ((PAY - CUT, D), BF16, None)],
        steps=1,
    )
    x_up, x_down = x_shift(blocks[2], 1), x_shift(blocks[3], -1)
    up, down = y_shift(ends[0], 1), y_shift(ends[1], -1)
    own_mine, own_theirs = back_projected(0, 1, [*ends, stack])
    x_up, x_down, up, down = after((x_up, x_down, up, down), own_mine)
    own_theirs = core_swap(after(own_theirs, x_up, x_down, up, down))
    ends = call(
        patch_fn,
        "patch",
        [(blocks[1], None), (x_up, None), (blocks[4], None), (x_down, None)],
        [((ROWS + 32, CH), BF16, None)] * 2,
        steps=1,
    )
    late = blocks[0], x_shift(ends[0], 1), x_shift(ends[1], -1)
    mine, theirs = back_projected(1, 2, [*ends, up, down, own_theirs])
    late = after(tuple(late), mine)
    theirs = core_swap(after(theirs, *late))
    quarters, late = over_z(late, ((0, 96), (ROWS, 0)), 128)
    (layer_out,) = call(
        layer_out_fn,
        "layer_out",
        [(out[0], None), (tokens, None), (total, ((1, 8, LOCAL), lambda i: (0, 0, 0)))],
        [((LOCAL, D), F32, None)],
        steps=1,
        wait=[quarters[1]],
    )
    mine, theirs, up, down = after((mine, theirs, up, down), quarters[1])
    tail = jnp.zeros((PAY - CUT, D), BF16)
    above = add(mine[1], theirs[1], jnp.concatenate([up, tail], axis=0))
    head = jnp.zeros((CUT, D), BF16)
    below = add(mine[0], theirs[0], jnp.concatenate([head, down], axis=0))
    back_got = y_shift(above, 1), y_shift(below, -1)
    piece = add(*after(tuple(late), layer_out, above, below))
    late = over_y(piece)
    early = after(early, *late[1:], *back_got)
    parts = [value.reshape(PAY, D) for value in (own_mine, own_theirs)] + list(back_got)
    ahead = add(*[part[LOCAL:] for part in parts])
    ahead = lax.ppermute(ahead, "ctx", [(1, 0)])
    rest, late = gathered(after(tuple(late), ahead))
    (grad_tokens,) = call(
        finish_fn,
        "finish",
        [(scalars(x), SMEM)]
        + [(part, None) for part in [*parts, ahead, tokens, cot, norm_gain[None]]],
        [((LOCAL, D), F32, None)],
        steps=1,
    )

    quarter = ((1, 4, 192, HP), lambda i: (i, 0, 0, 0))
    grad_gate, grad_final = call(
        place_early_fn,
        "place_early",
        [(where, SMEM), (early, quarter), (core_swap(early), quarter)],
        [
            ((ROWS, INNER), F32, ((96, INNER), lambda i: (i, 0))),
            ((4, 192, D), F32, ((4, 48, D), lambda i: (0, i, 0))),
        ],
        steps=4,
        wait=[rest[1]],
    )
    taps, bias, gating, rates, offset, norm, skip, grad_step = call(
        place_small_fn,
        "place_small",
        [(where, SMEM), (rest[0], None), (rest[1], None), (norm_gain.reshape(4, ROWS), None)],
        [((4, CONV_CH), F32, None)]
        + [((n,), F32, None) for n in (CONV_CH, INNER, HEADS, HEADS, D, HEADS)]
        + [((HEADS, ROWS), F32, None)],
        steps=1,
        scratch=[
            pltpu.VMEM((128, ROWS), F32),
            pltpu.VMEM((8, CONV_CH), F32),
            pltpu.VMEM((8, 128), F32),
        ],
    )
    late = list(after(tuple(late), grad_gate, taps, grad_tokens))
    late = late + [core_swap(part) for part in late]
    (grad_mixer,) = call(
        place_late_fn,
        "place_late",
        [(value, HBM) for value in late],
        [((ROWS, CONV_CH), F32, ((96, CONV_CH), lambda i, at: ((at[2] - i + 4) % 4, 0)))],
        steps=4,
        scratch=[pltpu.VMEM((2, 2, 5, 96, HP), BF16), pltpu.SemaphoreType.DMA((2, 2))],
        ahead=[scalars(y, core, z)],
    )
    shape = (1, LOCAL, D)
    return (
        layer_out.reshape(shape),
        grad_tokens.reshape(shape),
        grad_gate,
        grad_mixer,
        grad_step.T,
        grad_final.reshape(2 * 384, D),
        norm,
        taps,
        bias,
        offset,
        rates,
        skip,
        gating,
    )


def solution(mesh):
    apart = jax.sharding.Mesh(mesh.devices.reshape(2, 4, 4, 2, 2), AXES)
    batch = ("fsdp", "y", "low", "core")
    tokens = P(batch, "ctx", None)
    rows = P("fsdp", None)
    return jax.shard_map(
        per_device,
        mesh=apart,
        in_specs=(tokens, P(batch, None), tokens, rows, rows, rows, rows) + (P(),) * 7,
        out_specs=(tokens, tokens, rows, rows, rows, rows) + (P(),) * 7,
        check_vma=False,
    )
```

```python
import functools

import jax
import jax.numpy as jnp
from jax import lax
from jax.experimental import pallas as pl
from jax.experimental.pallas import tpu as pltpu
from jax.sharding import PartitionSpec as P

D = 1536
INNER = 3072
STATE = 128
HEADS = 48
HEAD_DIM = 64
CONV_CH = 3328
LOCAL = 256
GROUP = 8
OWN = 6
HP = OWN * HEAD_DIM
CH = HP + 2 * STATE
ROWS = D // 4
EPS = 1e-05
AXES = ("ctx", "fsdp", "y", "low", "core")
F32 = jnp.float32
BF16 = jnp.bfloat16
HIGH = lax.Precision.HIGHEST
MASKED = -1e30
PAY = LOCAL + 16
CUT = 144
WIDE = CH + 128 + HP
HALF = 208
MIX = CH + 128
SCALE = 1.0
DURATION = {
    "pack": 4, "prep": 3, "params": 2, "forward_first": 10, "forward_near": 18, "forward_far": 10, "d_mixed": 7, "gate": 7,
    "out_proj": 7, "ungate": 8, "grad_final": 0.1, "grad_gate": 0.1, "back": 38, "grad_mixer": 13,
    "back_proj": 6, "split": 3, "patch": 2, "ends": 1, "finish": 3, "layer_out": 2, "lines": 2, "place_early": 7, "place_late": 6, "place_small": 2,
}
VMEM_LIMIT = 63 * 1024 * 1024


def place_of(ctx, x, y, low, core):
    return (ctx * 4 + x) * 16 + (y * 2 + low) * 2 + core


def pairs_of(move):
    pairs = []
    for ctx in range(2):
        for x in range(4):
            for y in range(4):
                for low in range(2):
                    for core in range(2):
                        to = move(ctx, x, y, low, core)
                        if to is not None:
                            pairs.append((place_of(ctx, x, y, low, core), place_of(*to)))
    return pairs


def move(value, to):
    return lax.ppermute(value, AXES, pairs_of(to))


def x_shift(value, steps):
    return lax.ppermute(value, "fsdp", [(i, (i + steps) % 4) for i in range(4)])


def y_shift(value, steps):
    return lax.ppermute(value, "y", [(i, (i + steps) % 4) for i in range(4)])


def core_swap(value):
    return lax.ppermute(value, "core", [(0, 1), (1, 0)])


def z_shift(value, steps):
    def to(ctx, x, y, low, core):
        z = (2 * ctx + low + steps) % 4
        return (z // 2, x, y, z % 2, core)

    return move(value, to)


def after(value, *others):
    return lax.optimization_barrier((value,) + others)[0]


def add(*values):
    total = values[0].astype(F32)
    for value in values[1:]:
        total = total + value.astype(F32)
    return total.astype(BF16)


def mm(a, b, dims, precision=None):
    return lax.dot_general(a, b, (dims, ((), ())), precision=precision, preferred_element_type=F32)


NN = ((1,), (0,))
NT = ((1,), (1,))
TN = ((0,), (0,))
SMEM = object()
HBM = object()


def call(fn, name, inputs, outputs, steps=GROUP, scratch=(), aliases=None, ahead=(), wait=()):
    us = DURATION[name] * SCALE
    first = len(ahead) + len(inputs)
    inputs = inputs + [(value, HBM) for value in wait]

    def kernel(*refs):
        fn(*refs[:first], *refs[first + len(wait) :])

    def block(shape, how):
        if how is SMEM:
            return pl.BlockSpec(memory_space=pltpu.SMEM)
        if how is HBM:
            return pl.BlockSpec(memory_space=pl.ANY)
        if how is None:
            return pl.BlockSpec(tuple(shape), lambda i, *s: (0,) * len(shape))
        return pl.BlockSpec(*how)

    return pl.pallas_call(
        kernel,
        name=name,
        grid_spec=pltpu.PrefetchScalarGridSpec(
            num_scalar_prefetch=len(ahead),
            grid=(steps,),
            in_specs=[block(value.shape, how) for value, how in inputs],
            out_specs=[block(shape, how) for shape, _, how in outputs],
            scratch_shapes=list(scratch),
        ),
        out_shape=[jax.ShapeDtypeStruct(shape, dtype) for shape, dtype, _ in outputs],
        input_output_aliases=aliases or {},
        cost_estimate=pl.CostEstimate(
            flops=int(us * 1.15e9), bytes_accessed=int(us * 3.6e6), transcendentals=0
        ),
        compiler_params=pltpu.CompilerParams(
            dimension_semantics=("arbitrary",), vmem_limit_bytes=VMEM_LIMIT
        ),
    )(*ahead, *[value for value, _ in inputs])


def seq(*rest, first=0, low=0, high=GROUP):
    def at(i, *s):
        return (jnp.clip(i + first, low, high - 1) - low,) + (0,) * len(rest)

    return ((1,) + rest, at)


def by_device(*rest, steps=1, first=0):
    def at(i, at):
        i = i * steps + first
        y, core = (at[0] + 4 - i % 4) % 4, (at[1] + i // 4) % 2
        return (2 * y + core,) + (0,) * len(rest)

    return ((1,) + rest, at)


def lane_ids(rows, cols):
    return lax.broadcasted_iota(jnp.int32, (rows, cols), 1)


def pair(values, p, left):
    return jnp.where(left, values[:, 2 * p : 2 * p + 1], values[:, 2 * p + 1 : 2 * p + 2])


def small_parts(small):
    mine = lane_ids(LOCAL, 128) < OWN
    parts = small, pltpu.roll(small, 120, 1), pltpu.roll(small, 112, 1)
    return [jnp.where(mine, part, 0.0) for part in parts]


def summed_rows(values, dims):
    lane = lane_ids(LOCAL, 128)
    high = values.astype(BF16).astype(F32)
    rest = values - high
    middle = rest.astype(BF16).astype(F32)
    parts = jnp.where(lane < 8, high, jnp.where(lane < 16, middle, rest - middle))
    got = mm(triangle().astype(BF16), parts.astype(BF16), dims)
    return got + pltpu.roll(got, 120, 1) + pltpu.roll(got, 112, 1)


def head_sums(values, p):
    lane, row = lane_ids(128, 128), lax.broadcasted_iota(jnp.int32, (128, 128), 0)
    ones = jnp.where(lane == 2 * p + row // HEAD_DIM, 1.0, 0.0).astype(BF16)
    return mm(values.astype(BF16), ones, NN)


def triangle():
    row = lax.broadcasted_iota(jnp.int32, (LOCAL, LOCAL), 0)
    col = lax.broadcasted_iota(jnp.int32, (LOCAL, LOCAL), 1)
    return row >= col


def seg_columns(row):
    return jnp.broadcast_to(row, (128, LOCAL)).T


def same_before(seg, k):
    return jnp.concatenate([seg[:k], seg[: LOCAL - k]], axis=0) == seg


def mask_bias(seg, row):
    wide = jnp.concatenate([seg, seg], axis=1)
    return jnp.where((wide == row) & triangle(), 0.0, MASKED)


def prep_kernel_fn(at_ref, tok_ref, ahead_ref, gain_ref, seg_ref, out_ref, buf_ref):
    def normed(values):
        values = values.astype(F32)
        inv = lax.rsqrt(jnp.mean(values * values, axis=1, keepdims=True) + EPS)
        return (values * inv * gain_ref[...]).astype(BF16)

    buf_ref[0:LOCAL] = normed(tok_ref[...])
    seg = seg_ref[...].astype(F32)
    seg = jnp.where(at_ref[1] == 0, seg[:, :LOCAL], seg[:, LOCAL:])
    part = jnp.concatenate([seg, jnp.zeros((1, ROWS - LOCAL), F32)], axis=1)
    row = jnp.concatenate([part] * 4, axis=1)
    number = lax.broadcasted_iota(jnp.int32, (16, D), 0)
    extra = jnp.where(number >= 8, normed(ahead_ref[...]).astype(F32), 0.0)
    buf_ref[LOCAL:PAY] = jnp.where(number == 0, row, extra).astype(BF16)
    for r in range(4):
        start = pl.multiple_of(ROWS * lax.rem(at_ref[0] + r, 4), 128)
        out_ref[:, ROWS * r : ROWS * r + ROWS] = buf_ref[:, pl.ds(start, ROWS)]


def pack_kernel_fn(
    at_ref, gate_ref, mixer_ref, final_ref, step_ref,
    slab_ref, rows_ref, buf_ref, wide_ref, turn_ref, sem,
):
    y, core = at_ref[0], at_ref[1]
    copies = []
    for i, src in enumerate((mixer_ref, gate_ref)):
        for a in range(2):
            first = (2 * core + a) * 768 + 384 * lax.div(y, 2) + 128 * lax.rem(y, 2)
            where = pl.ds(pl.multiple_of(first, 128), 256)
            copies.append((src.at[:, where], buf_ref.at[2 * i + a]))
    copies.append((mixer_ref.at[:, pl.ds(INNER, 2 * STATE)], buf_ref.at[4]))
    copies.append((final_ref.at[pl.ds(pl.multiple_of(192 * y, 64), 192)], rows_ref))
    copies = [pltpu.make_async_copy(a, b, sem.at[i]) for i, (a, b) in enumerate(copies)]
    for copy in copies:
        copy.start()
    turn_ref[...] = jnp.zeros_like(turn_ref)
    step = step_ref[...].astype(F32)
    for line in range(4):
        for c in range(2):

            @pl.when((y == line) & (core == c))
            def _(line=line, c=c):
                for a in range(2):
                    at = 12 * (2 * c + a) + 3 * line
                    for to in range(3 * a, 24, 8):
                        turn_ref[to : to + 3] = step[at : at + 3]

    wide_ref[:, CH:MIX] = turn_ref[...].T
    for copy in copies:
        copy.wait()
    for odd in range(2):

        @pl.when(lax.rem(y, 2) == odd)
        def _(odd=odd):
            for i, base in enumerate((0, MIX)):
                for a in range(2):
                    block = buf_ref[2 * i + a].astype(F32)
                    to = base + 192 * a
                    wide_ref[:, to : to + 192] = block[:, 64 * odd : 64 * odd + 192]

    slab_ref[...] = wide_ref[...].astype(BF16)
    slab_ref[:, HP:CH] = buf_ref[4]


def params_kernel_fn(
    at_ref, taps_ref, bias_ref, offset_ref, rates_ref, skip_ref, gating_ref,
    par_ref, hp_ref, gain_ref,
):
    par_ref[...] = jnp.zeros_like(par_ref)
    hp_ref[...] = jnp.zeros_like(hp_ref)
    for line in range(4):
        for c in range(2):

            @pl.when((at_ref[0] == line) & (at_ref[1] == c))
            def _(line=line, c=c):
                for a in range(2):
                    at = slice((2 * c + a) * 768 + 192 * line, (2 * c + a) * 768 + 192 * line + 192)
                    to = slice(192 * a, 192 * a + 192)
                    par_ref[0:4, to] = taps_ref[:, at]
                    par_ref[4:5, to] = bias_ref[:, at]
                    gain_ref[0:1, to] = gating_ref[:, at]
                    at = slice(12 * (2 * c + a) + 3 * line, 12 * (2 * c + a) + 3 * line + 3)
                    for first in range(3 * a, 24, 8):
                        to = slice(first, first + 3)
                        hp_ref[0:1, to] = offset_ref[:, at]
                        hp_ref[1:2, to] = -jnp.exp(rates_ref[:, at])
                        hp_ref[2:3, to] = skip_ref[:, at]

    par_ref[0:4, HP:] = taps_ref[:, INNER:]
    par_ref[4:5, HP:] = bias_ref[:, INNER:]


class Pieces:
    def __init__(self, parts, buf, sem):
        self.parts, self.buf, self.sem = parts, buf, sem

    def fetch(self, step, slot):
        for k, refs in enumerate(self.parts):

            @pl.when(step == k)
            def _(refs=refs):
                first = 0
                for ref in refs:
                    to = self.buf.at[slot, first : first + ref.shape[0]]
                    pltpu.make_async_copy(ref, to, self.sem.at[slot]).start()
                    first += ref.shape[0]

    def next(self):
        step = pl.program_id(0)
        slot = lax.rem(step, 2)

        @pl.when(step == 0)
        def _():
            self.fetch(step, slot)

        @pl.when(step < len(self.parts) - 1)
        def _():
            self.fetch(step + 1, 1 - slot)

        pltpu.make_async_copy(self.buf.at[slot], self.buf.at[slot], self.sem.at[slot]).wait()
        return slot


def forward_body(
    ctx_ref, par_ref, hp_ref, n, wall_ref,
    nall_ref, xbc_ref, u_ref, out_ref, small_ref, z_ref, seg_ref, y_ref, state_ref, xc_ref,
):
    par = par_ref[...]
    hp = hp_ref[...]
    nall_ref[0] = n
    row = n[LOCAL:PAY, 0:LOCAL].astype(F32)[0:1]
    seg_ref[0] = jnp.broadcast_to(row, (8, LOCAL))
    seg = seg_columns(row)
    keeps = [same_before(seg, k) for k in range(1, 4)]
    z_ref[0] = mm(n[0:LOCAL], wall_ref[:, MIX:], NN).astype(BF16)
    for j in range(3):
        prod = mm(n, wall_ref[:, 256 * j : 256 * j + 256], NN)
        for half in range(2):
            first = 256 * j + 128 * half
            at = slice(first, first + 128)
            x = prod[:, 128 * half : 128 * half + 128]
            if first == CH:
                raw = x[0:LOCAL] + hp[0:1]
                continue
            low = x.astype(BF16)
            xbc_ref[0, :, at] = low
            x = low.astype(F32)
            ext = jnp.concatenate([x[LOCAL + 8 :], x[:LOCAL]], axis=0)
            u = par[4:5, at] + par[0:1, at] * x[:LOCAL]
            for k in range(1, 4):
                moved = ext[8 - k : 8 - k + LOCAL]
                u = u + par[k : k + 1, at] * jnp.where(keeps[k - 1], moved, 0.0)
            u_ref[0, :, at] = u.astype(BF16)
            xc_ref[:, at] = (u * jax.nn.sigmoid(u)).astype(BF16)
    dt = jnp.maximum(raw, 0.0) + jnp.log1p(jnp.exp(-jnp.abs(raw)))
    cum = summed_rows(dt * hp[1:2], NN)
    lane = lane_ids(LOCAL, 128)
    small_ref[0] = jnp.where(lane < 8, dt, jnp.where(lane < 16, pltpu.roll(cum, 8, 1), raw))
    left = lane < HEAD_DIM
    left1 = lane_ids(1, 128) < HEAD_DIM
    basis, out_basis = xc_ref[:, HP : HP + STATE], xc_ref[:, HP + STATE :]
    out_ref[0] = out_basis

    @pl.when(ctx_ref[0] == 0)
    def _():
        tail = jnp.where(seg == seg[LOCAL - 1 :], jnp.exp(cum[LOCAL - 1 :] - cum) * dt, 0.0)
        for p in range(3):
            at = slice(128 * p, 128 * p + 128)
            part = xc_ref[:, at].astype(F32) * pair(tail, p, left)
            state_ref[0, at] = mm(part.astype(BF16), basis, TN).astype(BF16)

    @pl.when(ctx_ref[0] != 0)
    def _():
        state_ref[0] = jnp.zeros((HP, STATE), BF16)

    cum_t = cum.T
    scores = mm(out_basis, basis, NT)
    bias = mask_bias(seg, row)
    for p in range(3):
        at = slice(128 * p, 128 * p + 128)
        x = xc_ref[:, at].astype(F32)
        scaled = (x * pair(dt, p, left)).astype(BF16)
        halves = []
        for h in (2 * p, 2 * p + 1):
            mix = jnp.exp(cum[:, h : h + 1] - cum_t[h : h + 1] + bias) * scores
            halves.append(mm(mix.astype(BF16), scaled, NN))
        y = jnp.where(left, halves[0], halves[1]) + pair(hp[2:3], p, left1) * x
        y_ref[0, :, at] = y.astype(BF16)


def forward_first_fn(ctx_ref, par_ref, hp_ref, mine, theirs, *refs):
    slabs, wall_ref, outs, (xc, buf, sem, wsem) = refs[:5], refs[5], refs[6:15], refs[15:]
    copies = []
    first = 0
    for i, ref in enumerate(slabs):
        rows = ref.shape[0]
        copies.append(pltpu.make_async_copy(ref, wall_ref.at[first : first + rows], wsem.at[i]))
        first += rows

    @pl.when(pl.program_id(0) == 0)
    def _():
        for copy in copies:
            copy.start()

    slot = Pieces([[mine], [theirs]], buf, sem).next()

    @pl.when(pl.program_id(0) == 0)
    def _():
        for copy in copies:
            copy.wait()

    forward_body(ctx_ref, par_ref, hp_ref, buf[slot], wall_ref, *outs, xc)


def forward_near_fn(ctx_ref, par_ref, hp_ref, wall_ref, *refs):
    parts, outs, (xc, buf, sem) = refs[:4], refs[13:22], refs[22:]
    slot = Pieces([[part] for part in parts], buf, sem).next()
    forward_body(ctx_ref, par_ref, hp_ref, buf[slot], wall_ref, *outs, xc)


def forward_far_fn(ctx_ref, par_ref, hp_ref, wall_ref, *refs):
    parts, outs, (xc, buf, sem) = refs[:4], refs[12:21], refs[21:]
    slot = Pieces([parts[:2], parts[2:]], buf, sem).next()
    forward_body(ctx_ref, par_ref, hp_ref, buf[slot], wall_ref, *outs, xc)


def dmix_kernel_fn(at_ref, *refs):
    g_refs, (own, near, far, away, dmix_ref, wf_ref, sem) = refs[:4], refs[4:]
    step = pl.program_id(0)
    up, down = wf_ref.at[0:192], wf_ref.at[192:HP]

    @pl.when(step == 0)
    def _():
        for r, (a, b) in enumerate(((own, near), (near, own), (away, far), (far, away))):

            @pl.when(at_ref[2] == r)
            def _(a=a, b=b):
                pltpu.make_async_copy(a, up, sem.at[0]).start()
                pltpu.make_async_copy(b, down, sem.at[1]).start()

        pltpu.make_async_copy(own, up, sem.at[0]).wait()
        pltpu.make_async_copy(own, down, sem.at[1]).wait()

    for k, ref in enumerate(g_refs):
        dmix_ref[k] = mm(ref[0], wf_ref[...], NT).astype(BF16)


def entered(k, ctx_ref, state_a_ref, state_b_ref, small_ref, seg_ref, use):
    @pl.when(ctx_ref[0] != 0)
    def _():
        number = 2 * pl.program_id(0) + k
        line, core = lax.rem(number, 4), lax.div(number, 4)
        near = jnp.where(line == 0, core, 2 + 2 * core + lax.div(line, 2))
        seg = seg_columns(seg_ref[k, 0:1])
        enter = jnp.where(seg == seg[0:1], jnp.exp(small_parts(small_ref[k])[1]), 0.0)
        left = lane_ids(LOCAL, 128) < HEAD_DIM
        for p in range(3):
            at = slice(128 * p, 128 * p + 128)
            state = jnp.where(line == 2, state_b_ref[core, at], state_a_ref[near, at])
            use(at, pair(enter, p, left), state)


def gate_kernel_fn(
    ctx_ref, y_ref, state_a_ref, state_b_ref, z_ref, dmix_ref, basis_ref, small_ref, seg_ref,
    gain_ref, yall_ref, low_ref, sums_ref, sum_ref,
):
    for k in range(2):
        sum_ref[...] = y_ref[k].astype(F32)

        def use(at, gate, state, k=k):
            sum_ref[:, at] += gate * mm(basis_ref[k], state, NT)

        entered(k, ctx_ref, state_a_ref, state_b_ref, small_ref, seg_ref, use)
        y = sum_ref[...]
        yall_ref[k] = y.astype(BF16)
        z = z_ref[k].astype(F32)
        gated = y * (z * jax.nn.sigmoid(z))
        raised = gated * gain_ref[0:1]
        low_ref[k] = raised.astype(BF16)
        first = jnp.sum(gated * gated, axis=1, keepdims=True)
        second = jnp.sum(dmix_ref[k].astype(F32) * raised, axis=1, keepdims=True)
        lane = lane_ids(LOCAL, 128)
        both = jnp.where(lane == 0, first, jnp.where(lane == 1, second, 0.0))
        sums_ref[k] = both.T[0:8]


def product_kernel_fn(at_ref, a_ref, w_ref, out_ref, buf, sem):
    step = pl.program_id(0)

    def copies(number):
        found = []
        for k in range(4):
            place = 2 * lax.rem(at_ref[0] + 4 - k, 4) + lax.rem(at_ref[1] + number, 2)
            found.append(pltpu.make_async_copy(buf.at[number, k], out_ref.at[place], sem.at[number, k]))
        return found

    for number in range(2):

        @pl.when(step == number)
        def _(number=number):
            for k, copy in enumerate(copies(number)):
                buf[number, k] = mm(a_ref[k], w_ref[...], NN).astype(BF16)
                copy.start()

    @pl.when(step == 1)
    def _():
        for number in range(2):
            for copy in copies(number):
                copy.wait()


def ungate_kernel_fn(
    at_ref, ctx_ref, y_ref, z_ref, dmix_ref, sums_ref, basis_ref, small_ref, seg_ref, gain_ref,
    mixed_ref, dy_ref, dz_ref, dstate_ref, dgain_ref, buf, sem,
):
    step = pl.program_id(0)
    slot = lax.rem(step, 2)

    def copy(number, k):
        place = 2 * lax.rem(at_ref[0] + 8 - 2 * number - k, 4)
        place = place + lax.rem(at_ref[1] + lax.div(number, 2), 2)
        spot = lax.rem(number, 2)
        return pltpu.make_async_copy(buf.at[spot, k], mixed_ref.at[place], sem.at[spot, k])

    @pl.when(step == 0)
    def _():
        dgain_ref[...] = jnp.zeros_like(dgain_ref)

    @pl.when(step >= 2)
    def _():
        for k in range(2):
            copy(step - 2, k).wait()

    gain = gain_ref[0:1]
    for k in range(2):
        pad = jnp.concatenate([sums_ref[k], jnp.zeros((120, LOCAL), F32)], axis=0).T
        inv = lax.rsqrt(pad[:, 0:1] / INNER + EPS)
        mean_ev = inv * pad[:, 1:2] / INNER
        y = y_ref[k].astype(F32)
        z = z_ref[k].astype(F32)
        dmix = dmix_ref[k].astype(F32)
        sig = jax.nn.sigmoid(z)
        act = z * sig
        v = y * act * inv
        buf[slot, k] = (v * gain).astype(BF16)
        copy(step, k).start()
        d_gated = inv * (dmix * gain - v * mean_ev)
        dy = (d_gated * act).astype(BF16)
        dy_ref[k] = dy
        dz_ref[k, 0:LOCAL] = (d_gated * y * sig * (1.0 + z * (1.0 - sig))).astype(BF16)
        dz_ref[k, LOCAL:PAY] = jnp.zeros((16, HP), BF16)
        dgain_ref[0:1] += jnp.sum(dmix * v, axis=0, keepdims=True)

        @pl.when(ctx_ref[0] != 0)
        def _(k=k, dy=dy):
            seg = seg_columns(seg_ref[k, 0:1])
            enter = jnp.where(seg == seg[0:1], jnp.exp(small_parts(small_ref[k])[1]), 0.0)
            left = lane_ids(LOCAL, 128) < HEAD_DIM
            for p in range(3):
                at = slice(128 * p, 128 * p + 128)
                part = (dy[:, at].astype(F32) * pair(enter, p, left)).astype(BF16)
                dstate_ref[k, at] = mm(part, basis_ref[k], TN).astype(BF16)

        @pl.when(ctx_ref[0] == 0)
        def _(k=k):
            dstate_ref[k] = jnp.zeros((HP, STATE), BF16)

    @pl.when(step == 3)
    def _():
        for number in (2, 3):
            for k in range(2):
                copy(number, k).wait()


def back_kernel_fn(
    ctx_ref, dy_ref, u_ref, xbc_ref, small_ref, seg_ref, par_ref, hp_ref, state_a_ref, state_b_ref,
    dstate_ref, skip0_ref, par0_ref, head0_ref,
    dx_ref, dskip_ref, dpar_ref, dhead_ref, turn_ref, dxc_ref, dc_ref, dd_ref, xc_ref, slope_ref,
):
    step = pl.program_id(0)
    hp = hp_ref[...]
    par = par_ref[...]
    dt, cum, raw = small_parts(small_ref[0])
    cum_t = cum.T
    for j in range(5):
        at = slice(128 * j, 128 * j + 128)
        u = u_ref[0, :, at].astype(F32)
        sig = jax.nn.sigmoid(u)
        xc_ref[:, at] = (u * sig).astype(BF16)
        slope_ref[:, at] = sig * (1.0 + u * (1.0 - sig))
    basis, out_basis = xc_ref[:, HP : HP + STATE], xc_ref[:, HP + STATE :]
    scores = mm(basis, out_basis, NT)
    row = seg_ref[0, 0:1]
    seg = seg_columns(row)
    same = jnp.concatenate([seg, seg], axis=1) == row
    first = lax.broadcasted_iota(jnp.int32, (LOCAL, LOCAL), 0)
    bias = jnp.where(same & (first <= lane_ids(LOCAL, LOCAL)), 0.0, MASKED)
    lane = lane_ids(LOCAL, 128)
    left = lane < HEAD_DIM
    left1 = lane_ids(1, 128) < HEAD_DIM

    @pl.when(step == 0)
    def _():
        dskip_ref[...] = skip0_ref[...]
        dpar_ref[...] = par0_ref[...]
        dhead_ref[...] = head0_ref[...]
        turn_ref[...] = jnp.zeros_like(turn_ref)

    d_scores = jnp.zeros((LOCAL, LOCAL), F32)
    sums = jnp.zeros((LOCAL, 128), F32)
    for p in range(3):
        at = slice(128 * p, 128 * p + 128)
        x = xc_ref[:, at].astype(F32)
        g = dy_ref[0, :, at]
        steps = pair(dt, p, left)
        scaled = (x * steps).astype(BF16)
        halves = []
        for h in (2 * p, 2 * p + 1):
            mine = left if h % 2 == 0 else ~left
            prod = mm(scaled, jnp.where(mine, g, jnp.zeros_like(g)), NT)
            mix = jnp.exp(cum_t[h : h + 1] - cum[:, h : h + 1] + bias)
            weighed = mix * prod
            d_scores = d_scores + weighed
            pulled = weighed * scores
            turn_ref[h : h + 1] = jnp.sum(pulled, axis=0, keepdims=True)
            folded = pulled[:, :128] + pulled[:, 128:]
            high = folded.astype(BF16)
            rest = (folded - high.astype(F32)).astype(BF16)
            ones = jnp.where(lane == h, 1.0, 0.0).astype(BF16)
            sums = sums + mm(jnp.concatenate([high, rest], axis=1), ones, NN)
            halves.append(mm((mix * scores).astype(BF16), g, NN))
        gf = g.astype(F32)
        skip = pair(hp[2:3], p, left1)
        dxc_ref[:, at] = steps * jnp.where(left, halves[0], halves[1]) + skip * gf
        dskip_ref[0:1, at] += jnp.sum(gf * x, axis=0, keepdims=True)
    dd_ref[...] = jnp.where(dt > 1e-37, sums / jnp.maximum(dt, 1e-37), 0.0)
    dc_ref[...] = turn_ref[...].T - sums
    low = d_scores.astype(BF16)
    dxc_ref[:, HP : HP + STATE] = mm(low, out_basis, NN)
    dxc_ref[:, HP + STATE :] = mm(low, basis, TN)

    @pl.when(ctx_ref[0] != 0)
    def _():
        enter = jnp.where(seg == seg[0:1], jnp.exp(cum), 0.0)
        d_out = jnp.zeros((LOCAL, STATE), F32)
        extra = jnp.zeros((LOCAL, 128), F32)
        for p in range(3):
            at = slice(128 * p, 128 * p + 128)
            state = jnp.where(lax.rem(step, 4) == 2, state_b_ref[0, at], state_a_ref[0, at])
            scaled = dy_ref[0, :, at].astype(F32) * pair(enter, p, left)
            d_out = d_out + mm(scaled.astype(BF16), state, NN)
            extra = extra + head_sums(scaled * mm(out_basis, state, NT), p)
        dxc_ref[:, HP + STATE :] += d_out
        dc_ref[...] += extra

    @pl.when(ctx_ref[0] == 0)
    def _():
        tail = jnp.where(seg == seg[LOCAL - 1 :], jnp.exp(cum[LOCAL - 1 :] - cum), 0.0)
        weight = tail * dt
        d_basis = jnp.zeros((LOCAL, STATE), F32)
        d_weight = jnp.zeros((LOCAL, 128), F32)
        for p in range(3):
            at = slice(128 * p, 128 * p + 128)
            x = xc_ref[:, at].astype(F32)
            w = pair(weight, p, left)
            ds = dstate_ref[0, at]
            seen = mm(basis, ds, NT)
            dxc_ref[:, at] += w * seen
            d_basis = d_basis + mm((x * w).astype(BF16), ds, NN)
            d_weight = d_weight + head_sums(x * seen, p)
        dxc_ref[:, HP : HP + STATE] += d_basis
        dd_ref[...] += tail * d_weight
        moved = weight * d_weight
        dc_ref[...] -= moved
        dc_ref[LOCAL - 1 : LOCAL] += jnp.sum(moved, axis=0, keepdims=True)

    dc = jnp.where(lane < OWN, dc_ref[...], 0.0)
    dc = dc + pltpu.roll(dc, 8, 1) + pltpu.roll(dc, 16, 1)
    d_decay = summed_rows(dc, TN)
    rate = hp[1:2]
    d_raw = (dd_ref[...] + d_decay * rate) * jax.nn.sigmoid(raw)
    d_raw = jnp.where(lane < OWN, d_raw, 0.0)
    dhead_ref[0:1] += jnp.sum(d_decay * dt, axis=0, keepdims=True) * rate
    dhead_ref[1:2] += jnp.sum(d_raw, axis=0, keepdims=True)
    dx_ref[0, 0:LOCAL, CH:MIX] = d_raw.astype(BF16)
    dx_ref[0, LOCAL:PAY, CH:MIX] = jnp.zeros((16, 128), BF16)

    keeps = [same_before(seg, k) for k in range(1, 4)]
    zeros = jnp.zeros((8, 128), F32)
    for j in range(5):
        at = slice(128 * j, 128 * j + 128)
        x = xbc_ref[0, :, at].astype(F32)
        ext = jnp.concatenate([x[LOCAL + 8 :], x[:LOCAL]], axis=0)
        du = dxc_ref[:, at] * slope_ref[:, at]
        dpar_ref[4:5, at] += jnp.sum(du, axis=0, keepdims=True)
        dpar_ref[0:1, at] += jnp.sum(du * x[:LOCAL], axis=0, keepdims=True)
        total = par[0:1, at] * du
        before = zeros
        for k in range(1, 4):
            kept = jnp.where(keeps[k - 1], du, 0.0)
            moved = ext[8 - k : 8 - k + LOCAL]
            dpar_ref[k : k + 1, at] += jnp.sum(kept * moved, axis=0, keepdims=True)
            back = jnp.concatenate([zeros, kept * par[k : k + 1, at], zeros], axis=0)
            total = total + back[8 + k : 8 + k + LOCAL]
            before = before + back[k : k + 8]
        dx_ref[0, 0:LOCAL, at] = total.astype(BF16)
        dx_ref[0, LOCAL:PAY, at] = jnp.concatenate([zeros, before], axis=0).astype(BF16)


def norm_row(grad, weight):
    column = jnp.sum(grad * weight.astype(F32), axis=1, keepdims=True)
    return jnp.broadcast_to(column, (ROWS, 128)).T[0:1]


def early_grad_fn(at_ref, n_ref, d_ref, wall_ref, keep_ref, got_ref, *refs):
    step = pl.program_id(0)
    outs, norm_ref = refs[:4], refs[4]
    grad = mm(n_ref[...], d_ref[...], TN)

    @pl.when(step == 0)
    def _():
        norm_ref[...] = jnp.zeros_like(norm_ref)

    norm_ref[pl.ds(step, 1)] = norm_row(grad, wall_ref[:, MIX:])
    low = grad.astype(BF16)
    owner = lax.rem(at_ref[0] + step, 4)
    for r in range(4):
        for mine, src in ((True, keep_ref), (False, got_ref)):

            @pl.when((step == r) & ((lax.div(owner, 2) == at_ref[1]) == mine))
            def _(src=src, out=outs[r]):
                for q in range(4):
                    first = pl.multiple_of(192 * lax.rem(owner, 2) + 48 * q, 16)
                    out[192 * q : 192 * q + 96] = low[96 * q : 96 * q + 96]
                    out[192 * q + 96 : 192 * q + 144] = src[pl.ds(first, 48), 0:ROWS]
                    out[192 * q + 144 : 192 * q + 192] = src[pl.ds(first, 48), ROWS:]


def late_grad_fn(
    at_ref, n_ref, d_ref, wall_ref, norm_ref, par_ref, gain_ref, skip_ref, head_ref, *refs
):
    step = pl.program_id(0)
    outs, small_ref = refs[:5], refs[5]
    grad = mm(n_ref[...], d_ref[...], TN)
    rows = grad[:, CH:].T[0:16].astype(BF16)
    low = grad[:, 0:CH].astype(BF16)

    @pl.when(step == 0)
    def _():
        small_ref[...] = jnp.zeros_like(small_ref)
        small_ref[4:9] = par_ref[0:5]
        small_ref[9:10, 0:HP] = gain_ref[0:1]
        small_ref[10:12, 0:128] = head_ref[0:2]
        lane = lane_ids(1, 128)
        skip = jnp.zeros((1, 128), F32)
        for h in range(OWN):
            part = skip_ref[0:1, HEAD_DIM * h : HEAD_DIM * h + HEAD_DIM]
            skip = jnp.where(lane == h, jnp.sum(part, axis=1, keepdims=True), skip)
        small_ref[12:13, 0:128] = skip

    owner = lax.rem(at_ref[0] + step, 4)
    row = norm_row(grad, wall_ref[:, 0:MIX]) + norm_ref[pl.ds(step, 1)]
    small_ref[pl.ds(owner, 1), 0:ROWS] = row
    for r, out in enumerate((outs[0], outs[1], outs[3], outs[4])):

        @pl.when(step == (0, 1, 2, 3)[r])
        def _(out=out, r=r):
            if r == 2:
                outs[2][...] = low[0:HALF]
                out[0 : ROWS - HALF] = low[HALF:]
            else:
                out[0:ROWS] = low
            out[-16:, 0:ROWS] = rows
            out[-16:, ROWS:] = jnp.zeros((16, CH - ROWS), BF16)

    @pl.when(step == 3)
    def _():
        for out in (outs[0], outs[1], outs[3], outs[4]):
            out[-32:-16] = small_ref[...].astype(BF16)


def patch_fn(a_ref, up_ref, b_ref, down_ref, first_ref, second_ref):
    first_ref[...] = a_ref[...]
    first_ref[0:HALF] = (a_ref[0:HALF].astype(F32) + up_ref[...].astype(F32)).astype(BF16)
    second_ref[...] = b_ref[...]
    second_ref[HALF:] = (b_ref[HALF:].astype(F32) + down_ref[...].astype(F32)).astype(BF16)


def ends_fn(a_ref, b_ref, up_ref, down_ref):
    total = a_ref[0].astype(F32) + b_ref[0].astype(F32)
    up_ref[...] = total[:CUT].astype(BF16)
    down_ref[...] = total[CUT:].astype(BF16)


def lines_fn(a_ref, b_ref, c_ref, d_ref, lines_ref, small_ref):
    total = jnp.zeros((96, 2 * STATE), F32)
    for line, ref in enumerate((a_ref, b_ref, c_ref, d_ref)):
        lines_ref[line] = ref[0:96, 0:HP]
        total = total + ref[0:96, HP:].astype(F32)
        small_ref[line] = ref[96:]
    lines_ref[4, :, 0 : 2 * STATE] = total.astype(BF16)
    lines_ref[4, :, 2 * STATE :] = jnp.zeros((96, 128), BF16)


def final_grad_fn(at_ref, m_ref, g_ref, send_ref, keep_ref):
    low = mm(m_ref[...], g_ref[...], TN).astype(BF16)

    @pl.when(pl.program_id(0) < 2)
    def _():
        send_ref[...] = low

    @pl.when(pl.program_id(0) >= 2)
    def _():
        keep_ref[...] = low


def split_fn(parts, at_ref, *refs):
    blocks, outs, sum_ref = refs[:-5], refs[-5:-1], refs[-1]
    total = blocks[0][...].astype(F32)
    for block in blocks[1:]:
        total = total + block[...].astype(F32)
    sum_ref[...] = total.astype(BF16)
    for k, out in enumerate(outs):
        quarter = lax.rem(at_ref[0] + k, 4)
        to = 0
        for first, rows in parts:
            if rows:
                start = pl.multiple_of(first + rows * quarter, 16)
                out[to : to + rows] = sum_ref[pl.ds(start, rows)]
                to += rows
            else:
                out[to:] = sum_ref[first:]


def back_proj_fn(ax_ref, bx_ref, az_ref, bz_ref, wall_ref, a_ref, b_ref):
    dx = jnp.concatenate([ax_ref[0], bx_ref[0]], axis=0)
    dz = jnp.concatenate([az_ref[0], bz_ref[0]], axis=0)
    for r in range(4):
        at = slice(ROWS * r, ROWS * r + ROWS)
        part = mm(dx, wall_ref[at, 0:MIX], NT) + mm(dz, wall_ref[at, MIX:], NT)
        low = part.astype(BF16)
        a_ref[0, :, at] = low[:PAY]
        b_ref[0, :, at] = low[PAY:]


def finish_fn(at_ref, a_ref, b_ref, c_ref, d_ref, ahead_ref, tok_ref, cot_ref, gain_ref, out_ref):
    values = tok_ref[...].astype(F32)
    inv = lax.rsqrt(jnp.mean(values * values, axis=1, keepdims=True) + EPS)
    mean = jnp.zeros((LOCAL, 1), F32)
    spots = [pl.multiple_of(ROWS * lax.rem(at_ref[0] + r, 4), 128) for r in range(4)]
    for r, spot in enumerate(spots):
        at, to = slice(ROWS * r, ROWS * r + ROWS), pl.ds(spot, ROWS)
        total = a_ref[0:LOCAL, at].astype(F32) + b_ref[0:LOCAL, at].astype(F32)
        total = total + c_ref[0:LOCAL, at].astype(F32) + d_ref[0:LOCAL, at].astype(F32)
        last = jnp.concatenate([jnp.zeros((LOCAL - 8, ROWS), F32), ahead_ref[8:16, at].astype(F32)], axis=0)
        e1 = (total + last) * gain_ref[:, to]
        out_ref[:, to] = e1
        w = tok_ref[:, to].astype(F32) * inv
        mean = mean + jnp.sum(e1 * w, axis=1, keepdims=True)
    mean = mean / D
    for r in range(4):
        to = slice(ROWS * r, ROWS * r + ROWS)
        w = tok_ref[:, to].astype(F32) * inv
        out_ref[:, to] = cot_ref[:, to].astype(F32) + inv * (out_ref[:, to] - w * mean)


def layer_out_fn(out_ref, tok_ref, sums_ref, res_ref):
    pad = jnp.concatenate([sums_ref[0], jnp.zeros((120, LOCAL), F32)], axis=0).T
    factor = lax.rsqrt(pad[:, 0:1] / INNER + EPS)
    res_ref[...] = tok_ref[...].astype(F32) + factor * out_ref[...].astype(F32)


def place_early_fn(at_ref, mine_ref, sib_ref, out_ref, final_ref):
    def fill(refs):
        for c in range(2):
            for line in range(4):
                block = refs[c][0, lax.rem(at_ref[0] - line + 4, 4)].astype(F32)
                for a in range(2):
                    first = (2 * c + a) * 768 + 192 * line
                    out_ref[:, first : first + 192] = block[0:96, 192 * a : 192 * a + 192]
                    first = 768 * c + 384 * a
                    final_ref[line, :, first : first + 384] = block[96 + 48 * a : 144 + 48 * a]

    for mine, refs in ((0, (mine_ref, sib_ref)), (1, (sib_ref, mine_ref))):

        @pl.when(at_ref[1] == mine)
        def _(refs=refs):
            fill(refs)


def place_late_fn(at_ref, *refs):
    arrays, (out_ref, buf, sem) = refs[:8], refs[8:]
    y, core = at_ref[0], at_ref[1]
    step = pl.program_id(0)

    def fetch(number, slot):
        for k in range(4):

            @pl.when(number == k)
            def _(k=k):
                for i in range(2):
                    to = buf.at[slot, lax.rem(core + i, 2)]
                    pltpu.make_async_copy(arrays[4 * i + k], to, sem.at[slot, i]).start()

    slot = lax.rem(step, 2)

    @pl.when(step == 0)
    def _():
        fetch(step, slot)

    @pl.when(step < 3)
    def _():
        fetch(step + 1, 1 - slot)

    for i in range(2):
        pltpu.make_async_copy(arrays[0], buf.at[slot, i], sem.at[slot, i]).wait()
    for c in range(2):
        for line in range(4):
            block = buf[slot, c, lax.rem(y - line + 4, 4)].astype(F32)
            for a in range(2):
                first = (2 * c + a) * 768 + 192 * line
                out_ref[:, first : first + 192] = block[:, 192 * a : 192 * a + 192]
    total = buf[slot, 0, 4].astype(F32) + buf[slot, 1, 4].astype(F32)
    out_ref[:, INNER:] = total[:, 0 : 2 * STATE]


def place_small_fn(
    at_ref, own_ref, sib_ref, gain_ref,
    taps_ref, bias_ref, gating_ref, rates_ref, offset_ref, norm_ref, skip_ref, step_ref, buf_ref,
    line_ref, heads_ref,
):
    y, core = at_ref[0], at_ref[1]
    buf_ref[...] = jnp.zeros_like(buf_ref)
    taps = jnp.zeros((8, 2 * STATE), F32)
    norm = jnp.zeros((4, ROWS), F32)
    for mine, sets in ((0, (own_ref, sib_ref)), (1, (sib_ref, own_ref))):

        @pl.when(core == mine)
        def _(sets=sets):
            for c in range(2):
                for line in range(4):
                    rows = sets[c][lax.rem(y - line + 4, 4)].astype(F32)
                    for a in range(2):
                        at = (2 * c + a) * 768 + 192 * line
                        at = slice(at, at + 192)
                        part = rows[:, 192 * a : 192 * a + 192]
                        taps_ref[:, at] = part[4:8]
                        line_ref[0:2, at] = part[8:10]
                        at = 12 * (2 * c + a) + 3 * line
                        heads_ref[0:3, at : at + 3] = rows[10:13, 3 * a : 3 * a + 3]
                        buf_ref[at : at + 3] = rows[16 + 3 * a : 19 + 3 * a, 0:ROWS]

    for ref in (own_ref, sib_ref):
        for slot in range(4):
            rows = ref[slot].astype(F32)
            taps = taps + rows[4:12, HP:CH]
            norm = norm + rows[0:4, 0:ROWS]
    taps_ref[:, INNER:] = taps[0:4]
    line_ref[0:1, INNER:] = taps[4:5]
    norm = norm / gain_ref[...]
    for a in range(4):
        norm_ref[ROWS * a : ROWS * a + ROWS] = norm[a]
    bias_ref[...] = line_ref[0]
    gating_ref[...] = line_ref[1, 0:INNER]
    skip_ref[...] = heads_ref[2, 0:HEADS]
    rates_ref[...] = heads_ref[0, 0:HEADS]
    offset_ref[...] = heads_ref[1, 0:HEADS]
    step_ref[...] = buf_ref[0:HEADS]


def per_device(
    tokens,
    segments,
    cotangent,
    gate_proj,
    mixer_proj,
    step_proj,
    final_proj,
    norm_gain,
    conv_kernel,
    conv_bias,
    step_offset,
    log_rates,
    skip_gain,
    gating_gain,
):
    ctx = lax.axis_index("ctx")
    x = lax.axis_index("fsdp")
    y = lax.axis_index("y")
    core = lax.axis_index("core")
    turn = (x - 2 * core + 4) % 4

    def scalars(*values):
        return jnp.stack([jnp.asarray(v, jnp.int32) for v in values])

    z = ctx * 2 + lax.axis_index("low")
    flag, where = scalars(ctx), scalars(y, core)

    tokens = tokens.reshape(LOCAL, D)
    cot = cotangent.reshape(LOCAL, D)
    slab, final_rows = call(
        pack_kernel_fn,
        "pack",
        [
            (where, SMEM), (gate_proj, HBM), (mixer_proj, HBM), (final_proj, HBM),
            (step_proj.T, None),
        ],
        [((ROWS, WIDE), BF16, None), ((192, D), BF16, None)],
        steps=1,
        scratch=[
            pltpu.VMEM((5, ROWS, 256), BF16),
            pltpu.VMEM((ROWS, WIDE), F32),
            pltpu.VMEM((128, ROWS), F32),
            pltpu.SemaphoreType.DMA((6,)),
        ],
    )

    def first_hop(own, shift):
        return [own, shift(own, 1), shift(own, -1)]

    def far_hop(hop, shift, cut):
        own, below, above = hop
        ends = below[:cut], above[cut:]
        return ends, [own, below, shift(ends[0], 1), shift(ends[1], -1), above]

    slabs = first_hop(slab, x_shift)
    ahead = lax.ppermute(after(tokens, slab)[LOCAL - 16 :], "ctx", [(0, 1)])
    (payload,) = call(
        prep_kernel_fn,
        "prep",
        [
            (scalars(x, ctx), SMEM), (tokens, None), (ahead, None), (norm_gain[None], None),
            (segments, None),
        ],
        [((PAY, D), BF16, None)],
        steps=1,
        scratch=[pltpu.VMEM((PAY, D), BF16)],
    )
    mine = first_hop(payload, y_shift)
    par, hp, gain = call(
        params_kernel_fn,
        "params",
        [
            (where, SMEM), (conv_kernel, None), (conv_bias[None], None),
            (step_offset[None], None), (log_rates[None], None), (skip_gain[None], None),
            (gating_gain[None], None),
        ],
        [((8, CH), F32, None), ((8, 128), F32, None), ((8, HP), F32, None)],
        steps=1,
        wait=[payload],
    )
    _, slabs = far_hop(slabs, x_shift, 192)
    own_theirs = core_swap(payload)
    mine = list(after(tuple(mine), own_theirs, slabs[2], slabs[3]))
    cot_all = lax.all_gather(after(cot, mine[1], mine[2]), ("y", "core"), axis=0)

    def owner(r, c):
        return (2 * c + r) % 4

    def from_owners(steps):
        def to(ctx, x, y, low, core):
            r = (x - 2 * core) % 4
            return (ctx, owner(steps[r], core), y, low, core) if r in steps else None

        return to

    def token_outputs(place, count, spot):
        def at(shape):
            return (1,) + shape, lambda i: (place(i),) + (0,) * len(shape)

        outs = [
            ((PAY, D), BF16),
            ((PAY, CH), BF16),
            ((LOCAL, CH), BF16),
            ((LOCAL, STATE), BF16),
            ((LOCAL, 128), F32),
            ((LOCAL, HP), BF16),
            ((8, LOCAL), F32),
            ((LOCAL, HP), BF16),
        ]
        outs = [((GROUP,) + shape, dtype, at(shape)) for shape, dtype in outs]
        state = (1, HP, STATE), lambda i: (spot(i), 0, 0)
        return outs + [((count, HP, STATE), BF16, state)]

    base = [(flag, SMEM), (par, None), (hp, None)]
    scratch = [
        pltpu.VMEM((LOCAL, CH), BF16),
        pltpu.VMEM((2, PAY, D), BF16),
        pltpu.SemaphoreType.DMA((2,)),
    ]
    own, below, far_a, far_b, above = slabs
    wall, *kept = call(
        forward_first_fn,
        "forward_first",
        base
        + [(part, HBM) for part in (payload, own_theirs)]
        + [(part, HBM) for part in (own, above, far_a, far_b, below)],
        [((D, WIDE), BF16, None)] + token_outputs(lambda i: 4 * i, 6, lambda i: i),
        steps=2,
        scratch=scratch + [pltpu.SemaphoreType.DMA((5,))],
    )
    _, below, above = mine
    theirs = [core_swap(below), core_swap(above)]
    below, above, *theirs = after((below, above, *theirs), kept[-1])
    far = y_shift(below[:CUT], 1), y_shift(above[CUT:], -1)
    final_rows = after(final_rows, kept[-1])
    near = move(final_rows, from_owners({0: 1, 1: 0}))
    kept = call(
        forward_near_fn,
        "forward_near",
        base
        + [(wall, None)]
        + [(part, HBM) for part in [below, above, *theirs]]
        + [(part, HBM) for part in kept],
        token_outputs(lambda i: 4 * (i // 2) + 1 + 2 * (i % 2), 6, lambda i: 2 + i),
        steps=4,
        scratch=scratch,
        aliases={8 + i: i for i in range(9)},
    )
    *kept, state_a = kept
    state_in_a = lax.ppermute(state_a, "ctx", [(0, 1)])
    final_rows, *far = after((final_rows, *far), state_a)
    theirs = [core_swap(part) for part in far]
    far_rows = move(final_rows, from_owners({0: 3, 1: 2}))
    away = move(final_rows, from_owners({0: 2, 1: 3}))
    *kept, state_b = call(
        forward_far_fn,
        "forward_far",
        base
        + [(wall, None)]
        + [(part, HBM) for part in [*far, *theirs]]
        + [(part, HBM) for part in kept],
        token_outputs(lambda i: 4 * i + 2, 2, lambda i: i),
        steps=2,
        scratch=scratch,
        aliases={8 + i: i for i in range(8)},
    )
    nall, xbc, u, out_basis, small, gate, segs, y_local = kept
    state_in_b = lax.ppermute(state_b, "ctx", [(0, 1)])

    def state_blocks(first=0):
        def near_at(i, *s):
            line, core = (i + first) % 4, (i + first) // 4
            return (jnp.where(line == 0, core, 2 + 2 * core + line // 2), 0, 0)

        def far_at(i, *s):
            return ((i + first) // 4, 0, 0)

        return [(state_in_a, ((1, HP, STATE), near_at)), (state_in_b, ((1, HP, STATE), far_at))]

    rows = (GROUP, LOCAL, HP)
    wide = seq(LOCAL, HP)
    token = seq(LOCAL, 128)
    line = seq(8, LOCAL)
    dmix, w_final = call(
        dmix_kernel_fn,
        "d_mixed",
        [(cot_all, by_device(LOCAL, D, steps=4, first=k)) for k in range(4)]
        + [(part, HBM) for part in [final_rows, near, far_rows, away]],
        [(rows, BF16, ((4, LOCAL, HP), lambda i, at: (i, 0, 0))), ((HP, D), BF16, None)],
        steps=2,
        scratch=[pltpu.SemaphoreType.DMA((2,))],
        ahead=[scalars(y, core, turn)],
    )
    two = lambda *rest: ((2,) + rest, lambda i, *s: (i,) + (0,) * len(rest))
    pairs = two(LOCAL, HP)
    tokens_two = two(LOCAL, 128)
    y_all, gated, sums = call(
        gate_kernel_fn,
        "gate",
        [(flag, SMEM), (y_local, pairs), (state_in_a, None), (state_in_b, None), (gate, pairs)]
        + [(dmix, pairs), (out_basis, tokens_two), (small, tokens_two), (segs, two(8, LOCAL))]
        + [(gain, None)],
        [(rows, BF16, pairs), (rows, BF16, pairs), ((GROUP, 8, LOCAL), F32, two(8, LOCAL))],
        steps=4,
        scratch=[pltpu.VMEM((LOCAL, HP), F32)],
    )

    (out,) = call(
        product_kernel_fn,
        "out_proj",
        [(where, SMEM), (gated, ((4, LOCAL, HP), lambda i: (i, 0, 0))), (w_final, None)],
        [((GROUP, LOCAL, D), BF16, HBM)],
        steps=2,
        scratch=[pltpu.VMEM((2, 4, LOCAL, D), BF16), pltpu.SemaphoreType.DMA((2, 4))],
    )
    swapped = core_swap(sums)
    sums = sums + jnp.concatenate([swapped[4:], swapped[:4]], axis=0)
    shifted = [y_shift(sums, steps) for steps in (1, 2, 3)]
    shifted = after(tuple(shifted), out)
    total = sums
    for steps, got in zip((1, 2, 3), shifted, strict=True):
        got = got.reshape(2, 4, 8, LOCAL)
        got = jnp.concatenate([got[:, 4 - steps :], got[:, : 4 - steps]], axis=1)
        total = total + got.reshape(GROUP, 8, LOCAL)
    out = lax.psum_scatter(out, ("y", "core"), scatter_dimension=0, tiled=True)
    mixed, dy, dz, dstate, dgain = call(
        ungate_kernel_fn,
        "ungate",
        [(where, SMEM), (flag, SMEM), (y_all, pairs), (gate, pairs), (dmix, pairs)]
        + [(total, two(8, LOCAL)), (out_basis, tokens_two), (small, tokens_two)]
        + [(segs, two(8, LOCAL)), (gain, None)],
        [
            (rows, BF16, HBM),
            (rows, BF16, pairs),
            ((GROUP, PAY, HP), BF16, two(PAY, HP)),
            ((GROUP, HP, STATE), BF16, two(HP, STATE)),
            ((8, HP), F32, None),
        ],
        steps=4,
        scratch=[pltpu.VMEM((2, 2, LOCAL, HP), BF16), pltpu.SemaphoreType.DMA((2, 2))],
    )
    dstate_in = lax.ppermute(dstate, "ctx", [(1, 0)])

    mixed_rows = mixed.reshape(GROUP * LOCAL, HP)

    half = lambda i, at: (0, 2 * ((at[1] + 1 + i // 2) % 2) + i % 2)
    final_send, final_kept = call(
        final_grad_fn,
        "grad_final",
        [
            (mixed_rows, None),
            (cot_all.reshape(GROUP * LOCAL, D), ((GROUP * LOCAL, ROWS), half)),
        ],
        [
            ((HP, 768), BF16, ((HP, ROWS), lambda i, at: (0, jnp.minimum(i, 1)))),
            ((HP, 768), BF16, ((HP, ROWS), lambda i, at: (0, jnp.maximum(i - 2, 0)))),
        ],
        steps=4,
        ahead=[where],
    )
    final_got = core_swap(final_send)

    normed_rows = nall.reshape(GROUP * PAY, D)

    def grad_inputs(grads):
        return [
            (scalars(x, core), SMEM),
            (normed_rows, ((GROUP * PAY, ROWS), lambda i, *s: (0, i))),
            (grads, None),
            (wall, ((ROWS, WIDE), lambda i, *s: (i, 0))),
        ]

    def over_x(blocks):
        own, ahead, far, behind = blocks
        return own, x_shift(far, 2), x_shift(ahead, 1), x_shift(behind, -1)

    def over_z(blocks, parts, rows, wait=()):
        shape = blocks[0].shape
        quarters = call(
            functools.partial(split_fn, parts),
            "split",
            [(scalars(z), SMEM)] + [(block, None) for block in blocks],
            [((rows, shape[1]), BF16, None)] * 4,
            steps=1,
            scratch=[pltpu.VMEM(shape, BF16)],
            wait=wait,
        )
        return quarters, [quarters[0]] + [z_shift(quarters[k], k) for k in (2, 1, 3)]

    def over_y(piece):
        return [piece] + [y_shift(piece, s) for s in (1, 2, 3)]

    def gathered(lines):
        own, small = call(
            lines_fn,
            "lines",
            [(line, None) for line in lines],
            [((5, 96, HP), BF16, None), ((4, 32, CH), BF16, None)],
            steps=1,
        )
        mine = [own] + [z_shift(own, k) for k in (2, 1, 3)]
        mine = [mine[0], mine[2], mine[1], mine[3]]
        return (small, core_swap(small)), mine

    *early, norm_gate = call(
        early_grad_fn,
        "grad_gate",
        grad_inputs(dz.reshape(GROUP * PAY, HP)) + [(final_kept, None), (final_got, None)],
        [((2 * ROWS, HP), BF16, None)] * 4 + [((8, HP), F32, None)],
        steps=4,
    )
    early_block = early[0]
    early = over_x(early)

    sums = [jnp.zeros((8, HP), F32), jnp.zeros((8, CH), F32), jnp.zeros((8, 128), F32)]
    dx, dskip, dpar, dhead = call(
        back_kernel_fn,
        "back",
        [
            (flag, SMEM), (dy, wide), (u, seq(LOCAL, CH)), (xbc, seq(PAY, CH)), (small, token),
            (segs, line), (par, None), (hp, None),
        ]
        + state_blocks()
        + [(dstate_in, seq(HP, STATE))]
        + [(value, None) for value in sums],
        [
            ((GROUP, PAY, MIX), BF16, seq(PAY, MIX)),
            ((8, HP), F32, None),
            ((8, CH), F32, None),
            ((8, 128), F32, None),
        ],
        scratch=[
            pltpu.VMEM((128, LOCAL), F32),
            pltpu.VMEM((LOCAL, CH), F32),
            pltpu.VMEM((LOCAL, 128), F32),
            pltpu.VMEM((LOCAL, 128), F32),
            pltpu.VMEM((LOCAL, CH), BF16),
            pltpu.VMEM((LOCAL, CH), F32),
        ],
        wait=[early_block],
    )
    quarters, early = over_z(after(tuple(early), dpar), ((0, 192),), 192)

    def back_projected(first, count, wait):
        mine = lambda i: (first + 2 * i, 0, 0)
        theirs = lambda i: (4 + first + 2 * i, 0, 0)
        block, out = (1, PAY, MIX), ((1, PAY, D), lambda i: (i, 0, 0))
        a, b = call(
            back_proj_fn,
            "back_proj",
            [
                (dx, (block, mine)), (dx, (block, theirs)),
                (dz, ((1, PAY, HP), mine)), (dz, ((1, PAY, HP), theirs)), (wall, None),
            ],
            [((count, PAY, D), BF16, out)] * 2,
            steps=count,
            wait=wait,
        )
        return a, b

    far_mine, far_theirs = back_projected(2, 1, [*quarters[1:], out])
    piece = add(*after(tuple(early), far_mine))
    early = over_y(piece)
    far_theirs = core_swap(far_theirs)
    blocks = call(
        late_grad_fn,
        "grad_mixer",
        grad_inputs(dx.reshape(GROUP * PAY, MIX))
        + [(value, None) for value in (norm_gate, dpar, dgain, dskip, dhead)],
        [((rows, CH), BF16, None) for rows in (ROWS + 32, ROWS + 32, HALF, HALF, ROWS + 32)],
        steps=4,
        wait=[far_mine, piece],
        scratch=[pltpu.VMEM((16, CH), F32)],
    )
    stack = jnp.stack(after(tuple(early), blocks[0]))
    early = lax.all_gather(stack, ("ctx", "low"), axis=0)

    far_mine, far_theirs = after((far_mine, far_theirs), blocks[0])
    ends = call(
        ends_fn,
        "ends",
        [(far_mine, None), (far_theirs, None)],
        [((CUT, D), BF16, None), ((PAY - CUT, D), BF16, None)],
        steps=1,
    )
    x_up, x_down = x_shift(blocks[2], 1), x_shift(blocks[3], -1)
    up, down = y_shift(ends[0], 1), y_shift(ends[1], -1)
    own_mine, own_theirs = back_projected(0, 1, [*ends, stack])
    x_up, x_down, up, down = after((x_up, x_down, up, down), own_mine)
    own_theirs = core_swap(after(own_theirs, x_up, x_down, up, down))
    ends = call(
        patch_fn,
        "patch",
        [(blocks[1], None), (x_up, None), (blocks[4], None), (x_down, None)],
        [((ROWS + 32, CH), BF16, None)] * 2,
        steps=1,
    )
    late = blocks[0], x_shift(ends[0], 1), x_shift(ends[1], -1)
    mine, theirs = back_projected(1, 2, [*ends, up, down, own_theirs])
    late = after(tuple(late), mine)
    theirs = core_swap(after(theirs, *late))
    quarters, late = over_z(late, ((0, 96), (ROWS, 0)), 128)
    (layer_out,) = call(
        layer_out_fn,
        "layer_out",
        [(out[0], None), (tokens, None), (total, ((1, 8, LOCAL), lambda i: (0, 0, 0)))],
        [((LOCAL, D), F32, None)],
        steps=1,
        wait=[quarters[1]],
    )
    mine, theirs, up, down = after((mine, theirs, up, down), quarters[1])
    tail = jnp.zeros((PAY - CUT, D), BF16)
    above = add(mine[1], theirs[1], jnp.concatenate([up, tail], axis=0))
    head = jnp.zeros((CUT, D), BF16)
    below = add(mine[0], theirs[0], jnp.concatenate([head, down], axis=0))
    back_got = y_shift(above, 1), y_shift(below, -1)
    piece = add(*after(tuple(late), layer_out, above, below))
    late = over_y(piece)
    early = after(early, *late[1:], *back_got)
    parts = [value.reshape(PAY, D) for value in (own_mine, own_theirs)] + list(back_got)
    ahead = add(*[part[LOCAL:] for part in parts])
    ahead = lax.ppermute(ahead, "ctx", [(1, 0)])
    rest, late = gathered(after(tuple(late), ahead))
    (grad_tokens,) = call(
        finish_fn,
        "finish",
        [(scalars(x), SMEM)]
        + [(part, None) for part in [*parts, ahead, tokens, cot, norm_gain[None]]],
        [((LOCAL, D), F32, None)],
        steps=1,
    )

    quarter = ((1, 4, 192, HP), lambda i: (i, 0, 0, 0))
    grad_gate, grad_final = call(
        place_early_fn,
        "place_early",
        [(where, SMEM), (early, quarter), (core_swap(early), quarter)],
        [
            ((ROWS, INNER), F32, ((96, INNER), lambda i: (i, 0))),
            ((4, 192, D), F32, ((4, 48, D), lambda i: (0, i, 0))),
        ],
        steps=4,
        wait=[rest[1]],
    )
    taps, bias, gating, rates, offset, norm, skip, grad_step = call(
        place_small_fn,
        "place_small",
        [(where, SMEM), (rest[0], None), (rest[1], None), (norm_gain.reshape(4, ROWS), None)],
        [((4, CONV_CH), F32, None)]
        + [((n,), F32, None) for n in (CONV_CH, INNER, HEADS, HEADS, D, HEADS)]
        + [((HEADS, ROWS), F32, None)],
        steps=1,
        scratch=[
            pltpu.VMEM((128, ROWS), F32),
            pltpu.VMEM((8, CONV_CH), F32),
            pltpu.VMEM((8, 128), F32),
        ],
    )
    late = list(after(tuple(late), grad_gate, taps, grad_tokens))
    late = late + [core_swap(part) for part in late]
    (grad_mixer,) = call(
        place_late_fn,
        "place_late",
        [(value, HBM) for value in late],
        [((ROWS, CONV_CH), F32, ((96, CONV_CH), lambda i, at: ((at[2] - i + 4) % 4, 0)))],
        steps=4,
        scratch=[pltpu.VMEM((2, 2, 5, 96, HP), BF16), pltpu.SemaphoreType.DMA((2, 2))],
        ahead=[scalars(y, core, z)],
    )
    shape = (1, LOCAL, D)
    return (
        layer_out.reshape(shape),
        grad_tokens.reshape(shape),
        grad_gate,
        grad_mixer,
        grad_step.T,
        grad_final.reshape(2 * 384, D),
        norm,
        taps,
        bias,
        offset,
        rates,
        skip,
        gating,
    )


def solution(mesh):
    apart = jax.sharding.Mesh(mesh.devices.reshape(2, 4, 4, 2, 2), AXES)
    batch = ("fsdp", "y", "low", "core")
    tokens = P(batch, "ctx", None)
    rows = P("fsdp", None)
    return jax.shard_map(
        per_device,
        mesh=apart,
        in_specs=(tokens, P(batch, None), tokens, rows, rows, rows, rows) + (P(),) * 7,
        out_specs=(tokens, tokens, rows, rows, rows, rows) + (P(),) * 7,
        check_vma=False,
    )
```

```python
import functools

import jax
import jax.numpy as jnp
from jax import lax
from jax.experimental import pallas as pl
from jax.experimental.pallas import tpu as pltpu
from jax.sharding import PartitionSpec as P

D = 1536
INNER = 3072
STATE = 128
HEADS = 48
HEAD_DIM = 64
CONV_CH = 3328
LOCAL = 256
GROUP = 8
OWN = 6
HP = OWN * HEAD_DIM
CH = HP + 2 * STATE
ROWS = D // 4
EPS = 1e-05
AXES = ("ctx", "fsdp", "y", "low", "core")
F32 = jnp.float32
BF16 = jnp.bfloat16
HIGH = lax.Precision.HIGHEST
MASKED = -1e30
PAY = LOCAL + 16
CUT = 144
WIDE = CH + 128 + HP
HALF = 208
MIX = CH + 128
SCALE = 1.0
DURATION = {
    "pack": 4, "prep": 3, "params": 2, "forward_first": 10, "forward_near": 18, "forward_far": 10, "d_mixed": 7, "gate": 7,
    "out_proj": 7, "ungate": 8, "grad_final": 0.1, "grad_gate": 0.1, "back": 38, "grad_mixer": 13,
    "back_proj": 6, "split": 3, "patch": 2, "ends": 1, "finish": 3, "layer_out": 2, "lines": 2, "place_early": 7, "place_late": 6, "place_small": 2,
}
VMEM_LIMIT = 63 * 1024 * 1024


def place_of(ctx, x, y, low, core):
    return (ctx * 4 + x) * 16 + (y * 2 + low) * 2 + core


def pairs_of(move):
    pairs = []
    for ctx in range(2):
        for x in range(4):
            for y in range(4):
                for low in range(2):
                    for core in range(2):
                        to = move(ctx, x, y, low, core)
                        if to is not None:
                            pairs.append((place_of(ctx, x, y, low, core), place_of(*to)))
    return pairs


def move(value, to):
    return lax.ppermute(value, AXES, pairs_of(to))


def x_shift(value, steps):
    return lax.ppermute(value, "fsdp", [(i, (i + steps) % 4) for i in range(4)])


def y_shift(value, steps):
    return lax.ppermute(value, "y", [(i, (i + steps) % 4) for i in range(4)])


def core_swap(value):
    return lax.ppermute(value, "core", [(0, 1), (1, 0)])


def z_shift(value, steps):
    def to(ctx, x, y, low, core):
        z = (2 * ctx + low + steps) % 4
        return (z // 2, x, y, z % 2, core)

    return move(value, to)


def after(value, *others):
    return lax.optimization_barrier((value,) + others)[0]


def add(*values):
    total = values[0].astype(F32)
    for value in values[1:]:
        total = total + value.astype(F32)
    return total.astype(BF16)


def mm(a, b, dims, precision=None):
    return lax.dot_general(a, b, (dims, ((), ())), precision=precision, preferred_element_type=F32)


NN = ((1,), (0,))
NT = ((1,), (1,))
TN = ((0,), (0,))
SMEM = object()
HBM = object()


def call(fn, name, inputs, outputs, steps=GROUP, scratch=(), aliases=None, ahead=(), wait=()):
    us = DURATION[name] * SCALE
    first = len(ahead) + len(inputs)
    inputs = inputs + [(value, HBM) for value in wait]

    def kernel(*refs):
        fn(*refs[:first], *refs[first + len(wait) :])

    def block(shape, how):
        if how is SMEM:
            return pl.BlockSpec(memory_space=pltpu.SMEM)
        if how is HBM:
            return pl.BlockSpec(memory_space=pl.ANY)
        if how is None:
            return pl.BlockSpec(tuple(shape), lambda i, *s: (0,) * len(shape))
        return pl.BlockSpec(*how)

    return pl.pallas_call(
        kernel,
        name=name,
        grid_spec=pltpu.PrefetchScalarGridSpec(
            num_scalar_prefetch=len(ahead),
            grid=(steps,),
            in_specs=[block(value.shape, how) for value, how in inputs],
            out_specs=[block(shape, how) for shape, _, how in outputs],
            scratch_shapes=list(scratch),
        ),
        out_shape=[jax.ShapeDtypeStruct(shape, dtype) for shape, dtype, _ in outputs],
        input_output_aliases=aliases or {},
        cost_estimate=pl.CostEstimate(
            flops=int(us * 1.15e9), bytes_accessed=int(us * 3.6e6), transcendentals=0
        ),
        compiler_params=pltpu.CompilerParams(
            dimension_semantics=("arbitrary",), vmem_limit_bytes=VMEM_LIMIT
        ),
    )(*ahead, *[value for value, _ in inputs])


def seq(*rest, first=0, low=0, high=GROUP):
    def at(i, *s):
        return (jnp.clip(i + first, low, high - 1) - low,) + (0,) * len(rest)

    return ((1,) + rest, at)


def by_device(*rest, steps=1, first=0):
    def at(i, at):
        i = i * steps + first
        y, core = (at[0] + 4 - i % 4) % 4, (at[1] + i // 4) % 2
        return (2 * y + core,) + (0,) * len(rest)

    return ((1,) + rest, at)


def lane_ids(rows, cols):
    return lax.broadcasted_iota(jnp.int32, (rows, cols), 1)


def pair(values, p, left):
    return jnp.where(left, values[:, 2 * p : 2 * p + 1], values[:, 2 * p + 1 : 2 * p + 2])


def small_parts(small):
    mine = lane_ids(LOCAL, 128) < OWN
    parts = small, pltpu.roll(small, 120, 1), pltpu.roll(small, 112, 1)
    return [jnp.where(mine, part, 0.0) for part in parts]


def summed_rows(values, dims):
    lane = lane_ids(LOCAL, 128)
    high = values.astype(BF16).astype(F32)
    rest = values - high
    middle = rest.astype(BF16).astype(F32)
    parts = jnp.where(lane < 8, high, jnp.where(lane < 16, middle, rest - middle))
    got = mm(triangle().astype(BF16), parts.astype(BF16), dims)
    return got + pltpu.roll(got, 120, 1) + pltpu.roll(got, 112, 1)


def head_sums(values, p):
    lane, row = lane_ids(128, 128), lax.broadcasted_iota(jnp.int32, (128, 128), 0)
    ones = jnp.where(lane == 2 * p + row // HEAD_DIM, 1.0, 0.0).astype(BF16)
    return mm(values.astype(BF16), ones, NN)


def row_total(values, place):
    folded = values[:, 0:128] + values[:, 128:256] + values[:, 256:384]
    high = folded.astype(BF16)
    rest = (folded - high.astype(F32)).astype(BF16)
    ones = jnp.where(lane_ids(LOCAL, 128) == place, 1.0, 0.0).astype(BF16)
    return mm(jnp.concatenate([high, rest], axis=1), ones, NN)


def triangle():
    row = lax.broadcasted_iota(jnp.int32, (LOCAL, LOCAL), 0)
    col = lax.broadcasted_iota(jnp.int32, (LOCAL, LOCAL), 1)
    return row >= col


def seg_columns(row):
    return jnp.broadcast_to(row, (128, LOCAL)).T


def same_before(seg, k):
    return jnp.concatenate([seg[:k], seg[: LOCAL - k]], axis=0) == seg


def mask_bias(seg, row):
    wide = jnp.concatenate([seg, seg], axis=1)
    return jnp.where((wide == row) & triangle(), 0.0, MASKED)


def prep_kernel_fn(at_ref, tok_ref, ahead_ref, gain_ref, seg_ref, out_ref, buf_ref):
    def normed(values):
        values = values.astype(F32)
        inv = lax.rsqrt(jnp.mean(values * values, axis=1, keepdims=True) + EPS)
        return (values * inv * gain_ref[...]).astype(BF16)

    buf_ref[0:LOCAL] = normed(tok_ref[...])
    seg = seg_ref[...].astype(F32)
    seg = jnp.where(at_ref[1] == 0, seg[:, :LOCAL], seg[:, LOCAL:])
    part = jnp.concatenate([seg, jnp.zeros((1, ROWS - LOCAL), F32)], axis=1)
    row = jnp.concatenate([part] * 4, axis=1)
    number = lax.broadcasted_iota(jnp.int32, (16, D), 0)
    extra = jnp.where(number >= 8, normed(ahead_ref[...]).astype(F32), 0.0)
    buf_ref[LOCAL:PAY] = jnp.where(number == 0, row, extra).astype(BF16)
    for r in range(4):
        start = pl.multiple_of(ROWS * lax.rem(at_ref[0] + r, 4), 128)
        out_ref[:, ROWS * r : ROWS * r + ROWS] = buf_ref[:, pl.ds(start, ROWS)]


def pack_kernel_fn(
    at_ref, gate_ref, mixer_ref, final_ref, step_ref,
    slab_ref, rows_ref, buf_ref, wide_ref, turn_ref, sem,
):
    y, core = at_ref[0], at_ref[1]
    copies = []
    for i, src in enumerate((mixer_ref, gate_ref)):
        for a in range(2):
            first = (2 * core + a) * 768 + 384 * lax.div(y, 2) + 128 * lax.rem(y, 2)
            where = pl.ds(pl.multiple_of(first, 128), 256)
            copies.append((src.at[:, where], buf_ref.at[2 * i + a]))
    copies.append((mixer_ref.at[:, pl.ds(INNER, 2 * STATE)], buf_ref.at[4]))
    copies.append((final_ref.at[pl.ds(pl.multiple_of(192 * y, 64), 192)], rows_ref))
    copies = [pltpu.make_async_copy(a, b, sem.at[i]) for i, (a, b) in enumerate(copies)]
    for copy in copies:
        copy.start()
    turn_ref[...] = jnp.zeros_like(turn_ref)
    step = step_ref[...].astype(F32)
    for line in range(4):
        for c in range(2):

            @pl.when((y == line) & (core == c))
            def _(line=line, c=c):
                for a in range(2):
                    at = 12 * (2 * c + a) + 3 * line
                    for to in range(3 * a, 24, 8):
                        turn_ref[to : to + 3] = step[at : at + 3]

    wide_ref[:, CH:MIX] = turn_ref[...].T
    for copy in copies:
        copy.wait()
    for odd in range(2):

        @pl.when(lax.rem(y, 2) == odd)
        def _(odd=odd):
            for i, base in enumerate((0, MIX)):
                for a in range(2):
                    block = buf_ref[2 * i + a].astype(F32)
                    to = base + 192 * a
                    wide_ref[:, to : to + 192] = block[:, 64 * odd : 64 * odd + 192]

    slab_ref[...] = wide_ref[...].astype(BF16)
    slab_ref[:, HP:CH] = buf_ref[4]


def params_kernel_fn(
    at_ref, taps_ref, bias_ref, offset_ref, rates_ref, skip_ref, gating_ref,
    par_ref, hp_ref, gain_ref,
):
    par_ref[...] = jnp.zeros_like(par_ref)
    hp_ref[...] = jnp.zeros_like(hp_ref)
    for line in range(4):
        for c in range(2):

            @pl.when((at_ref[0] == line) & (at_ref[1] == c))
            def _(line=line, c=c):
                for a in range(2):
                    at = slice((2 * c + a) * 768 + 192 * line, (2 * c + a) * 768 + 192 * line + 192)
                    to = slice(192 * a, 192 * a + 192)
                    par_ref[0:4, to] = taps_ref[:, at]
                    par_ref[4:5, to] = bias_ref[:, at]
                    gain_ref[0:1, to] = gating_ref[:, at]
                    at = slice(12 * (2 * c + a) + 3 * line, 12 * (2 * c + a) + 3 * line + 3)
                    for first in range(3 * a, 24, 8):
                        to = slice(first, first + 3)
                        hp_ref[0:1, to] = offset_ref[:, at]
                        hp_ref[1:2, to] = -jnp.exp(rates_ref[:, at])
                        hp_ref[2:3, to] = skip_ref[:, at]

    par_ref[0:4, HP:] = taps_ref[:, INNER:]
    par_ref[4:5, HP:] = bias_ref[:, INNER:]


class Pieces:
    def __init__(self, parts, buf, sem):
        self.parts, self.buf, self.sem = parts, buf, sem

    def fetch(self, step, slot):
        for k, refs in enumerate(self.parts):

            @pl.when(step == k)
            def _(refs=refs):
                first = 0
                for ref in refs:
                    to = self.buf.at[slot, first : first + ref.shape[0]]
                    pltpu.make_async_copy(ref, to, self.sem.at[slot]).start()
                    first += ref.shape[0]

    def next(self):
        step = pl.program_id(0)
        slot = lax.rem(step, 2)

        @pl.when(step == 0)
        def _():
            self.fetch(step, slot)

        @pl.when(step < len(self.parts) - 1)
        def _():
            self.fetch(step + 1, 1 - slot)

        pltpu.make_async_copy(self.buf.at[slot], self.buf.at[slot], self.sem.at[slot]).wait()
        return slot


def forward_body(
    ctx_ref, par_ref, hp_ref, n, wall_ref,
    nall_ref, xbc_ref, u_ref, out_ref, small_ref, z_ref, seg_ref, y_ref, state_ref, xc_ref,
):
    par = par_ref[...]
    hp = hp_ref[...]
    nall_ref[0] = n
    row = n[LOCAL:PAY, 0:LOCAL].astype(F32)[0:1]
    seg_ref[0] = jnp.broadcast_to(row, (8, LOCAL))
    seg = seg_columns(row)
    keeps = [same_before(seg, k) for k in range(1, 4)]
    z_ref[0] = mm(n[0:LOCAL], wall_ref[:, MIX:], NN).astype(BF16)
    for j in range(3):
        prod = mm(n, wall_ref[:, 256 * j : 256 * j + 256], NN)
        for half in range(2):
            first = 256 * j + 128 * half
            at = slice(first, first + 128)
            x = prod[:, 128 * half : 128 * half + 128]
            if first == CH:
                raw = x[0:LOCAL] + hp[0:1]
                continue
            low = x.astype(BF16)
            xbc_ref[0, :, at] = low
            x = low.astype(F32)
            ext = jnp.concatenate([x[LOCAL + 8 :], x[:LOCAL]], axis=0)
            u = par[4:5, at] + par[0:1, at] * x[:LOCAL]
            for k in range(1, 4):
                moved = ext[8 - k : 8 - k + LOCAL]
                u = u + par[k : k + 1, at] * jnp.where(keeps[k - 1], moved, 0.0)
            u_ref[0, :, at] = u.astype(BF16)
            xc_ref[:, at] = (u * jax.nn.sigmoid(u)).astype(BF16)
    dt = jnp.maximum(raw, 0.0) + jnp.log1p(jnp.exp(-jnp.abs(raw)))
    cum = summed_rows(dt * hp[1:2], NN)
    lane = lane_ids(LOCAL, 128)
    small_ref[0] = jnp.where(lane < 8, dt, jnp.where(lane < 16, pltpu.roll(cum, 8, 1), raw))
    left = lane < HEAD_DIM
    left1 = lane_ids(1, 128) < HEAD_DIM
    basis, out_basis = xc_ref[:, HP : HP + STATE], xc_ref[:, HP + STATE :]
    out_ref[0] = out_basis

    @pl.when(ctx_ref[0] == 0)
    def _():
        tail = jnp.where(seg == seg[LOCAL - 1 :], jnp.exp(cum[LOCAL - 1 :] - cum) * dt, 0.0)
        for p in range(3):
            at = slice(128 * p, 128 * p + 128)
            part = xc_ref[:, at].astype(F32) * pair(tail, p, left)
            state_ref[0, at] = mm(part.astype(BF16), basis, TN).astype(BF16)

    @pl.when(ctx_ref[0] != 0)
    def _():
        state_ref[0] = jnp.zeros((HP, STATE), BF16)

    cum_t = cum.T
    scores = mm(out_basis, basis, NT)
    bias = mask_bias(seg, row)
    for p in range(3):
        at = slice(128 * p, 128 * p + 128)
        x = xc_ref[:, at].astype(F32)
        scaled = (x * pair(dt, p, left)).astype(BF16)
        halves = []
        for h in (2 * p, 2 * p + 1):
            mix = jnp.exp(cum[:, h : h + 1] - cum_t[h : h + 1] + bias) * scores
            halves.append(mm(mix.astype(BF16), scaled, NN))
        y = jnp.where(left, halves[0], halves[1]) + pair(hp[2:3], p, left1) * x
        y_ref[0, :, at] = y.astype(BF16)


def forward_first_fn(ctx_ref, par_ref, hp_ref, mine, theirs, *refs):
    slabs, wall_ref, outs, (xc, buf, sem, wsem) = refs[:5], refs[5], refs[6:15], refs[15:]
    copies = []
    first = 0
    for i, ref in enumerate(slabs):
        rows = ref.shape[0]
        copies.append(pltpu.make_async_copy(ref, wall_ref.at[first : first + rows], wsem.at[i]))
        first += rows

    @pl.when(pl.program_id(0) == 0)
    def _():
        for copy in copies:
            copy.start()

    slot = Pieces([[mine], [theirs]], buf, sem).next()

    @pl.when(pl.program_id(0) == 0)
    def _():
        for copy in copies:
            copy.wait()

    forward_body(ctx_ref, par_ref, hp_ref, buf[slot], wall_ref, *outs, xc)


def forward_near_fn(ctx_ref, par_ref, hp_ref, wall_ref, *refs):
    parts, outs, (xc, buf, sem) = refs[:4], refs[13:22], refs[22:]
    slot = Pieces([[part] for part in parts], buf, sem).next()
    forward_body(ctx_ref, par_ref, hp_ref, buf[slot], wall_ref, *outs, xc)


def forward_far_fn(ctx_ref, par_ref, hp_ref, wall_ref, *refs):
    parts, outs, (xc, buf, sem) = refs[:4], refs[12:21], refs[21:]
    slot = Pieces([parts[:2], parts[2:]], buf, sem).next()
    forward_body(ctx_ref, par_ref, hp_ref, buf[slot], wall_ref, *outs, xc)


def dmix_kernel_fn(at_ref, *refs):
    g_refs, (own, near, far, away, dmix_ref, wf_ref, sem) = refs[:4], refs[4:]
    step = pl.program_id(0)
    up, down = wf_ref.at[0:192], wf_ref.at[192:HP]

    @pl.when(step == 0)
    def _():
        for r, (a, b) in enumerate(((own, near), (near, own), (away, far), (far, away))):

            @pl.when(at_ref[2] == r)
            def _(a=a, b=b):
                pltpu.make_async_copy(a, up, sem.at[0]).start()
                pltpu.make_async_copy(b, down, sem.at[1]).start()

        pltpu.make_async_copy(own, up, sem.at[0]).wait()
        pltpu.make_async_copy(own, down, sem.at[1]).wait()

    for k, ref in enumerate(g_refs):
        dmix_ref[k] = mm(ref[0], wf_ref[...], NT).astype(BF16)


def entered(k, ctx_ref, state_a_ref, state_b_ref, small_ref, seg_ref, use):
    @pl.when(ctx_ref[0] != 0)
    def _():
        number = 2 * pl.program_id(0) + k
        line, core = lax.rem(number, 4), lax.div(number, 4)
        near = jnp.where(line == 0, core, 2 + 2 * core + lax.div(line, 2))
        seg = seg_columns(seg_ref[k, 0:1])
        enter = jnp.where(seg == seg[0:1], jnp.exp(small_parts(small_ref[k])[1]), 0.0)
        left = lane_ids(LOCAL, 128) < HEAD_DIM
        for p in range(3):
            at = slice(128 * p, 128 * p + 128)
            state = jnp.where(line == 2, state_b_ref[core, at], state_a_ref[near, at])
            use(at, pair(enter, p, left), state)


def gate_kernel_fn(
    ctx_ref, y_ref, state_a_ref, state_b_ref, z_ref, dmix_ref, basis_ref, small_ref, seg_ref,
    gain_ref, yall_ref, low_ref, sums_ref, sum_ref,
):
    for k in range(2):
        sum_ref[...] = y_ref[k].astype(F32)

        def use(at, gate, state, k=k):
            sum_ref[:, at] += gate * mm(basis_ref[k], state, NT)

        entered(k, ctx_ref, state_a_ref, state_b_ref, small_ref, seg_ref, use)
        y = sum_ref[...]
        yall_ref[k] = y.astype(BF16)
        z = z_ref[k].astype(F32)
        gated = y * (z * jax.nn.sigmoid(z))
        raised = gated * gain_ref[0:1]
        low_ref[k] = raised.astype(BF16)
        both = row_total(gated * gated, 0) + row_total(dmix_ref[k].astype(F32) * raised, 1)
        sums_ref[k] = both.T[0:8]


def product_kernel_fn(at_ref, a_ref, w_ref, out_ref, buf, sem):
    step = pl.program_id(0)

    def copies(number):
        found = []
        for k in range(4):
            place = 2 * lax.rem(at_ref[0] + 4 - k, 4) + lax.rem(at_ref[1] + number, 2)
            found.append(pltpu.make_async_copy(buf.at[number, k], out_ref.at[place], sem.at[number, k]))
        return found

    for number in range(2):

        @pl.when(step == number)
        def _(number=number):
            for k, copy in enumerate(copies(number)):
                buf[number, k] = mm(a_ref[k], w_ref[...], NN).astype(BF16)
                copy.start()

    @pl.when(step == 1)
    def _():
        for number in range(2):
            for copy in copies(number):
                copy.wait()


def ungate_kernel_fn(
    at_ref, ctx_ref, y_ref, z_ref, dmix_ref, sums_ref, basis_ref, small_ref, seg_ref, gain_ref,
    mixed_ref, dy_ref, dz_ref, dstate_ref, dgain_ref, buf, sem,
):
    step = pl.program_id(0)
    slot = lax.rem(step, 2)

    def copy(number, k):
        place = 2 * lax.rem(at_ref[0] + 8 - 2 * number - k, 4)
        place = place + lax.rem(at_ref[1] + lax.div(number, 2), 2)
        spot = lax.rem(number, 2)
        return pltpu.make_async_copy(buf.at[spot, k], mixed_ref.at[place], sem.at[spot, k])

    @pl.when(step == 0)
    def _():
        dgain_ref[...] = jnp.zeros_like(dgain_ref)

    @pl.when(step >= 2)
    def _():
        for k in range(2):
            copy(step - 2, k).wait()

    gain = gain_ref[0:1]
    for k in range(2):
        pad = jnp.concatenate([sums_ref[k], jnp.zeros((120, LOCAL), F32)], axis=0).T
        inv = lax.rsqrt(pad[:, 0:1] / INNER + EPS)
        mean_ev = inv * pad[:, 1:2] / INNER
        y = y_ref[k].astype(F32)
        z = z_ref[k].astype(F32)
        dmix = dmix_ref[k].astype(F32)
        sig = jax.nn.sigmoid(z)
        act = z * sig
        v = y * act * inv
        buf[slot, k] = (v * gain).astype(BF16)
        copy(step, k).start()
        d_gated = inv * (dmix * gain - v * mean_ev)
        dy = (d_gated * act).astype(BF16)
        dy_ref[k] = dy
        dz_ref[k, 0:LOCAL] = (d_gated * y * sig * (1.0 + z * (1.0 - sig))).astype(BF16)
        dz_ref[k, LOCAL:PAY] = jnp.zeros((16, HP), BF16)
        dgain_ref[0:1] += jnp.sum(dmix * v, axis=0, keepdims=True)

        @pl.when(ctx_ref[0] != 0)
        def _(k=k, dy=dy):
            seg = seg_columns(seg_ref[k, 0:1])
            enter = jnp.where(seg == seg[0:1], jnp.exp(small_parts(small_ref[k])[1]), 0.0)
            left = lane_ids(LOCAL, 128) < HEAD_DIM
            for p in range(3):
                at = slice(128 * p, 128 * p + 128)
                part = (dy[:, at].astype(F32) * pair(enter, p, left)).astype(BF16)
                dstate_ref[k, at] = mm(part, basis_ref[k], TN).astype(BF16)

        @pl.when(ctx_ref[0] == 0)
        def _(k=k):
            dstate_ref[k] = jnp.zeros((HP, STATE), BF16)

    @pl.when(step == 3)
    def _():
        for number in (2, 3):
            for k in range(2):
                copy(number, k).wait()


def back_kernel_fn(
    ctx_ref, dy_ref, u_ref, xbc_ref, small_ref, seg_ref, par_ref, hp_ref, state_a_ref, state_b_ref,
    dstate_ref, skip0_ref, par0_ref, head0_ref,
    dx_ref, dskip_ref, dpar_ref, dhead_ref, turn_ref, dxc_ref, dc_ref, dd_ref, xc_ref, slope_ref,
):
    step = pl.program_id(0)
    hp = hp_ref[...]
    par = par_ref[...]
    dt, cum, raw = small_parts(small_ref[0])
    cum_t = cum.T
    for j in range(5):
        at = slice(128 * j, 128 * j + 128)
        u = u_ref[0, :, at].astype(F32)
        sig = jax.nn.sigmoid(u)
        xc_ref[:, at] = (u * sig).astype(BF16)
        slope_ref[:, at] = sig * (1.0 + u * (1.0 - sig))
    basis, out_basis = xc_ref[:, HP : HP + STATE], xc_ref[:, HP + STATE :]
    scores = mm(basis, out_basis, NT)
    row = seg_ref[0, 0:1]
    seg = seg_columns(row)
    same = jnp.concatenate([seg, seg], axis=1) == row
    first = lax.broadcasted_iota(jnp.int32, (LOCAL, LOCAL), 0)
    bias = jnp.where(same & (first <= lane_ids(LOCAL, LOCAL)), 0.0, MASKED)
    lane = lane_ids(LOCAL, 128)
    left = lane < HEAD_DIM
    left1 = lane_ids(1, 128) < HEAD_DIM

    @pl.when(step == 0)
    def _():
        dskip_ref[...] = skip0_ref[...]
        dpar_ref[...] = par0_ref[...]
        dhead_ref[...] = head0_ref[...]
        turn_ref[...] = jnp.zeros_like(turn_ref)

    d_scores = jnp.zeros((LOCAL, LOCAL), F32)
    sums = jnp.zeros((LOCAL, 128), F32)
    for p in range(3):
        at = slice(128 * p, 128 * p + 128)
        x = xc_ref[:, at].astype(F32)
        g = dy_ref[0, :, at]
        steps = pair(dt, p, left)
        scaled = (x * steps).astype(BF16)
        halves = []
        for h in (2 * p, 2 * p + 1):
            mine = left if h % 2 == 0 else ~left
            prod = mm(scaled, jnp.where(mine, g, jnp.zeros_like(g)), NT)
            mix = jnp.exp(cum_t[h : h + 1] - cum[:, h : h + 1] + bias)
            weighed = mix * prod
            d_scores = d_scores + weighed
            pulled = weighed * scores
            turn_ref[h : h + 1] = jnp.sum(pulled, axis=0, keepdims=True)
            folded = pulled[:, :128] + pulled[:, 128:]
            high = folded.astype(BF16)
            rest = (folded - high.astype(F32)).astype(BF16)
            ones = jnp.where(lane == h, 1.0, 0.0).astype(BF16)
            sums = sums + mm(jnp.concatenate([high, rest], axis=1), ones, NN)
            halves.append(mm((mix * scores).astype(BF16), g, NN))
        gf = g.astype(F32)
        skip = pair(hp[2:3], p, left1)
        dxc_ref[:, at] = steps * jnp.where(left, halves[0], halves[1]) + skip * gf
        dskip_ref[0:1, at] += jnp.sum(gf * x, axis=0, keepdims=True)
    dd_ref[...] = jnp.where(dt > 1e-37, sums / jnp.maximum(dt, 1e-37), 0.0)
    dc_ref[...] = turn_ref[...].T - sums
    low = d_scores.astype(BF16)
    dxc_ref[:, HP : HP + STATE] = mm(low, out_basis, NN)
    dxc_ref[:, HP + STATE :] = mm(low, basis, TN)

    @pl.when(ctx_ref[0] != 0)
    def _():
        enter = jnp.where(seg == seg[0:1], jnp.exp(cum), 0.0)
        d_out = jnp.zeros((LOCAL, STATE), F32)
        extra = jnp.zeros((LOCAL, 128), F32)
        for p in range(3):
            at = slice(128 * p, 128 * p + 128)
            state = jnp.where(lax.rem(step, 4) == 2, state_b_ref[0, at], state_a_ref[0, at])
            scaled = dy_ref[0, :, at].astype(F32) * pair(enter, p, left)
            d_out = d_out + mm(scaled.astype(BF16), state, NN)
            extra = extra + head_sums(scaled * mm(out_basis, state, NT), p)
        dxc_ref[:, HP + STATE :] += d_out
        dc_ref[...] += extra

    @pl.when(ctx_ref[0] == 0)
    def _():
        tail = jnp.where(seg == seg[LOCAL - 1 :], jnp.exp(cum[LOCAL - 1 :] - cum), 0.0)
        weight = tail * dt
        d_basis = jnp.zeros((LOCAL, STATE), F32)
        d_weight = jnp.zeros((LOCAL, 128), F32)
        for p in range(3):
            at = slice(128 * p, 128 * p + 128)
            x = xc_ref[:, at].astype(F32)
            w = pair(weight, p, left)
            ds = dstate_ref[0, at]
            seen = mm(basis, ds, NT)
            dxc_ref[:, at] += w * seen
            d_basis = d_basis + mm((x * w).astype(BF16), ds, NN)
            d_weight = d_weight + head_sums(x * seen, p)
        dxc_ref[:, HP : HP + STATE] += d_basis
        dd_ref[...] += tail * d_weight
        moved = weight * d_weight
        dc_ref[...] -= moved
        dc_ref[LOCAL - 1 : LOCAL] += jnp.sum(moved, axis=0, keepdims=True)

    dc = jnp.where(lane < OWN, dc_ref[...], 0.0)
    dc = dc + pltpu.roll(dc, 8, 1) + pltpu.roll(dc, 16, 1)
    d_decay = summed_rows(dc, TN)
    rate = hp[1:2]
    d_raw = (dd_ref[...] + d_decay * rate) * jax.nn.sigmoid(raw)
    d_raw = jnp.where(lane < OWN, d_raw, 0.0)
    dhead_ref[0:1] += jnp.sum(d_decay * dt, axis=0, keepdims=True) * rate
    dhead_ref[1:2] += jnp.sum(d_raw, axis=0, keepdims=True)
    dx_ref[0, 0:LOCAL, CH:MIX] = d_raw.astype(BF16)
    dx_ref[0, LOCAL:PAY, CH:MIX] = jnp.zeros((16, 128), BF16)

    keeps = [same_before(seg, k) for k in range(1, 4)]
    zeros = jnp.zeros((8, 128), F32)
    for j in range(5):
        at = slice(128 * j, 128 * j + 128)
        x = xbc_ref[0, :, at].astype(F32)
        ext = jnp.concatenate([x[LOCAL + 8 :], x[:LOCAL]], axis=0)
        du = dxc_ref[:, at] * slope_ref[:, at]
        dpar_ref[4:5, at] += jnp.sum(du, axis=0, keepdims=True)
        dpar_ref[0:1, at] += jnp.sum(du * x[:LOCAL], axis=0, keepdims=True)
        total = par[0:1, at] * du
        before = zeros
        for k in range(1, 4):
            kept = jnp.where(keeps[k - 1], du, 0.0)
            moved = ext[8 - k : 8 - k + LOCAL]
            dpar_ref[k : k + 1, at] += jnp.sum(kept * moved, axis=0, keepdims=True)
            back = jnp.concatenate([zeros, kept * par[k : k + 1, at], zeros], axis=0)
            total = total + back[8 + k : 8 + k + LOCAL]
            before = before + back[k : k + 8]
        dx_ref[0, 0:LOCAL, at] = total.astype(BF16)
        dx_ref[0, LOCAL:PAY, at] = jnp.concatenate([zeros, before], axis=0).astype(BF16)


def norm_row(grad, weight):
    column = jnp.sum(grad * weight.astype(F32), axis=1, keepdims=True)
    return jnp.broadcast_to(column, (ROWS, 128)).T[0:1]


def early_grad_fn(at_ref, n_ref, d_ref, wall_ref, keep_ref, got_ref, *refs):
    step = pl.program_id(0)
    outs, norm_ref = refs[:4], refs[4]
    grad = mm(n_ref[...], d_ref[...], TN)

    @pl.when(step == 0)
    def _():
        norm_ref[...] = jnp.zeros_like(norm_ref)

    norm_ref[pl.ds(step, 1)] = norm_row(grad, wall_ref[:, MIX:])
    low = grad.astype(BF16)
    owner = lax.rem(at_ref[0] + step, 4)
    for r in range(4):
        for mine, src in ((True, keep_ref), (False, got_ref)):

            @pl.when((step == r) & ((lax.div(owner, 2) == at_ref[1]) == mine))
            def _(src=src, out=outs[r]):
                for q in range(4):
                    first = pl.multiple_of(192 * lax.rem(owner, 2) + 48 * q, 16)
                    out[192 * q : 192 * q + 96] = low[96 * q : 96 * q + 96]
                    out[192 * q + 96 : 192 * q + 144] = src[pl.ds(first, 48), 0:ROWS]
                    out[192 * q + 144 : 192 * q + 192] = src[pl.ds(first, 48), ROWS:]


def late_grad_fn(
    at_ref, n_ref, d_ref, wall_ref, norm_ref, par_ref, gain_ref, skip_ref, head_ref, *refs
):
    step = pl.program_id(0)
    outs, small_ref = refs[:5], refs[5]
    grad = mm(n_ref[...], d_ref[...], TN)
    rows = grad[:, CH:].T[0:16].astype(BF16)
    low = grad[:, 0:CH].astype(BF16)

    @pl.when(step == 0)
    def _():
        small_ref[...] = jnp.zeros_like(small_ref)
        small_ref[4:9] = par_ref[0:5]
        small_ref[9:10, 0:HP] = gain_ref[0:1]
        small_ref[10:12, 0:128] = head_ref[0:2]
        lane = lane_ids(1, 128)
        skip = jnp.zeros((1, 128), F32)
        for h in range(OWN):
            part = skip_ref[0:1, HEAD_DIM * h : HEAD_DIM * h + HEAD_DIM]
            skip = jnp.where(lane == h, jnp.sum(part, axis=1, keepdims=True), skip)
        small_ref[12:13, 0:128] = skip

    owner = lax.rem(at_ref[0] + step, 4)
    row = norm_row(grad, wall_ref[:, 0:MIX]) + norm_ref[pl.ds(step, 1)]
    small_ref[pl.ds(owner, 1), 0:ROWS] = row
    for r, out in enumerate((outs[0], outs[1], outs[3], outs[4])):

        @pl.when(step == (0, 1, 2, 3)[r])
        def _(out=out, r=r):
            if r == 2:
                outs[2][...] = low[0:HALF]
                out[0 : ROWS - HALF] = low[HALF:]
            else:
                out[0:ROWS] = low
            out[-16:, 0:ROWS] = rows
            out[-16:, ROWS:] = jnp.zeros((16, CH - ROWS), BF16)

    @pl.when(step == 3)
    def _():
        for out in (outs[0], outs[1], outs[3], outs[4]):
            out[-32:-16] = small_ref[...].astype(BF16)


def patch_fn(a_ref, up_ref, b_ref, down_ref, first_ref, second_ref):
    first_ref[...] = a_ref[...]
    first_ref[0:HALF] = (a_ref[0:HALF].astype(F32) + up_ref[...].astype(F32)).astype(BF16)
    second_ref[...] = b_ref[...]
    second_ref[HALF:] = (b_ref[HALF:].astype(F32) + down_ref[...].astype(F32)).astype(BF16)


def ends_fn(a_ref, b_ref, up_ref, down_ref):
    total = a_ref[0].astype(F32) + b_ref[0].astype(F32)
    up_ref[...] = total[:CUT].astype(BF16)
    down_ref[...] = total[CUT:].astype(BF16)


def lines_fn(a_ref, b_ref, c_ref, d_ref, lines_ref, small_ref):
    total = jnp.zeros((96, 2 * STATE), F32)
    for line, ref in enumerate((a_ref, b_ref, c_ref, d_ref)):
        lines_ref[line] = ref[0:96, 0:HP]
        total = total + ref[0:96, HP:].astype(F32)
        small_ref[line] = ref[96:]
    lines_ref[4, :, 0 : 2 * STATE] = total.astype(BF16)
    lines_ref[4, :, 2 * STATE :] = jnp.zeros((96, 128), BF16)


def final_grad_fn(at_ref, m_ref, g_ref, send_ref, keep_ref):
    low = mm(m_ref[...], g_ref[...], TN).astype(BF16)

    @pl.when(pl.program_id(0) < 2)
    def _():
        send_ref[...] = low

    @pl.when(pl.program_id(0) >= 2)
    def _():
        keep_ref[...] = low


def split_fn(parts, at_ref, *refs):
    blocks, outs, sum_ref = refs[:-5], refs[-5:-1], refs[-1]
    total = blocks[0][...].astype(F32)
    for block in blocks[1:]:
        total = total + block[...].astype(F32)
    sum_ref[...] = total.astype(BF16)
    for k, out in enumerate(outs):
        quarter = lax.rem(at_ref[0] + k, 4)
        to = 0
        for first, rows in parts:
            if rows:
                start = pl.multiple_of(first + rows * quarter, 16)
                out[to : to + rows] = sum_ref[pl.ds(start, rows)]
                to += rows
            else:
                out[to:] = sum_ref[first:]


def back_proj_fn(ax_ref, bx_ref, az_ref, bz_ref, wall_ref, a_ref, b_ref):
    dx = jnp.concatenate([ax_ref[0], bx_ref[0]], axis=0)
    dz = jnp.concatenate([az_ref[0], bz_ref[0]], axis=0)
    for r in range(4):
        at = slice(ROWS * r, ROWS * r + ROWS)
        part = mm(dx, wall_ref[at, 0:MIX], NT) + mm(dz, wall_ref[at, MIX:], NT)
        low = part.astype(BF16)
        a_ref[0, :, at] = low[:PAY]
        b_ref[0, :, at] = low[PAY:]


def finish_fn(at_ref, a_ref, b_ref, c_ref, d_ref, ahead_ref, tok_ref, cot_ref, gain_ref, out_ref):
    values = tok_ref[...].astype(F32)
    inv = lax.rsqrt(jnp.mean(values * values, axis=1, keepdims=True) + EPS)
    mean = jnp.zeros((LOCAL, 128), F32)
    spots = [pl.multiple_of(ROWS * lax.rem(at_ref[0] + r, 4), 128) for r in range(4)]
    for r, spot in enumerate(spots):
        at, to = slice(ROWS * r, ROWS * r + ROWS), pl.ds(spot, ROWS)
        total = a_ref[0:LOCAL, at].astype(F32) + b_ref[0:LOCAL, at].astype(F32)
        total = total + c_ref[0:LOCAL, at].astype(F32) + d_ref[0:LOCAL, at].astype(F32)
        last = jnp.concatenate([jnp.zeros((LOCAL - 8, ROWS), F32), ahead_ref[8:16, at].astype(F32)], axis=0)
        e1 = (total + last) * gain_ref[:, to]
        out_ref[:, to] = e1
        w = tok_ref[:, to].astype(F32) * inv
        part = e1 * w
        mean = mean + part[:, 0:128] + part[:, 128:256] + part[:, 256:384]
    mean = jnp.sum(mean, axis=1, keepdims=True) / D
    for r in range(4):
        to = slice(ROWS * r, ROWS * r + ROWS)
        w = tok_ref[:, to].astype(F32) * inv
        out_ref[:, to] = cot_ref[:, to].astype(F32) + inv * (out_ref[:, to] - w * mean)


def layer_out_fn(out_ref, tok_ref, sums_ref, res_ref):
    pad = jnp.concatenate([sums_ref[0], jnp.zeros((120, LOCAL), F32)], axis=0).T
    factor = lax.rsqrt(pad[:, 0:1] / INNER + EPS)
    res_ref[...] = tok_ref[...].astype(F32) + factor * out_ref[...].astype(F32)


def place_early_fn(at_ref, mine_ref, sib_ref, out_ref, final_ref):
    def fill(refs):
        for c in range(2):
            for line in range(4):
                block = refs[c][0, lax.rem(at_ref[0] - line + 4, 4)].astype(F32)
                for a in range(2):
                    first = (2 * c + a) * 768 + 192 * line
                    out_ref[:, first : first + 192] = block[0:96, 192 * a : 192 * a + 192]
                    first = 768 * c + 384 * a
                    final_ref[line, :, first : first + 384] = block[96 + 48 * a : 144 + 48 * a]

    for mine, refs in ((0, (mine_ref, sib_ref)), (1, (sib_ref, mine_ref))):

        @pl.when(at_ref[1] == mine)
        def _(refs=refs):
            fill(refs)


def place_late_fn(at_ref, *refs):
    arrays, (out_ref, buf, sem) = refs[:8], refs[8:]
    y, core = at_ref[0], at_ref[1]
    step = pl.program_id(0)

    def fetch(number, slot):
        for k in range(4):

            @pl.when(number == k)
            def _(k=k):
                for i in range(2):
                    to = buf.at[slot, lax.rem(core + i, 2)]
                    pltpu.make_async_copy(arrays[4 * i + k], to, sem.at[slot, i]).start()

    slot = lax.rem(step, 2)

    @pl.when(step == 0)
    def _():
        fetch(step, slot)

    @pl.when(step < 3)
    def _():
        fetch(step + 1, 1 - slot)

    for i in range(2):
        pltpu.make_async_copy(arrays[0], buf.at[slot, i], sem.at[slot, i]).wait()
    for c in range(2):
        for line in range(4):
            block = buf[slot, c, lax.rem(y - line + 4, 4)].astype(F32)
            for a in range(2):
                first = (2 * c + a) * 768 + 192 * line
                out_ref[:, first : first + 192] = block[:, 192 * a : 192 * a + 192]
    total = buf[slot, 0, 4].astype(F32) + buf[slot, 1, 4].astype(F32)
    out_ref[:, INNER:] = total[:, 0 : 2 * STATE]


def place_small_fn(
    at_ref, own_ref, sib_ref, gain_ref,
    taps_ref, bias_ref, gating_ref, rates_ref, offset_ref, norm_ref, skip_ref, step_ref, buf_ref,
    line_ref, heads_ref,
):
    y, core = at_ref[0], at_ref[1]
    buf_ref[...] = jnp.zeros_like(buf_ref)
    taps = jnp.zeros((8, 2 * STATE), F32)
    norm = jnp.zeros((4, ROWS), F32)
    for mine, sets in ((0, (own_ref, sib_ref)), (1, (sib_ref, own_ref))):

        @pl.when(core == mine)
        def _(sets=sets):
            for c in range(2):
                for line in range(4):
                    rows = sets[c][lax.rem(y - line + 4, 4)].astype(F32)
                    for a in range(2):
                        at = (2 * c + a) * 768 + 192 * line
                        at = slice(at, at + 192)
                        part = rows[:, 192 * a : 192 * a + 192]
                        taps_ref[:, at] = part[4:8]
                        line_ref[0:2, at] = part[8:10]
                        at = 12 * (2 * c + a) + 3 * line
                        heads_ref[0:3, at : at + 3] = rows[10:13, 3 * a : 3 * a + 3]
                        buf_ref[at : at + 3] = rows[16 + 3 * a : 19 + 3 * a, 0:ROWS]

    for ref in (own_ref, sib_ref):
        for slot in range(4):
            rows = ref[slot].astype(F32)
            taps = taps + rows[4:12, HP:CH]
            norm = norm + rows[0:4, 0:ROWS]
    taps_ref[:, INNER:] = taps[0:4]
    line_ref[0:1, INNER:] = taps[4:5]
    norm = norm / gain_ref[...]
    for a in range(4):
        norm_ref[ROWS * a : ROWS * a + ROWS] = norm[a]
    bias_ref[...] = line_ref[0]
    gating_ref[...] = line_ref[1, 0:INNER]
    skip_ref[...] = heads_ref[2, 0:HEADS]
    rates_ref[...] = heads_ref[0, 0:HEADS]
    offset_ref[...] = heads_ref[1, 0:HEADS]
    step_ref[...] = buf_ref[0:HEADS]


def per_device(
    tokens,
    segments,
    cotangent,
    gate_proj,
    mixer_proj,
    step_proj,
    final_proj,
    norm_gain,
    conv_kernel,
    conv_bias,
    step_offset,
    log_rates,
    skip_gain,
    gating_gain,
):
    ctx = lax.axis_index("ctx")
    x = lax.axis_index("fsdp")
    y = lax.axis_index("y")
    core = lax.axis_index("core")
    turn = (x - 2 * core + 4) % 4

    def scalars(*values):
        return jnp.stack([jnp.asarray(v, jnp.int32) for v in values])

    z = ctx * 2 + lax.axis_index("low")
    flag, where = scalars(ctx), scalars(y, core)

    tokens = tokens.reshape(LOCAL, D)
    cot = cotangent.reshape(LOCAL, D)
    slab, final_rows = call(
        pack_kernel_fn,
        "pack",
        [
            (where, SMEM), (gate_proj, HBM), (mixer_proj, HBM), (final_proj, HBM),
            (step_proj.T, None),
        ],
        [((ROWS, WIDE), BF16, None), ((192, D), BF16, None)],
        steps=1,
        scratch=[
            pltpu.VMEM((5, ROWS, 256), BF16),
            pltpu.VMEM((ROWS, WIDE), F32),
            pltpu.VMEM((128, ROWS), F32),
            pltpu.SemaphoreType.DMA((6,)),
        ],
    )

    def first_hop(own, shift):
        return [own, shift(own, 1), shift(own, -1)]

    def far_hop(hop, shift, cut):
        own, below, above = hop
        ends = below[:cut], above[cut:]
        return ends, [own, below, shift(ends[0], 1), shift(ends[1], -1), above]

    slabs = first_hop(slab, x_shift)
    ahead = lax.ppermute(after(tokens, slab)[LOCAL - 16 :], "ctx", [(0, 1)])
    (payload,) = call(
        prep_kernel_fn,
        "prep",
        [
            (scalars(x, ctx), SMEM), (tokens, None), (ahead, None), (norm_gain[None], None),
            (segments, None),
        ],
        [((PAY, D), BF16, None)],
        steps=1,
        scratch=[pltpu.VMEM((PAY, D), BF16)],
    )
    mine = first_hop(payload, y_shift)
    par, hp, gain = call(
        params_kernel_fn,
        "params",
        [
            (where, SMEM), (conv_kernel, None), (conv_bias[None], None),
            (step_offset[None], None), (log_rates[None], None), (skip_gain[None], None),
            (gating_gain[None], None),
        ],
        [((8, CH), F32, None), ((8, 128), F32, None), ((8, HP), F32, None)],
        steps=1,
        wait=[payload],
    )
    _, slabs = far_hop(slabs, x_shift, 192)
    own_theirs = core_swap(payload)
    mine = list(after(tuple(mine), own_theirs, slabs[2], slabs[3]))
    cot_all = lax.all_gather(after(cot, mine[1], mine[2]), ("y", "core"), axis=0)

    def owner(r, c):
        return (2 * c + r) % 4

    def from_owners(steps):
        def to(ctx, x, y, low, core):
            r = (x - 2 * core) % 4
            return (ctx, owner(steps[r], core), y, low, core) if r in steps else None

        return to

    def token_outputs(place, count, spot):
        def at(shape):
            return (1,) + shape, lambda i: (place(i),) + (0,) * len(shape)

        outs = [
            ((PAY, D), BF16),
            ((PAY, CH), BF16),
            ((LOCAL, CH), BF16),
            ((LOCAL, STATE), BF16),
            ((LOCAL, 128), F32),
            ((LOCAL, HP), BF16),
            ((8, LOCAL), F32),
            ((LOCAL, HP), BF16),
        ]
        outs = [((GROUP,) + shape, dtype, at(shape)) for shape, dtype in outs]
        state = (1, HP, STATE), lambda i: (spot(i), 0, 0)
        return outs + [((count, HP, STATE), BF16, state)]

    base = [(flag, SMEM), (par, None), (hp, None)]
    scratch = [
        pltpu.VMEM((LOCAL, CH), BF16),
        pltpu.VMEM((2, PAY, D), BF16),
        pltpu.SemaphoreType.DMA((2,)),
    ]
    own, below, far_a, far_b, above = slabs
    wall, *kept = call(
        forward_first_fn,
        "forward_first",
        base
        + [(part, HBM) for part in (payload, own_theirs)]
        + [(part, HBM) for part in (own, above, far_a, far_b, below)],
        [((D, WIDE), BF16, None)] + token_outputs(lambda i: 4 * i, 6, lambda i: i),
        steps=2,
        scratch=scratch + [pltpu.SemaphoreType.DMA((5,))],
    )
    _, below, above = mine
    theirs = [core_swap(below), core_swap(above)]
    below, above, *theirs = after((below, above, *theirs), kept[-1])
    far = y_shift(below[:CUT], 1), y_shift(above[CUT:], -1)
    final_rows = after(final_rows, kept[-1])
    near = move(final_rows, from_owners({0: 1, 1: 0}))
    kept = call(
        forward_near_fn,
        "forward_near",
        base
        + [(wall, None)]
        + [(part, HBM) for part in [below, above, *theirs]]
        + [(part, HBM) for part in kept],
        token_outputs(lambda i: 4 * (i // 2) + 1 + 2 * (i % 2), 6, lambda i: 2 + i),
        steps=4,
        scratch=scratch,
        aliases={8 + i: i for i in range(9)},
    )
    *kept, state_a = kept
    state_in_a = lax.ppermute(state_a, "ctx", [(0, 1)])
    final_rows, *far = after((final_rows, *far), state_a)
    theirs = [core_swap(part) for part in far]
    far_rows = move(final_rows, from_owners({0: 3, 1: 2}))
    away = move(final_rows, from_owners({0: 2, 1: 3}))
    *kept, state_b = call(
        forward_far_fn,
        "forward_far",
        base
        + [(wall, None)]
        + [(part, HBM) for part in [*far, *theirs]]
        + [(part, HBM) for part in kept],
        token_outputs(lambda i: 4 * i + 2, 2, lambda i: i),
        steps=2,
        scratch=scratch,
        aliases={8 + i: i for i in range(8)},
    )
    nall, xbc, u, out_basis, small, gate, segs, y_local = kept
    state_in_b = lax.ppermute(state_b, "ctx", [(0, 1)])

    def state_blocks(first=0):
        def near_at(i, *s):
            line, core = (i + first) % 4, (i + first) // 4
            return (jnp.where(line == 0, core, 2 + 2 * core + line // 2), 0, 0)

        def far_at(i, *s):
            return ((i + first) // 4, 0, 0)

        return [(state_in_a, ((1, HP, STATE), near_at)), (state_in_b, ((1, HP, STATE), far_at))]

    rows = (GROUP, LOCAL, HP)
    wide = seq(LOCAL, HP)
    token = seq(LOCAL, 128)
    line = seq(8, LOCAL)
    dmix, w_final = call(
        dmix_kernel_fn,
        "d_mixed",
        [(cot_all, by_device(LOCAL, D, steps=4, first=k)) for k in range(4)]
        + [(part, HBM) for part in [final_rows, near, far_rows, away]],
        [(rows, BF16, ((4, LOCAL, HP), lambda i, at: (i, 0, 0))), ((HP, D), BF16, None)],
        steps=2,
        scratch=[pltpu.SemaphoreType.DMA((2,))],
        ahead=[scalars(y, core, turn)],
    )
    two = lambda *rest: ((2,) + rest, lambda i, *s: (i,) + (0,) * len(rest))
    pairs = two(LOCAL, HP)
    tokens_two = two(LOCAL, 128)
    y_all, gated, sums = call(
        gate_kernel_fn,
        "gate",
        [(flag, SMEM), (y_local, pairs), (state_in_a, None), (state_in_b, None), (gate, pairs)]
        + [(dmix, pairs), (out_basis, tokens_two), (small, tokens_two), (segs, two(8, LOCAL))]
        + [(gain, None)],
        [(rows, BF16, pairs), (rows, BF16, pairs), ((GROUP, 8, LOCAL), F32, two(8, LOCAL))],
        steps=4,
        scratch=[pltpu.VMEM((LOCAL, HP), F32)],
    )

    (out,) = call(
        product_kernel_fn,
        "out_proj",
        [(where, SMEM), (gated, ((4, LOCAL, HP), lambda i: (i, 0, 0))), (w_final, None)],
        [((GROUP, LOCAL, D), BF16, HBM)],
        steps=2,
        scratch=[pltpu.VMEM((2, 4, LOCAL, D), BF16), pltpu.SemaphoreType.DMA((2, 4))],
    )
    swapped = core_swap(sums)
    sums = sums + jnp.concatenate([swapped[4:], swapped[:4]], axis=0)
    shifted = [y_shift(sums, steps) for steps in (1, 2, 3)]
    shifted = after(tuple(shifted), out)
    total = sums
    for steps, got in zip((1, 2, 3), shifted, strict=True):
        got = got.reshape(2, 4, 8, LOCAL)
        got = jnp.concatenate([got[:, 4 - steps :], got[:, : 4 - steps]], axis=1)
        total = total + got.reshape(GROUP, 8, LOCAL)
    out = lax.psum_scatter(out, ("y", "core"), scatter_dimension=0, tiled=True)
    mixed, dy, dz, dstate, dgain = call(
        ungate_kernel_fn,
        "ungate",
        [(where, SMEM), (flag, SMEM), (y_all, pairs), (gate, pairs), (dmix, pairs)]
        + [(total, two(8, LOCAL)), (out_basis, tokens_two), (small, tokens_two)]
        + [(segs, two(8, LOCAL)), (gain, None)],
        [
            (rows, BF16, HBM),
            (rows, BF16, pairs),
            ((GROUP, PAY, HP), BF16, two(PAY, HP)),
            ((GROUP, HP, STATE), BF16, two(HP, STATE)),
            ((8, HP), F32, None),
        ],
        steps=4,
        scratch=[pltpu.VMEM((2, 2, LOCAL, HP), BF16), pltpu.SemaphoreType.DMA((2, 2))],
    )
    dstate_in = lax.ppermute(dstate, "ctx", [(1, 0)])

    mixed_rows = mixed.reshape(GROUP * LOCAL, HP)

    half = lambda i, at: (0, 2 * ((at[1] + 1 + i // 2) % 2) + i % 2)
    final_send, final_kept = call(
        final_grad_fn,
        "grad_final",
        [
            (mixed_rows, None),
            (cot_all.reshape(GROUP * LOCAL, D), ((GROUP * LOCAL, ROWS), half)),
        ],
        [
            ((HP, 768), BF16, ((HP, ROWS), lambda i, at: (0, jnp.minimum(i, 1)))),
            ((HP, 768), BF16, ((HP, ROWS), lambda i, at: (0, jnp.maximum(i - 2, 0)))),
        ],
        steps=4,
        ahead=[where],
    )
    final_got = core_swap(final_send)

    normed_rows = nall.reshape(GROUP * PAY, D)

    def grad_inputs(grads):
        return [
            (scalars(x, core), SMEM),
            (normed_rows, ((GROUP * PAY, ROWS), lambda i, *s: (0, i))),
            (grads, None),
            (wall, ((ROWS, WIDE), lambda i, *s: (i, 0))),
        ]

    def over_x(blocks):
        own, ahead, far, behind = blocks
        return own, x_shift(far, 2), x_shift(ahead, 1), x_shift(behind, -1)

    def over_z(blocks, parts, rows, wait=()):
        shape = blocks[0].shape
        quarters = call(
            functools.partial(split_fn, parts),
            "split",
            [(scalars(z), SMEM)] + [(block, None) for block in blocks],
            [((rows, shape[1]), BF16, None)] * 4,
            steps=1,
            scratch=[pltpu.VMEM(shape, BF16)],
            wait=wait,
        )
        return quarters, [quarters[0]] + [z_shift(quarters[k], k) for k in (2, 1, 3)]

    def over_y(piece):
        return [piece] + [y_shift(piece, s) for s in (1, 2, 3)]

    def gathered(lines):
        own, small = call(
            lines_fn,
            "lines",
            [(line, None) for line in lines],
            [((5, 96, HP), BF16, None), ((4, 32, CH), BF16, None)],
            steps=1,
        )
        mine = [own] + [z_shift(own, k) for k in (2, 1, 3)]
        mine = [mine[0], mine[2], mine[1], mine[3]]
        return (small, core_swap(small)), mine

    *early, norm_gate = call(
        early_grad_fn,
        "grad_gate",
        grad_inputs(dz.reshape(GROUP * PAY, HP)) + [(final_kept, None), (final_got, None)],
        [((2 * ROWS, HP), BF16, None)] * 4 + [((8, HP), F32, None)],
        steps=4,
    )
    early_block = early[0]
    early = over_x(early)

    sums = [jnp.zeros((8, HP), F32), jnp.zeros((8, CH), F32), jnp.zeros((8, 128), F32)]
    dx, dskip, dpar, dhead = call(
        back_kernel_fn,
        "back",
        [
            (flag, SMEM), (dy, wide), (u, seq(LOCAL, CH)), (xbc, seq(PAY, CH)), (small, token),
            (segs, line), (par, None), (hp, None),
        ]
        + state_blocks()
        + [(dstate_in, seq(HP, STATE))]
        + [(value, None) for value in sums],
        [
            ((GROUP, PAY, MIX), BF16, seq(PAY, MIX)),
            ((8, HP), F32, None),
            ((8, CH), F32, None),
            ((8, 128), F32, None),
        ],
        scratch=[
            pltpu.VMEM((128, LOCAL), F32),
            pltpu.VMEM((LOCAL, CH), F32),
            pltpu.VMEM((LOCAL, 128), F32),
            pltpu.VMEM((LOCAL, 128), F32),
            pltpu.VMEM((LOCAL, CH), BF16),
            pltpu.VMEM((LOCAL, CH), F32),
        ],
        wait=[early_block],
    )
    quarters, early = over_z(after(tuple(early), dpar), ((0, 192),), 192)

    def back_projected(first, count, wait):
        mine = lambda i: (first + 2 * i, 0, 0)
        theirs = lambda i: (4 + first + 2 * i, 0, 0)
        block, out = (1, PAY, MIX), ((1, PAY, D), lambda i: (i, 0, 0))
        a, b = call(
            back_proj_fn,
            "back_proj",
            [
                (dx, (block, mine)), (dx, (block, theirs)),
                (dz, ((1, PAY, HP), mine)), (dz, ((1, PAY, HP), theirs)), (wall, None),
            ],
            [((count, PAY, D), BF16, out)] * 2,
            steps=count,
            wait=wait,
        )
        return a, b

    far_mine, far_theirs = back_projected(2, 1, [*quarters[1:], out])
    piece = add(*after(tuple(early), far_mine))
    early = over_y(piece)
    far_theirs = core_swap(far_theirs)
    blocks = call(
        late_grad_fn,
        "grad_mixer",
        grad_inputs(dx.reshape(GROUP * PAY, MIX))
        + [(value, None) for value in (norm_gate, dpar, dgain, dskip, dhead)],
        [((rows, CH), BF16, None) for rows in (ROWS + 32, ROWS + 32, HALF, HALF, ROWS + 32)],
        steps=4,
        wait=[far_mine, piece],
        scratch=[pltpu.VMEM((16, CH), F32)],
    )
    stack = jnp.stack(after(tuple(early), blocks[0]))
    early = lax.all_gather(stack, ("ctx", "low"), axis=0)

    far_mine, far_theirs = after((far_mine, far_theirs), blocks[0])
    ends = call(
        ends_fn,
        "ends",
        [(far_mine, None), (far_theirs, None)],
        [((CUT, D), BF16, None), ((PAY - CUT, D), BF16, None)],
        steps=1,
    )
    x_up, x_down = x_shift(blocks[2], 1), x_shift(blocks[3], -1)
    up, down = y_shift(ends[0], 1), y_shift(ends[1], -1)
    own_mine, own_theirs = back_projected(0, 1, [*ends, stack])
    x_up, x_down, up, down = after((x_up, x_down, up, down), own_mine)
    own_theirs = core_swap(after(own_theirs, x_up, x_down, up, down))
    ends = call(
        patch_fn,
        "patch",
        [(blocks[1], None), (x_up, None), (blocks[4], None), (x_down, None)],
        [((ROWS + 32, CH), BF16, None)] * 2,
        steps=1,
    )
    late = blocks[0], x_shift(ends[0], 1), x_shift(ends[1], -1)
    mine, theirs = back_projected(1, 2, [*ends, up, down, own_theirs])
    late = after(tuple(late), mine)
    theirs = core_swap(after(theirs, *late))
    quarters, late = over_z(late, ((0, 96), (ROWS, 0)), 128)
    (layer_out,) = call(
        layer_out_fn,
        "layer_out",
        [(out[0], None), (tokens, None), (total, ((1, 8, LOCAL), lambda i: (0, 0, 0)))],
        [((LOCAL, D), F32, None)],
        steps=1,
        wait=[quarters[1]],
    )
    mine, theirs, up, down = after((mine, theirs, up, down), quarters[1])
    tail = jnp.zeros((PAY - CUT, D), BF16)
    above = add(mine[1], theirs[1], jnp.concatenate([up, tail], axis=0))
    head = jnp.zeros((CUT, D), BF16)
    below = add(mine[0], theirs[0], jnp.concatenate([head, down], axis=0))
    back_got = y_shift(above, 1), y_shift(below, -1)
    piece = add(*after(tuple(late), layer_out, above, below))
    late = over_y(piece)
    early = after(early, *late[1:], *back_got)
    parts = [value.reshape(PAY, D) for value in (own_mine, own_theirs)] + list(back_got)
    ahead = add(*[part[LOCAL:] for part in parts])
    ahead = lax.ppermute(ahead, "ctx", [(1, 0)])
    rest, late = gathered(after(tuple(late), ahead))
    (grad_tokens,) = call(
        finish_fn,
        "finish",
        [(scalars(x), SMEM)]
        + [(part, None) for part in [*parts, ahead, tokens, cot, norm_gain[None]]],
        [((LOCAL, D), F32, None)],
        steps=1,
    )

    quarter = ((1, 4, 192, HP), lambda i: (i, 0, 0, 0))
    grad_gate, grad_final = call(
        place_early_fn,
        "place_early",
        [(where, SMEM), (early, quarter), (core_swap(early), quarter)],
        [
            ((ROWS, INNER), F32, ((96, INNER), lambda i: (i, 0))),
            ((4, 192, D), F32, ((4, 48, D), lambda i: (0, i, 0))),
        ],
        steps=4,
        wait=[rest[1]],
    )
    taps, bias, gating, rates, offset, norm, skip, grad_step = call(
        place_small_fn,
        "place_small",
        [(where, SMEM), (rest[0], None), (rest[1], None), (norm_gain.reshape(4, ROWS), None)],
        [((4, CONV_CH), F32, None)]
        + [((n,), F32, None) for n in (CONV_CH, INNER, HEADS, HEADS, D, HEADS)]
        + [((HEADS, ROWS), F32, None)],
        steps=1,
        scratch=[
            pltpu.VMEM((128, ROWS), F32),
            pltpu.VMEM((8, CONV_CH), F32),
            pltpu.VMEM((8, 128), F32),
        ],
    )
    late = list(after(tuple(late), grad_gate, taps, grad_tokens))
    late = late + [core_swap(part) for part in late]
    (grad_mixer,) = call(
        place_late_fn,
        "place_late",
        [(value, HBM) for value in late],
        [((ROWS, CONV_CH), F32, ((96, CONV_CH), lambda i, at: ((at[2] - i + 4) % 4, 0)))],
        steps=4,
        scratch=[pltpu.VMEM((2, 2, 5, 96, HP), BF16), pltpu.SemaphoreType.DMA((2, 2))],
        ahead=[scalars(y, core, z)],
    )
    shape = (1, LOCAL, D)
    return (
        layer_out.reshape(shape),
        grad_tokens.reshape(shape),
        grad_gate,
        grad_mixer,
        grad_step.T,
        grad_final.reshape(2 * 384, D),
        norm,
        taps,
        bias,
        offset,
        rates,
        skip,
        gating,
    )


def solution(mesh):
    apart = jax.sharding.Mesh(mesh.devices.reshape(2, 4, 4, 2, 2), AXES)
    batch = ("fsdp", "y", "low", "core")
    tokens = P(batch, "ctx", None)
    rows = P("fsdp", None)
    return jax.shard_map(
        per_device,
        mesh=apart,
        in_specs=(tokens, P(batch, None), tokens, rows, rows, rows, rows) + (P(),) * 7,
        out_specs=(tokens, tokens, rows, rows, rows, rows) + (P(),) * 7,
        check_vma=False,
    )
```
